32 devices in a mesh: fibre: 16 (over z, x, core), freq: 2 (over y).
Axes of the slice: x: 2, y: 2, z: 4, core: 2. Of those that a mesh axis runs over, the one named last changes fastest.
Arguments:
- traces: bfloat16 [2, 1024, 4096], P(None, 'fibre'), may hold values from -50 to 50, as said below
- live: int32 [1024], P('fibre'), may hold values 0 or 1
- reach: int32 [16], P('fibre'), may hold values from 1 to 8
Outputs:
- correlations: float32 [16, 8, 64, 64, 128], P('fibre', 'freq')
The draws below stay inside these ranges and needn't reach their ends.
Inputs may be any that keep to these rules, and one draw needn't show every extreme that they name: `traces`: records of the fibre's channels.
All inputs are finite; a program needn't handle non-finite values. No bound on the sum of `live` on one device may be relied on, other than what follows from the above.
Results may differ from the reference program's by a relative error of at most 0.0057.
Values may be sent and summed in bfloat16 or wider, within the bound.
No kernel may reach another device: no remote copies, remote signals or barrier semaphores. Data moves between devices by JAX's collectives and lax.ppermute only.
A program may use at most 64 MiB of HBM per device.

```python
import math
import jax
import jax.numpy as jnp
from jax import lax

CH_BLK = 64
NF = 2048
NS = 4096
BAND = 64
OFF = 8
LAGS = 128
WIN = 2
NBLK = 16
CH = 1024


def draw_traces(key, part):
    first_key, gain_key = jax.random.split(key, 2)
    channel_gain = jnp.exp(jax.random.uniform(gain_key, (1, CH, 1), minval=0.0, maxval=math.log(10.0)))
    values = jnp.clip(jax.random.normal(first_key, (WIN, CH, NS)), -5.0, 5.0)
    return jnp.clip(values * channel_gain, -50.0, 50.0).astype(jnp.float32).astype(jnp.bfloat16)


def place_ends(result, key, low, largest):
    shape = result.shape
    place = [jax.random.randint(jax.random.fold_in(key, axis), (), 0, shape[axis]) for axis in range(len(shape))]
    result = result.at[tuple(place)].set(low)
    longest = shape.index(max(shape))
    place[longest] = (place[longest] + 1) % shape[longest]
    return result.at[tuple(place)].set(largest)


def setup_inputs(seed: int = 0) -> dict:
    keys = jax.random.split(jax.random.key(seed), 4)
    traces = draw_traces(jax.random.fold_in(keys[3], 71), 0)
    live = place_ends((jax.random.randint(keys[1], (CH,), 0, 8) < 7).astype(jnp.int32), jax.random.fold_in(keys[1], 1), 0, 1)
    reach = place_ends(jax.random.randint(keys[2], (NBLK,), 1, OFF + 1), jax.random.fold_in(keys[2], 1), 1, OFF).astype(jnp.int32)
    return {"traces": traces, "live": live, "reach": reach}


def phase_angle(freq_ids, sample_ids, period):
    product = freq_ids[:, None] * sample_ids[None, :] % period
    return product.astype(jnp.float32) * (2.0 * math.pi / period)

def reference(traces, live, reach):
    row_count = WIN * CH
    flat_rows = traces.reshape(row_count, NS)
    freq_ids = jnp.arange(NF, dtype=jnp.int32)
    sample_ids = jnp.arange(NS, dtype=jnp.int32)
    angles = phase_angle(freq_ids, sample_ids, NS)
    cosine = jnp.cos(angles).astype(jnp.bfloat16)
    sine_table = (-jnp.sin(angles)).astype(jnp.bfloat16)
    real_part = jnp.dot(flat_rows, cosine.T, preferred_element_type=jnp.float32)
    imag_part = jnp.dot(flat_rows, sine_table.T, preferred_element_type=jnp.float32)
    spectra = jnp.stack([real_part, imag_part])
    band_power = (spectra[0] * spectra[0] + spectra[1] * spectra[1]).reshape(row_count, NF // BAND, BAND).mean(-1)
    whiten_gain = jnp.repeat(1.0 / jnp.sqrt(band_power + 1e-06), BAND, axis=1)
    alive_rows = jnp.tile(live.astype(jnp.float32), WIN)
    whitened = (spectra * whiten_gain[None] * alive_rows[None, :, None]).astype(jnp.bfloat16)
    whitened = whitened.reshape(2, WIN, CH, NF)
    padded = jnp.concatenate([whitened, jnp.zeros((2, WIN, OFF * CH_BLK, NF), jnp.bfloat16)], axis=2)
    lag_steps = jnp.arange(LAGS, dtype=jnp.int32) - LAGS // 2 + NS
    lag_angles = phase_angle(freq_ids, lag_steps, NS)
    lag_table = jnp.concatenate([jnp.cos(lag_angles).astype(jnp.bfloat16), (-jnp.sin(lag_angles)).astype(jnp.bfloat16)])

    def one_block(block_index):
        own_block = lax.dynamic_slice_in_dim(padded, (block_index * CH_BLK).astype(jnp.int32), CH_BLK, 2).astype(jnp.float32)

        def one_offset(offset):
            first = ((block_index + offset) * CH_BLK).astype(jnp.int32)
            partner = lax.dynamic_slice_in_dim(padded, first, CH_BLK, 2).astype(jnp.float32)
            cross_real = (own_block[0][:, :, None, :] * partner[0][:, None, :, :] + own_block[1][:, :, None, :] * partner[1][:, None, :, :]).sum(0)
            cross_imag = (own_block[1][:, :, None, :] * partner[0][:, None, :, :] - own_block[0][:, :, None, :] * partner[1][:, None, :, :]).sum(0)
            cross_block = jnp.stack([cross_real, cross_imag], axis=2).astype(jnp.bfloat16).reshape(CH_BLK * CH_BLK, 2 * NF)
            return jnp.dot(cross_block, lag_table, preferred_element_type=jnp.float32).reshape(CH_BLK, CH_BLK, LAGS)
        return lax.map(one_offset, jnp.arange(OFF, dtype=jnp.int32))
    raw_lags = lax.map(one_block, jnp.arange(NBLK, dtype=jnp.int32))
    keep_mask = (jnp.arange(OFF, dtype=jnp.int32)[None, :] < reach[:, None]).astype(jnp.float32)
    normal_scale = 1.0 / math.sqrt(WIN * NF)
    return raw_lags * normal_scale * keep_mask[:, :, None, None, None]
```

```python
import functools
import math

import jax
import jax.numpy as jnp
import ml_dtypes
import numpy as np
from jax import lax
from jax.experimental import pallas as pl
from jax.experimental.pallas import tpu as pltpu
from jax.sharding import PartitionSpec as P

BAND = 64
OFF = 8
LAGS = 128
VMEM_LIMIT = 56 * 1024 * 1024


def leak_spectrum(freqs, samples, window, shift, slots, period):
    steps = np.arange(window)
    tone = np.exp(2j * np.pi * ((freqs[:, None] * (steps - shift)[None]) % samples) / samples)
    bins = np.exp(-2j * np.pi * ((steps[:, None] * slots[None]) % period) / period)
    return tone @ bins


@functools.lru_cache(maxsize=None)
def build_tables(samples):
    width = LAGS
    residues = samples // width
    groups = residues // 2
    half = width // 2
    per_band = BAND // residues
    order = np.concatenate([np.arange(i, half, per_band) for i in range(per_band)])
    steps = np.arange(width)
    slots = np.arange(width + 1)
    forward = np.zeros((groups, 2 * width, 4 * half))
    to_bins = np.zeros((2, groups, 4 * half, 4, width))
    root = 1.0 / math.sqrt(2.0)
    re_a, im_a, re_b, im_b = (slice(i * half, (i + 1) * half) for i in range(4))
    for g in range(groups):
        freq_a = g + residues * order
        freq_b = (residues - g if g else groups) + residues * order
        wave_a = np.exp(-2j * np.pi * ((steps[:, None] * freq_a[None]) % samples) / samples)
        wave_b = np.exp(-2j * np.pi * ((steps[:, None] * freq_b[None]) % samples) / samples)
        top, low = forward[g, :width], forward[g, width:]
        top[:, re_a], top[:, im_a] = wave_a.real, wave_a.imag
        if g == 0:
            low[:, re_b], low[:, im_b] = wave_b.real, wave_b.imag
        else:
            low[:, re_a], low[:, im_a] = -wave_a.imag, wave_a.real
            top[:, re_b], top[:, im_b] = wave_b.real, wave_b.imag
            low[:, re_b], low[:, im_b] = wave_b.imag, -wave_b.real
        for side in range(2):
            window, shift = ((width, 0), (2 * width, half))[side]
            leak = functools.partial(
                leak_spectrum, samples=samples, window=window, shift=shift, slots=slots, period=2 * width
            )
            pos_a, neg_a, pos_b, neg_b = leak(freq_a), leak(-freq_a), leak(freq_b), leak(-freq_b)
            spec = np.zeros((2, 4 * half, width + 1), complex)
            if g == 0:
                zero = (freq_a == 0)[:, None]
                spec[0, re_a] = np.where(zero, pos_a, root * (pos_a + neg_a))
                spec[0, im_a] = np.where(zero, 0.0, root * 1j * (pos_a - neg_a))
                spec[1, re_b] = root * (pos_b + neg_b)
                spec[1, im_b] = root * 1j * (pos_b - neg_b)
            else:
                spec[0, re_a], spec[0, im_a] = root * pos_a, root * 1j * pos_a
                spec[0, re_b], spec[0, im_b] = root * neg_b, -root * 1j * neg_b
                spec[1, re_b], spec[1, im_b] = root * pos_b, root * 1j * pos_b
                spec[1, re_a], spec[1, im_a] = root * neg_a, -root * 1j * neg_a
            table = to_bins[side, g]
            table[:, 0], table[:, 1] = spec[0, :, :width].real, spec[0, :, :width].imag
            table[:, 2], table[:, 3] = spec[1, :, :width].real, spec[1, :, :width].imag
            if g == 0:
                ends = (spec[0, :, 0].real, spec[1, :, 0].real, spec[0, :, width].real, spec[1, :, width].real)
            else:
                ends = tuple(
                    math.sqrt(2.0) * v
                    for v in (spec[0, :, 0].real, spec[0, :, 0].imag, spec[0, :, width].real, spec[0, :, width].imag)
                )
            for q in range(4):
                table[:, q, 0] = ends[q]
    lags = np.arange(LAGS)
    phase = 2 * np.pi * ((steps[:, None] * lags[None]) % (2 * width)) / (2 * width)
    lag = np.stack([2 * np.cos(phase), -2 * np.sin(phase)])
    lag[0, 0], lag[1, 0] = 1.0, (-1.0) ** lags
    bf16 = ml_dtypes.bfloat16
    forward_t = forward.transpose(0, 2, 1)
    forward_hi = forward_t.astype(bf16)
    forward_lo = (forward_t - forward_hi.astype(np.float64)).astype(bf16)
    bins_t = to_bins.transpose(0, 1, 3, 4, 2).reshape(2, groups, 4 * width, 4 * half).astype(bf16)
    lag_t = lag.reshape(2 * width, LAGS).T.astype(bf16)
    scale = residues / (2.0 * width * samples) / math.sqrt(samples)
    return forward_hi, forward_lo, bins_t, lag_t, scale


def real_dft(values):
    n = len(values)
    if n == 2:
        return [(values[0] + values[1], None), (values[0] - values[1], None)]
    even, odd = real_dft(values[0::2]), real_dft(values[1::2])
    out = [None] * (n // 2 + 1)
    for k in range(n // 4 + 1):
        (er, ei), (pr, pi) = even[k], odd[k]
        angle = -2.0 * math.pi * k / n
        c, s = math.cos(angle), math.sin(angle)
        if k == 0:
            out[0] = (er + pr, None)
            out[n // 2] = (er - pr, None)
            continue
        if 4 * k == n:
            out[k] = (er, -pr)
            continue
        if pi is None:
            tr, ti = pr * c, pr * s
        elif 8 * k == n:
            tr, ti = (pr + pi) * c, (pi - pr) * c
        else:
            tr, ti = pr * c - pi * s, pr * s + pi * c
        if ei is None:
            out[k] = (er + tr, ti)
            out[n // 2 - k] = (er - tr, ti)
        else:
            out[k] = (er + tr, ei + ti)
            out[n // 2 - k] = (er - tr, ti - ei)
    return out


def prepare_kernel(own, first_ref, second_ref, fhi_hbm, flo_hbm, bins_hbm, out_ref,
                   fhi, flo, bins, yhi, ylo, spec, wide, sems):
    windows, channels, samples = first_ref.shape
    width = LAGS
    residues = samples // width
    groups = residues // 2
    rows = 2 * windows * channels
    lanes = 2 * channels
    copies = [
        pltpu.make_async_copy(src, dst, sems.at[i])
        for i, (src, dst) in enumerate(((fhi_hbm, fhi), (flo_hbm, flo), (bins_hbm, bins)))
    ]
    for copy in copies:
        copy.start()

    step = 16
    per_window = channels // step

    def split(value):
        high = value.astype(jnp.bfloat16)
        return high, (value - high.astype(jnp.float32)).astype(jnp.bfloat16)

    def transform(n, carry):
        w, c = n // per_window, n % per_window
        for which, ref in enumerate((first_ref, second_ref)):
            if own and which:
                continue
            block = ref[w, pl.ds(pl.multiple_of(c * step, step), step), :].astype(jnp.float32)
            terms = real_dft([block[:, a * width:(a + 1) * width] for a in range(residues)])
            for g in range(groups):
                if g == 0:
                    parts = (terms[0][0], terms[groups][0])
                else:
                    parts = terms[g]
                for side, part in enumerate(parts):
                    hi, lo = split(part)
                    for copy_to in ((0, 1) if own else (which,)):
                        row = pl.multiple_of(w * lanes + copy_to * channels + c * step, step)
                        yhi[g, pl.ds(row, step), side * width:(side + 1) * width] = hi
                        ylo[g, pl.ds(row, step), side * width:(side + 1) * width] = lo
        return carry

    lax.fori_loop(0, windows * per_window, transform, 0)
    copies[0].wait()
    copies[1].wait()
    nt = (((1,), (1,)), ((), ()))
    bands = (samples // 2) // BAND

    def forward(g, power):
        value = lax.dot_general(fhi[g], yhi[g], nt, preferred_element_type=jnp.float32)
        value += lax.dot_general(flo[g], yhi[g], nt, preferred_element_type=jnp.float32)
        value += lax.dot_general(fhi[g], ylo[g], nt, preferred_element_type=jnp.float32)
        spec[g] = value
        squared = (value * value).reshape(2 * width // bands, bands, rows)
        return power + squared.sum(0)

    power = lax.fori_loop(0, groups, forward, jnp.zeros((bands, rows), jnp.float32))
    gain = 1.0 / jnp.sqrt(power * (1.0 / BAND) + 1e-6)
    copies[2].wait()

    def to_bins(g, carry):
        white = (spec[g].reshape(2 * width // bands, bands, rows) * gain[None]).reshape(2 * width, rows)
        value = jnp.dot(bins[g], white.astype(jnp.bfloat16), preferred_element_type=jnp.float32)
        parts = [value[q * width:(q + 1) * width] for q in range(4)]
        if own:
            left = lax.broadcasted_iota(jnp.int32, (width, rows), 1) % lanes < channels
            ends = lax.broadcasted_iota(jnp.int32, (width, rows), 0) == 0
            turned = [parts[1], -parts[0], parts[3], -parts[2]]
            zero = jnp.zeros_like(parts[0])
            real = [parts[q] if q < 2 else jnp.where(ends, zero, parts[q]) for q in range(4)]
            imag = [jnp.where(ends, zero if q < 2 else parts[q], turned[q]) for q in range(4)]
            parts = [jnp.where(left, real[q], imag[q]) for q in range(4)]
        for q in range(4):
            for w in range(windows):
                start = w * (groups * 4) + g * 4 + q
                wide[pl.ds(start, width, stride=windows * groups * 4), :] = parts[q][:, w * lanes:(w + 1) * lanes]
        return carry

    lax.fori_loop(0, groups, to_bins, 0)
    depth = windows * groups * 4

    def narrow(k, carry):
        block = wide[pl.ds(pl.multiple_of(k * depth, depth), depth), :]
        out_ref[k] = (block.T if own else block).astype(jnp.bfloat16)
        return carry

    lax.fori_loop(0, width, narrow, 0)


def prepare(first, second, tables, own):
    windows, channels, samples = first.shape
    forward_hi, forward_lo, bins_t = tables
    width = LAGS
    groups = samples // width // 2
    rows = 2 * windows * channels
    depth = windows * groups * 4
    lanes = 2 * channels
    shape = (width, lanes, depth) if own else (width, depth, lanes)
    any_spec = pl.BlockSpec(memory_space=pl.ANY)
    vmem_spec = pl.BlockSpec(memory_space=pltpu.VMEM)
    flops = 2 * groups * rows * (3 * 4 * width * width + 8 * width * width)
    return pl.pallas_call(
        functools.partial(prepare_kernel, own),
        out_shape=jax.ShapeDtypeStruct(shape, jnp.bfloat16),
        in_specs=[vmem_spec, vmem_spec, any_spec, any_spec, any_spec],
        out_specs=vmem_spec,
        scratch_shapes=[
            pltpu.VMEM(forward_hi.shape, jnp.bfloat16),
            pltpu.VMEM(forward_lo.shape, jnp.bfloat16),
            pltpu.VMEM(bins_t.shape, jnp.bfloat16),
            pltpu.VMEM((groups, rows, 2 * width), jnp.bfloat16),
            pltpu.VMEM((groups, rows, 2 * width), jnp.bfloat16),
            pltpu.VMEM((groups, 2 * width, rows), jnp.float32),
            pltpu.VMEM((width * depth, lanes), jnp.float32),
            pltpu.SemaphoreType.DMA((3,)),
        ],
        compiler_params=pltpu.CompilerParams(vmem_limit_bytes=VMEM_LIMIT),
        cost_estimate=pl.CostEstimate(flops=flops, bytes_accessed=14 * 2**20, transcendentals=0),
        name="prepare_own" if own else "prepare_partners",
    )(first, second, forward_hi, forward_lo, bins_t)


def stack_kernel(chunks, per_chunk, per_out, own_ref, first_ref, second_ref, lag_ref, keep_ref, out_ref, *cross):
    step = pl.program_id(0)
    width = LAGS
    lanes = first_ref.shape[2]
    channels = lanes // 2

    @pl.when(step < chunks)
    def _():
        def one(n, carry):
            k = step * per_chunk + n
            for side, ref in enumerate((first_ref, second_ref)):
                value = jnp.dot(own_ref[n], ref[n], preferred_element_type=jnp.float32)
                for part in range(2):
                    cross[side][pl.ds(part * width + k, channels, stride=2 * width), :] = (
                        value[part * channels:(part + 1) * channels]
                    )
            return carry

        lax.fori_loop(0, per_chunk, one, 0)

    @pl.when(step >= chunks)
    def _():
        def one(n, carry):
            i = (step - chunks) * per_out + n
            part = pl.ds(pl.multiple_of(i * 2 * width, 2 * width), 2 * width)
            block = jnp.concatenate([ref[part, :].astype(jnp.bfloat16) for ref in cross], axis=1)
            value = jnp.dot(lag_ref[...], block, preferred_element_type=jnp.float32).T
            for o in range(4):
                out_ref[o, n] = value[o * channels:(o + 1) * channels] * keep_ref[o]
            return carry

        lax.fori_loop(0, per_out, one, 0)


def stack(own, first, second, lag_t, keep):
    width, lanes, depth = own.shape
    channels = lanes // 2
    chunks, out_chunks = 4, 8
    per_chunk, per_out = width // chunks, channels // out_chunks
    block = lambda s: (jnp.minimum(s, chunks - 1), 0, 0)
    offsets = 4
    return pl.pallas_call(
        functools.partial(stack_kernel, chunks, per_chunk, per_out),
        grid=(chunks + out_chunks,),
        out_shape=jax.ShapeDtypeStruct((offsets, channels, channels, LAGS), jnp.float32),
        in_specs=[
            pl.BlockSpec((per_chunk, lanes, depth), block),
            pl.BlockSpec((per_chunk, depth, lanes), block),
            pl.BlockSpec((per_chunk, depth, lanes), block),
            pl.BlockSpec(lag_t.shape, lambda s: (0, 0)),
            pl.BlockSpec(memory_space=pltpu.SMEM),
        ],
        out_specs=pl.BlockSpec(
            (offsets, per_out, channels, LAGS), lambda s: (0, jnp.maximum(s - chunks, 0), 0, 0)
        ),
        scratch_shapes=[pltpu.VMEM((channels * 2 * width, lanes), jnp.float32)] * 2,
        compiler_params=pltpu.CompilerParams(
            vmem_limit_bytes=VMEM_LIMIT, dimension_semantics=("arbitrary",)
        ),
        name="stack_lags",
    )(own, first, second, lag_t, keep)


def per_device(traces, live, reach):
    windows, channels, samples = traces.shape
    blocks = lax.axis_size("fibre")
    splits = lax.axis_size("freq")
    owned = OFF // splits
    place = lax.axis_index("freq")
    forward_hi, forward_lo, bins_t, lag_t, scale = build_tables(samples)
    forward_hi, forward_lo = jnp.asarray(forward_hi), jnp.asarray(forward_lo)
    masked = traces * live.astype(traces.dtype)[None, :, None]

    def arrive(offset):
        pairs = []
        for b in range(blocks):
            for g in range(splits):
                source = b + g * owned + offset
                if source < blocks:
                    pairs.append((source * splits + g, b * splits + g))
        return lax.ppermute(masked, ("fibre", "freq"), pairs)

    own = prepare(masked, masked, (forward_hi, forward_lo, jnp.asarray(bins_t[1])), True)
    partners = [arrive(k) for k in range(owned)]
    partner_tables = (forward_hi, forward_lo, jnp.asarray(bins_t[0]))
    first = prepare(partners[0], partners[1], partner_tables, False)
    second = prepare(partners[2], partners[3], partner_tables, False)
    offset_ids = place * owned + jnp.arange(owned, dtype=jnp.int32)
    keep = jnp.where(offset_ids < reach[0], jnp.float32(scale), jnp.float32(0.0))
    return stack(own, first, second, jnp.asarray(lag_t), keep)[None]


def solution(mesh):
    placed = (P(None, "fibre", None), P("fibre"), P("fibre"))
    return jax.shard_map(
        per_device,
        mesh=mesh,
        in_specs=placed,
        out_specs=P("fibre", "freq", None, None, None),
        check_vma=False,
    )
```

```python
import functools
import math

import jax
import jax.numpy as jnp
import ml_dtypes
import numpy as np
from jax import lax
from jax.experimental import pallas as pl
from jax.experimental.pallas import tpu as pltpu
from jax.sharding import PartitionSpec as P

BAND = 64
OFF = 8
LAGS = 128
VMEM_LIMIT = 56 * 1024 * 1024


def leak_spectrum(freqs, samples, window, shift, slots, period):
    steps = np.arange(window)
    tone = np.exp(2j * np.pi * ((freqs[:, None] * (steps - shift)[None]) % samples) / samples)
    bins = np.exp(-2j * np.pi * ((steps[:, None] * slots[None]) % period) / period)
    return tone @ bins


@functools.lru_cache(maxsize=None)
def build_tables(samples):
    width = LAGS
    residues = samples // width
    groups = residues // 2
    half = width // 2
    per_band = BAND // residues
    order = np.concatenate([np.arange(i, half, per_band) for i in range(per_band)])
    steps = np.arange(width)
    slots = np.arange(width + 1)
    forward = np.zeros((groups, 2 * width, 4 * half))
    to_bins = np.zeros((2, groups, 4 * half, 4, width))
    root = 1.0 / math.sqrt(2.0)
    re_a, im_a, re_b, im_b = (slice(i * half, (i + 1) * half) for i in range(4))
    for g in range(groups):
        freq_a = g + residues * order
        freq_b = (residues - g if g else groups) + residues * order
        wave_a = np.exp(-2j * np.pi * ((steps[:, None] * freq_a[None]) % samples) / samples)
        wave_b = np.exp(-2j * np.pi * ((steps[:, None] * freq_b[None]) % samples) / samples)
        top, low = forward[g, :width], forward[g, width:]
        top[:, re_a], top[:, im_a] = wave_a.real, wave_a.imag
        if g == 0:
            low[:, re_b], low[:, im_b] = wave_b.real, wave_b.imag
        else:
            low[:, re_a], low[:, im_a] = -wave_a.imag, wave_a.real
            top[:, re_b], top[:, im_b] = wave_b.real, wave_b.imag
            low[:, re_b], low[:, im_b] = wave_b.imag, -wave_b.real
        for side in range(2):
            window, shift = ((width, 0), (2 * width, half))[side]
            leak = functools.partial(
                leak_spectrum, samples=samples, window=window, shift=shift, slots=slots, period=2 * width
            )
            pos_a, neg_a, pos_b, neg_b = leak(freq_a), leak(-freq_a), leak(freq_b), leak(-freq_b)
            spec = np.zeros((2, 4 * half, width + 1), complex)
            if g == 0:
                zero = (freq_a == 0)[:, None]
                spec[0, re_a] = np.where(zero, pos_a, root * (pos_a + neg_a))
                spec[0, im_a] = np.where(zero, 0.0, root * 1j * (pos_a - neg_a))
                spec[1, re_b] = root * (pos_b + neg_b)
                spec[1, im_b] = root * 1j * (pos_b - neg_b)
            else:
                spec[0, re_a], spec[0, im_a] = root * pos_a, root * 1j * pos_a
                spec[0, re_b], spec[0, im_b] = root * neg_b, -root * 1j * neg_b
                spec[1, re_b], spec[1, im_b] = root * pos_b, root * 1j * pos_b
                spec[1, re_a], spec[1, im_a] = root * neg_a, -root * 1j * neg_a
            table = to_bins[side, g]
            table[:, 0], table[:, 1] = spec[0, :, :width].real, spec[0, :, :width].imag
            table[:, 2], table[:, 3] = spec[1, :, :width].real, spec[1, :, :width].imag
            if g == 0:
                ends = (spec[0, :, 0].real, spec[1, :, 0].real, spec[0, :, width].real, spec[1, :, width].real)
            else:
                ends = tuple(
                    math.sqrt(2.0) * v
                    for v in (spec[0, :, 0].real, spec[0, :, 0].imag, spec[0, :, width].real, spec[0, :, width].imag)
                )
            for q in range(4):
                table[:, q, 0] = ends[q]
    lags = np.arange(LAGS)
    phase = 2 * np.pi * ((steps[:, None] * lags[None]) % (2 * width)) / (2 * width)
    lag = np.stack([2 * np.cos(phase), -2 * np.sin(phase)])
    lag[0, 0], lag[1, 0] = 1.0, (-1.0) ** lags
    bf16 = ml_dtypes.bfloat16
    forward_t = forward.transpose(0, 2, 1)
    forward_hi = forward_t.astype(bf16)
    forward_lo = (forward_t - forward_hi.astype(np.float64)).astype(bf16)
    bins_t = to_bins.transpose(0, 1, 3, 4, 2).reshape(2, groups, 4 * width, 4 * half).astype(bf16)
    lag_t = lag.reshape(2 * width, LAGS).T.astype(bf16)
    scale = residues / (2.0 * width * samples) / math.sqrt(samples)
    return forward_hi, forward_lo, bins_t, lag_t, scale


def real_dft(values):
    n = len(values)
    if n == 2:
        return [(values[0] + values[1], None), (values[0] - values[1], None)]
    even, odd = real_dft(values[0::2]), real_dft(values[1::2])
    out = [None] * (n // 2 + 1)
    for k in range(n // 4 + 1):
        (er, ei), (pr, pi) = even[k], odd[k]
        angle = -2.0 * math.pi * k / n
        c, s = math.cos(angle), math.sin(angle)
        if k == 0:
            out[0] = (er + pr, None)
            out[n // 2] = (er - pr, None)
            continue
        if 4 * k == n:
            out[k] = (er, -pr)
            continue
        if pi is None:
            tr, ti = pr * c, pr * s
        elif 8 * k == n:
            tr, ti = (pr + pi) * c, (pi - pr) * c
        else:
            tr, ti = pr * c - pi * s, pr * s + pi * c
        if ei is None:
            out[k] = (er + tr, ti)
            out[n // 2 - k] = (er - tr, ti)
        else:
            out[k] = (er + tr, ei + ti)
            out[n // 2 - k] = (er - tr, ti - ei)
    return out


def prepare_kernel(own, first_ref, second_ref, fhi_hbm, flo_hbm, bins_hbm, out_ref,
                   fhi, flo, bins, yhi, ylo, spec, wide, sems):
    windows, channels, samples = first_ref.shape
    width = LAGS
    residues = samples // width
    groups = residues // 2
    rows = 2 * windows * channels
    lanes = 2 * channels
    copies = [
        pltpu.make_async_copy(src, dst, sems.at[i])
        for i, (src, dst) in enumerate(((fhi_hbm, fhi), (flo_hbm, flo), (bins_hbm, bins)))
    ]
    for copy in copies:
        copy.start()

    step = 16
    per_window = channels // step

    def split(value):
        high = value.astype(jnp.bfloat16)
        return high, (value - high.astype(jnp.float32)).astype(jnp.bfloat16)

    def transform(n, carry):
        w, c = n // per_window, n % per_window
        for which, ref in enumerate((first_ref, second_ref)):
            if own and which:
                continue
            block = ref[w, pl.ds(pl.multiple_of(c * step, step), step), :].astype(jnp.float32)
            terms = real_dft([block[:, a * width:(a + 1) * width] for a in range(residues)])
            for g in range(groups):
                if g == 0:
                    parts = (terms[0][0], terms[groups][0])
                else:
                    parts = terms[g]
                for side, part in enumerate(parts):
                    hi, lo = split(part)
                    for copy_to in ((0, 1) if own else (which,)):
                        row = pl.multiple_of(w * lanes + copy_to * channels + c * step, step)
                        yhi[g, pl.ds(row, step), side * width:(side + 1) * width] = hi
                        ylo[g, pl.ds(row, step), side * width:(side + 1) * width] = lo
        return carry

    lax.fori_loop(0, windows * per_window, transform, 0)
    copies[0].wait()
    copies[1].wait()
    nt = (((1,), (1,)), ((), ()))
    bands = (samples // 2) // BAND

    def forward(g, power):
        value = lax.dot_general(fhi[g], yhi[g], nt, preferred_element_type=jnp.float32)
        value += lax.dot_general(flo[g], yhi[g], nt, preferred_element_type=jnp.float32)
        value += lax.dot_general(fhi[g], ylo[g], nt, preferred_element_type=jnp.float32)
        spec[g] = value
        squared = (value * value).reshape(2 * width // bands, bands, rows)
        return power + squared.sum(0)

    power = lax.fori_loop(0, groups, forward, jnp.zeros((bands, rows), jnp.float32), unroll=4)
    gain = 1.0 / jnp.sqrt(power * (1.0 / BAND) + 1e-6)
    copies[2].wait()

    def to_bins(g, carry):
        white = (spec[g].reshape(2 * width // bands, bands, rows) * gain[None]).reshape(2 * width, rows)
        value = jnp.dot(bins[g], white.astype(jnp.bfloat16), preferred_element_type=jnp.float32)
        parts = [value[q * width:(q + 1) * width] for q in range(4)]
        if own:
            left = lax.broadcasted_iota(jnp.int32, (width, rows), 1) % lanes < channels
            ends = lax.broadcasted_iota(jnp.int32, (width, rows), 0) == 0
            turned = [parts[1], -parts[0], parts[3], -parts[2]]
            zero = jnp.zeros_like(parts[0])
            real = [parts[q] if q < 2 else jnp.where(ends, zero, parts[q]) for q in range(4)]
            imag = [jnp.where(ends, zero if q < 2 else parts[q], turned[q]) for q in range(4)]
            parts = [jnp.where(left, real[q], imag[q]) for q in range(4)]
        for q in range(4):
            for w in range(windows):
                start = w * (groups * 4) + g * 4 + q
                wide[pl.ds(start, width, stride=windows * groups * 4), :] = parts[q][:, w * lanes:(w + 1) * lanes]
        return carry

    lax.fori_loop(0, groups, to_bins, 0, unroll=4)
    depth = windows * groups * 4

    def narrow(k, carry):
        block = wide[pl.ds(pl.multiple_of(k * depth, depth), depth), :]
        out_ref[k] = (block.T if own else block).astype(jnp.bfloat16)
        return carry

    lax.fori_loop(0, width, narrow, 0, unroll=8)


def prepare(first, second, tables, own):
    windows, channels, samples = first.shape
    forward_hi, forward_lo, bins_t = tables
    width = LAGS
    groups = samples // width // 2
    rows = 2 * windows * channels
    depth = windows * groups * 4
    lanes = 2 * channels
    shape = (width, lanes, depth) if own else (width, depth, lanes)
    any_spec = pl.BlockSpec(memory_space=pl.ANY)
    vmem_spec = pl.BlockSpec(memory_space=pltpu.VMEM)
    flops = 2 * groups * rows * (3 * 4 * width * width + 8 * width * width)
    return pl.pallas_call(
        functools.partial(prepare_kernel, own),
        out_shape=jax.ShapeDtypeStruct(shape, jnp.bfloat16),
        in_specs=[vmem_spec, vmem_spec, any_spec, any_spec, any_spec],
        out_specs=vmem_spec,
        scratch_shapes=[
            pltpu.VMEM(forward_hi.shape, jnp.bfloat16),
            pltpu.VMEM(forward_lo.shape, jnp.bfloat16),
            pltpu.VMEM(bins_t.shape, jnp.bfloat16),
            pltpu.VMEM((groups, rows, 2 * width), jnp.bfloat16),
            pltpu.VMEM((groups, rows, 2 * width), jnp.bfloat16),
            pltpu.VMEM((groups, 2 * width, rows), jnp.float32),
            pltpu.VMEM((width * depth, lanes), jnp.float32),
            pltpu.SemaphoreType.DMA((3,)),
        ],
        compiler_params=pltpu.CompilerParams(vmem_limit_bytes=VMEM_LIMIT),
        cost_estimate=pl.CostEstimate(flops=flops, bytes_accessed=14 * 2**20, transcendentals=0),
        name="prepare_own" if own else "prepare_partners",
    )(first, second, forward_hi, forward_lo, bins_t)


def stack_kernel(chunks, per_chunk, per_out, own_ref, first_ref, second_ref, lag_ref, keep_ref, out_ref, *cross):
    step = pl.program_id(0)
    width = LAGS
    lanes = first_ref.shape[2]
    channels = lanes // 2

    @pl.when(step < chunks)
    def _():
        def one(n, carry):
            k = step * per_chunk + n
            partners = jnp.concatenate([first_ref[n], second_ref[n]], axis=1)
            value = jnp.dot(own_ref[n], partners, preferred_element_type=jnp.float32)
            for side in range(2):
                for part in range(2):
                    cross[side][pl.ds(part * width + k, channels, stride=2 * width), :] = (
                        value[part * channels:(part + 1) * channels, side * lanes:(side + 1) * lanes]
                    )
            return carry

        lax.fori_loop(0, per_chunk, one, 0, unroll=8)

    @pl.when(step >= chunks)
    def _():
        def one(n, carry):
            i = (step - chunks) * per_out + n
            part = pl.ds(pl.multiple_of(i * 2 * width, 2 * width), 2 * width)
            block = jnp.concatenate([ref[part, :].astype(jnp.bfloat16) for ref in cross], axis=1)
            value = jnp.dot(lag_ref[...], block, preferred_element_type=jnp.float32).T
            for o in range(out_ref.shape[0]):
                out_ref[o, n] = value[o * channels:(o + 1) * channels] * keep_ref[o]
            return carry

        lax.fori_loop(0, per_out, one, 0, unroll=4)


def stack(own, first, second, lag_t, keep):
    width, lanes, depth = own.shape
    channels = lanes // 2
    chunks, out_chunks = 4, 8
    per_chunk, per_out = width // chunks, channels // out_chunks
    block = lambda s: (jnp.minimum(s, chunks - 1), 0, 0)
    offsets = keep.shape[0]
    return pl.pallas_call(
        functools.partial(stack_kernel, chunks, per_chunk, per_out),
        grid=(chunks + out_chunks,),
        out_shape=jax.ShapeDtypeStruct((offsets, channels, channels, LAGS), jnp.float32),
        in_specs=[
            pl.BlockSpec((per_chunk, lanes, depth), block),
            pl.BlockSpec((per_chunk, depth, lanes), block),
            pl.BlockSpec((per_chunk, depth, lanes), block),
            pl.BlockSpec(lag_t.shape, lambda s: (0, 0)),
            pl.BlockSpec(memory_space=pltpu.SMEM),
        ],
        out_specs=pl.BlockSpec(
            (offsets, per_out, channels, LAGS), lambda s: (0, jnp.maximum(s - chunks, 0), 0, 0)
        ),
        scratch_shapes=[pltpu.VMEM((channels * 2 * width, lanes), jnp.float32)] * 2,
        compiler_params=pltpu.CompilerParams(
            vmem_limit_bytes=VMEM_LIMIT, dimension_semantics=("arbitrary",)
        ),
        name="stack_lags",
    )(own, first, second, lag_t, keep)


def per_device(traces, live, reach):
    windows, channels, samples = traces.shape
    blocks = lax.axis_size("fibre")
    splits = lax.axis_size("freq")
    owned = OFF // splits
    place = lax.axis_index("freq")
    forward_hi, forward_lo, bins_t, lag_t, scale = build_tables(samples)
    forward_hi, forward_lo = jnp.asarray(forward_hi), jnp.asarray(forward_lo)
    masked = traces * live.astype(traces.dtype)[None, :, None]

    def arrive(offset):
        pairs = []
        for b in range(blocks):
            for g in range(splits):
                source = b + g * owned + offset
                if source < blocks:
                    pairs.append((source * splits + g, b * splits + g))
        return lax.ppermute(masked, ("fibre", "freq"), pairs)

    own = prepare(masked, masked, (forward_hi, forward_lo, jnp.asarray(bins_t[1])), True)
    partners = [arrive(k) for k in range(owned)]
    partner_tables = (forward_hi, forward_lo, jnp.asarray(bins_t[0]))
    first = prepare(partners[0], partners[1], partner_tables, False)
    second = prepare(partners[2], partners[3], partner_tables, False)
    offset_ids = place * owned + jnp.arange(owned, dtype=jnp.int32)
    keep = jnp.where(offset_ids < reach[0], jnp.float32(scale), jnp.float32(0.0))
    return stack(own, first, second, jnp.asarray(lag_t), keep)[None]


def solution(mesh):
    placed = (P(None, "fibre", None), P("fibre"), P("fibre"))
    return jax.shard_map(
        per_device,
        mesh=mesh,
        in_specs=placed,
        out_specs=P("fibre", "freq", None, None, None),
        check_vma=False,
    )
```

```python
import functools
import math

import jax
import jax.numpy as jnp
import ml_dtypes
import numpy as np
from jax import lax
from jax.experimental import pallas as pl
from jax.experimental.pallas import tpu as pltpu
from jax.sharding import PartitionSpec as P

BAND = 64
OFF = 8
LAGS = 128
VMEM_LIMIT = 56 * 1024 * 1024


def leak_spectrum(freqs, samples, window, shift, slots, period):
    steps = np.arange(window)
    tone = np.exp(2j * np.pi * ((freqs[:, None] * (steps - shift)[None]) % samples) / samples)
    bins = np.exp(-2j * np.pi * ((steps[:, None] * slots[None]) % period) / period)
    return tone @ bins


@functools.lru_cache(maxsize=None)
def build_tables(samples):
    width = LAGS
    residues = samples // width
    groups = residues // 2
    half = width // 2
    per_band = BAND // residues
    order = np.concatenate([np.arange(i, half, per_band) for i in range(per_band)])
    steps = np.arange(width)
    slots = np.arange(width + 1)
    forward = np.zeros((groups, 2 * width, 4 * half))
    to_bins = np.zeros((2, groups, 4 * half, 4, width))
    root = 1.0 / math.sqrt(2.0)
    re_a, im_a, re_b, im_b = (slice(i * half, (i + 1) * half) for i in range(4))
    for g in range(groups):
        freq_a = g + residues * order
        freq_b = (residues - g if g else groups) + residues * order
        wave_a = np.exp(-2j * np.pi * ((steps[:, None] * freq_a[None]) % samples) / samples)
        wave_b = np.exp(-2j * np.pi * ((steps[:, None] * freq_b[None]) % samples) / samples)
        top, low = forward[g, :width], forward[g, width:]
        top[:, re_a], top[:, im_a] = wave_a.real, wave_a.imag
        if g == 0:
            low[:, re_b], low[:, im_b] = wave_b.real, wave_b.imag
        else:
            low[:, re_a], low[:, im_a] = -wave_a.imag, wave_a.real
            top[:, re_b], top[:, im_b] = wave_b.real, wave_b.imag
            low[:, re_b], low[:, im_b] = wave_b.imag, -wave_b.real
        for side in range(2):
            window, shift = ((width, 0), (2 * width, half))[side]
            leak = functools.partial(
                leak_spectrum, samples=samples, window=window, shift=shift, slots=slots, period=2 * width
            )
            pos_a, neg_a, pos_b, neg_b = leak(freq_a), leak(-freq_a), leak(freq_b), leak(-freq_b)
            spec = np.zeros((2, 4 * half, width + 1), complex)
            if g == 0:
                zero = (freq_a == 0)[:, None]
                spec[0, re_a] = np.where(zero, pos_a, root * (pos_a + neg_a))
                spec[0, im_a] = np.where(zero, 0.0, root * 1j * (pos_a - neg_a))
                spec[1, re_b] = root * (pos_b + neg_b)
                spec[1, im_b] = root * 1j * (pos_b - neg_b)
            else:
                spec[0, re_a], spec[0, im_a] = root * pos_a, root * 1j * pos_a
                spec[0, re_b], spec[0, im_b] = root * neg_b, -root * 1j * neg_b
                spec[1, re_b], spec[1, im_b] = root * pos_b, root * 1j * pos_b
                spec[1, re_a], spec[1, im_a] = root * neg_a, -root * 1j * neg_a
            table = to_bins[side, g]
            table[:, 0], table[:, 1] = spec[0, :, :width].real, spec[0, :, :width].imag
            table[:, 2], table[:, 3] = spec[1, :, :width].real, spec[1, :, :width].imag
            if g == 0:
                ends = (spec[0, :, 0].real, spec[1, :, 0].real, spec[0, :, width].real, spec[1, :, width].real)
            else:
                ends = tuple(
                    math.sqrt(2.0) * v
                    for v in (spec[0, :, 0].real, spec[0, :, 0].imag, spec[0, :, width].real, spec[0, :, width].imag)
                )
            for q in range(4):
                table[:, q, 0] = ends[q]
    lags = np.arange(LAGS)
    phase = 2 * np.pi * ((steps[:, None] * lags[None]) % (2 * width)) / (2 * width)
    lag = np.stack([2 * np.cos(phase), -2 * np.sin(phase)])
    lag[0, 0], lag[1, 0] = 1.0, (-1.0) ** lags
    bf16 = ml_dtypes.bfloat16
    forward_t = forward.transpose(0, 2, 1)
    forward_hi = forward_t.astype(bf16)
    forward_lo = (forward_t - forward_hi.astype(np.float64)).astype(bf16)
    bins_t = to_bins.transpose(0, 1, 3, 4, 2).reshape(2, groups, 4 * width, 4 * half).astype(bf16)
    lag_t = lag.reshape(2 * width, LAGS).T.astype(bf16)
    scale = residues / (2.0 * width * samples) / math.sqrt(samples)
    return forward_hi, forward_lo, bins_t, lag_t, scale


def real_dft(values):
    n = len(values)
    if n == 2:
        return [(values[0] + values[1], None), (values[0] - values[1], None)]
    even, odd = real_dft(values[0::2]), real_dft(values[1::2])
    out = [None] * (n // 2 + 1)
    for k in range(n // 4 + 1):
        (er, ei), (pr, pi) = even[k], odd[k]
        angle = -2.0 * math.pi * k / n
        c, s = math.cos(angle), math.sin(angle)
        if k == 0:
            out[0] = (er + pr, None)
            out[n // 2] = (er - pr, None)
            continue
        if 4 * k == n:
            out[k] = (er, -pr)
            continue
        if pi is None:
            tr, ti = pr * c, pr * s
        elif 8 * k == n:
            tr, ti = (pr + pi) * c, (pi - pr) * c
        else:
            tr, ti = pr * c - pi * s, pr * s + pi * c
        if ei is None:
            out[k] = (er + tr, ti)
            out[n // 2 - k] = (er - tr, ti)
        else:
            out[k] = (er + tr, ei + ti)
            out[n // 2 - k] = (er - tr, ti - ei)
    return out


def prepare_kernel(own, first_ref, second_ref, fhi_hbm, flo_hbm, bins_hbm, out_ref,
                   fhi, flo, bins, yhi, ylo, spec, wide, sems):
    windows, channels, samples = first_ref.shape
    width = LAGS
    residues = samples // width
    groups = residues // 2
    rows = 2 * windows * channels
    lanes = 2 * channels
    copies = [
        pltpu.make_async_copy(src, dst, sems.at[i])
        for i, (src, dst) in enumerate(((fhi_hbm, fhi), (flo_hbm, flo), (bins_hbm, bins)))
    ]
    for copy in copies:
        copy.start()

    step = 16
    per_window = channels // step

    def split(value):
        high = value.astype(jnp.bfloat16)
        return high, (value - high.astype(jnp.float32)).astype(jnp.bfloat16)

    def transform(n, carry):
        w, c = n // per_window, n % per_window
        for which, ref in enumerate((first_ref, second_ref)):
            if own and which:
                continue
            block = ref[w, pl.ds(pl.multiple_of(c * step, step), step), :].astype(jnp.float32)
            terms = real_dft([block[:, a * width:(a + 1) * width] for a in range(residues)])
            for g in range(groups):
                if g == 0:
                    parts = (terms[0][0], terms[groups][0])
                else:
                    parts = terms[g]
                for side, part in enumerate(parts):
                    hi, lo = split(part)
                    for copy_to in ((0, 1) if own else (which,)):
                        row = pl.multiple_of(w * lanes + copy_to * channels + c * step, step)
                        yhi[g, pl.ds(row, step), side * width:(side + 1) * width] = hi
                        ylo[g, pl.ds(row, step), side * width:(side + 1) * width] = lo
        return carry

    lax.fori_loop(0, windows * per_window, transform, 0)
    copies[0].wait()
    copies[1].wait()
    nt = (((1,), (1,)), ((), ()))
    bands = (samples // 2) // BAND

    def forward(g, power):
        value = lax.dot_general(fhi[g], yhi[g], nt, preferred_element_type=jnp.float32)
        value += lax.dot_general(flo[g], yhi[g], nt, preferred_element_type=jnp.float32)
        value += lax.dot_general(fhi[g], ylo[g], nt, preferred_element_type=jnp.float32)
        spec[g] = value
        squared = (value * value).reshape(2 * width // bands, bands, rows)
        return power + squared.sum(0)

    power = lax.fori_loop(0, groups, forward, jnp.zeros((bands, rows), jnp.float32), unroll=4)
    gain = 1.0 / jnp.sqrt(power * (1.0 / BAND) + 1e-6)
    copies[2].wait()

    def to_bins(g, carry):
        white = (spec[g].reshape(2 * width // bands, bands, rows) * gain[None]).reshape(2 * width, rows)
        value = jnp.dot(bins[g], white.astype(jnp.bfloat16), preferred_element_type=jnp.float32)
        parts = [value[q * width:(q + 1) * width] for q in range(4)]
        if own:
            left = lax.broadcasted_iota(jnp.int32, (width, rows), 1) % lanes < channels
            ends = lax.broadcasted_iota(jnp.int32, (width, rows), 0) == 0
            turned = [parts[1], -parts[0], parts[3], -parts[2]]
            zero = jnp.zeros_like(parts[0])
            real = [parts[q] if q < 2 else jnp.where(ends, zero, parts[q]) for q in range(4)]
            imag = [jnp.where(ends, zero if q < 2 else parts[q], turned[q]) for q in range(4)]
            parts = [jnp.where(left, real[q], imag[q]) for q in range(4)]
        for q in range(4):
            for w in range(windows):
                start = w * (groups * 4) + g * 4 + q
                wide[pl.ds(start, width, stride=windows * groups * 4), :] = parts[q][:, w * lanes:(w + 1) * lanes]
        return carry

    lax.fori_loop(0, groups, to_bins, 0, unroll=4)
    depth = windows * groups * 4

    def narrow(k, carry):
        block = wide[pl.ds(pl.multiple_of(k * depth, depth), depth), :]
        out_ref[k] = (block.T if own else block).astype(jnp.bfloat16)
        return carry

    lax.fori_loop(0, width, narrow, 0, unroll=8)


def prepare(first, second, tables, own):
    windows, channels, samples = first.shape
    forward_hi, forward_lo, bins_t = tables
    width = LAGS
    groups = samples // width // 2
    rows = 2 * windows * channels
    depth = windows * groups * 4
    lanes = 2 * channels
    shape = (width, lanes, depth) if own else (width, depth, lanes)
    any_spec = pl.BlockSpec(memory_space=pl.ANY)
    vmem_spec = pl.BlockSpec(memory_space=pltpu.VMEM)
    flops = 2 * groups * rows * (3 * 4 * width * width + 8 * width * width)
    return pl.pallas_call(
        functools.partial(prepare_kernel, own),
        out_shape=jax.ShapeDtypeStruct(shape, jnp.bfloat16),
        in_specs=[vmem_spec, vmem_spec, any_spec, any_spec, any_spec],
        out_specs=vmem_spec,
        scratch_shapes=[
            pltpu.VMEM(forward_hi.shape, jnp.bfloat16),
            pltpu.VMEM(forward_lo.shape, jnp.bfloat16),
            pltpu.VMEM(bins_t.shape, jnp.bfloat16),
            pltpu.VMEM((groups, rows, 2 * width), jnp.bfloat16),
            pltpu.VMEM((groups, rows, 2 * width), jnp.bfloat16),
            pltpu.VMEM((groups, 2 * width, rows), jnp.float32),
            pltpu.VMEM((width * depth, lanes), jnp.float32),
            pltpu.SemaphoreType.DMA((3,)),
        ],
        compiler_params=pltpu.CompilerParams(vmem_limit_bytes=VMEM_LIMIT),
        cost_estimate=pl.CostEstimate(flops=flops, bytes_accessed=14 * 2**20, transcendentals=0),
        name="prepare_own" if own else "prepare_partners",
    )(first, second, forward_hi, forward_lo, bins_t)


def stack_kernel(chunks, per_chunk, per_out, own_ref, first_ref, second_ref, lag_ref, slot_ref, keep_ref, out_ref, *cross):
    step = pl.program_id(0)
    width = LAGS
    lanes = first_ref.shape[2]
    channels = lanes // 2

    @pl.when(step < chunks)
    def _():
        def one(n, carry):
            k = step * per_chunk + n
            partners = jnp.concatenate([first_ref[n], second_ref[n]], axis=1)
            value = jnp.dot(own_ref[n], partners, preferred_element_type=jnp.float32)
            for side in range(2):
                for part in range(2):
                    cross[side][pl.ds(part * width + k, channels, stride=2 * width), :] = (
                        value[part * channels:(part + 1) * channels, side * lanes:(side + 1) * lanes]
                    )
            return carry

        lax.fori_loop(0, per_chunk, one, 0, unroll=8)

    @pl.when(step >= chunks)
    def _():
        def one(n, carry):
            i = (step - chunks) * per_out + n
            part = pl.ds(pl.multiple_of(i * 2 * width, 2 * width), 2 * width)
            block = jnp.concatenate([ref[part, :].astype(jnp.bfloat16) for ref in cross], axis=1)
            value = jnp.dot(lag_ref[...], block, preferred_element_type=jnp.float32).T
            for o in range(out_ref.shape[0]):
                out_ref[slot_ref[o], n] = value[o * channels:(o + 1) * channels] * keep_ref[o]
            return carry

        lax.fori_loop(0, per_out, one, 0, unroll=4)


def stack(own, first, second, lag_t, slots, keep):
    width, lanes, depth = own.shape
    channels = lanes // 2
    chunks, out_chunks = 4, 8
    per_chunk, per_out = width // chunks, channels // out_chunks
    block = lambda s: (jnp.minimum(s, chunks - 1), 0, 0)
    offsets = keep.shape[0]
    return pl.pallas_call(
        functools.partial(stack_kernel, chunks, per_chunk, per_out),
        grid=(chunks + out_chunks,),
        out_shape=jax.ShapeDtypeStruct((offsets, channels, channels, LAGS), jnp.float32),
        in_specs=[
            pl.BlockSpec((per_chunk, lanes, depth), block),
            pl.BlockSpec((per_chunk, depth, lanes), block),
            pl.BlockSpec((per_chunk, depth, lanes), block),
            pl.BlockSpec(lag_t.shape, lambda s: (0, 0)),
            pl.BlockSpec(memory_space=pltpu.SMEM),
            pl.BlockSpec(memory_space=pltpu.SMEM),
        ],
        out_specs=pl.BlockSpec(
            (offsets, per_out, channels, LAGS), lambda s: (0, jnp.maximum(s - chunks, 0), 0, 0)
        ),
        scratch_shapes=[pltpu.VMEM((channels * 2 * width, lanes), jnp.float32)] * 2,
        compiler_params=pltpu.CompilerParams(
            vmem_limit_bytes=VMEM_LIMIT, dimension_semantics=("arbitrary",)
        ),
        name="stack_lags",
    )(own, first, second, lag_t, slots, keep)


def per_device(traces, live, reach):
    windows, channels, samples = traces.shape
    blocks = lax.axis_size("fibre")
    splits = lax.axis_size("freq")
    owned = OFF // splits
    place = lax.axis_index("freq")
    forward_hi, forward_lo, bins_t, lag_t, scale = build_tables(samples)
    forward_hi, forward_lo = jnp.asarray(forward_hi), jnp.asarray(forward_lo)
    masked = traces * live.astype(traces.dtype)[None, :, None]

    quads = blocks // owned
    half = owned // 2
    u = lax.axis_index("fibre") % owned
    core, pair = u % half, u // half

    def rank(q, pair, core, part):
        return (q * owned + pair * half + core) * splits + part

    def send(payload, route):
        pairs = []
        for q in range(quads):
            for p in range(2):
                for c in range(half):
                    for g in range(splits):
                        source = route(q, p, c, g)
                        if source[0] < quads:
                            pairs.append((rank(*source), rank(q, p, c, g)))
        return lax.ppermute(payload, ("fibre", "freq"), pairs)

    upper = send(masked, lambda q, p, c, g: (q + 1, p, c, g))
    own = prepare(masked, masked, (forward_hi, forward_lo, jnp.asarray(bins_t[1])), True)
    upper, own = lax.optimization_barrier((upper, own))
    across_payload = jnp.where((pair == 1) & (place == 0), masked, upper)
    across = send(across_payload, lambda q, p, c, g: (q + p * g, 1 - p, c, g))
    core_payload = jnp.where((core == 1) & (place == 0), masked, upper)
    beside = send(core_payload, lambda q, p, c, g: (q + c * g, p, 1 - c, g))
    across_beside = send(across, lambda q, p, c, g: (q, p, 1 - c, g))
    here = jnp.where(place == 0, masked, upper)

    partner_tables = (forward_hi, forward_lo, jnp.asarray(bins_t[0]))
    first = prepare(here, across, partner_tables, False)
    second = prepare(beside, across_beside, partner_tables, False)
    slots = jnp.stack([0, 2, 1 + 2 * core, 3 - 2 * core]).astype(jnp.int32)
    offset_ids = place * owned + slots
    keep = jnp.where(offset_ids < reach[0], jnp.float32(scale), jnp.float32(0.0))
    return stack(own, first, second, jnp.asarray(lag_t), slots, keep)[None]


def solution(mesh):
    placed = (P(None, "fibre", None), P("fibre"), P("fibre"))
    return jax.shard_map(
        per_device,
        mesh=mesh,
        in_specs=placed,
        out_specs=P("fibre", "freq", None, None, None),
        check_vma=False,
    )
```

```python
import functools
import math

import jax
import jax.numpy as jnp
import ml_dtypes
import numpy as np
from jax import lax
from jax.experimental import pallas as pl
from jax.experimental.pallas import tpu as pltpu
from jax.sharding import PartitionSpec as P

BAND = 64
OFF = 8
LAGS = 128
VMEM_LIMIT = 56 * 1024 * 1024


def leak_spectrum(freqs, samples, window, shift, slots, period):
    steps = np.arange(window)
    tone = np.exp(2j * np.pi * ((freqs[:, None] * (steps - shift)[None]) % samples) / samples)
    bins = np.exp(-2j * np.pi * ((steps[:, None] * slots[None]) % period) / period)
    return tone @ bins


@functools.lru_cache(maxsize=None)
def build_tables(samples):
    width = LAGS
    residues = samples // width
    groups = residues // 2
    half = width // 2
    per_band = BAND // residues
    order = np.concatenate([np.arange(i, half, per_band) for i in range(per_band)])
    steps = np.arange(width)
    slots = np.arange(width + 1)
    forward = np.zeros((groups, 2 * width, 4 * half))
    to_bins = np.zeros((2, groups, 4 * half, 4, width))
    root = 1.0 / math.sqrt(2.0)
    re_a, im_a, re_b, im_b = (slice(i * half, (i + 1) * half) for i in range(4))
    for g in range(groups):
        freq_a = g + residues * order
        freq_b = (residues - g if g else groups) + residues * order
        wave_a = np.exp(-2j * np.pi * ((steps[:, None] * freq_a[None]) % samples) / samples)
        wave_b = np.exp(-2j * np.pi * ((steps[:, None] * freq_b[None]) % samples) / samples)
        top, low = forward[g, :width], forward[g, width:]
        top[:, re_a], top[:, im_a] = wave_a.real, wave_a.imag
        if g == 0:
            low[:, re_b], low[:, im_b] = wave_b.real, wave_b.imag
        else:
            low[:, re_a], low[:, im_a] = -wave_a.imag, wave_a.real
            top[:, re_b], top[:, im_b] = wave_b.real, wave_b.imag
            low[:, re_b], low[:, im_b] = wave_b.imag, -wave_b.real
        for side in range(2):
            window, shift = ((width, 0), (2 * width, half))[side]
            leak = functools.partial(
                leak_spectrum, samples=samples, window=window, shift=shift, slots=slots, period=2 * width
            )
            pos_a, neg_a, pos_b, neg_b = leak(freq_a), leak(-freq_a), leak(freq_b), leak(-freq_b)
            spec = np.zeros((2, 4 * half, width + 1), complex)
            if g == 0:
                zero = (freq_a == 0)[:, None]
                spec[0, re_a] = np.where(zero, pos_a, root * (pos_a + neg_a))
                spec[0, im_a] = np.where(zero, 0.0, root * 1j * (pos_a - neg_a))
                spec[1, re_b] = root * (pos_b + neg_b)
                spec[1, im_b] = root * 1j * (pos_b - neg_b)
            else:
                spec[0, re_a], spec[0, im_a] = root * pos_a, root * 1j * pos_a
                spec[0, re_b], spec[0, im_b] = root * neg_b, -root * 1j * neg_b
                spec[1, re_b], spec[1, im_b] = root * pos_b, root * 1j * pos_b
                spec[1, re_a], spec[1, im_a] = root * neg_a, -root * 1j * neg_a
            table = to_bins[side, g]
            table[:, 0], table[:, 1] = spec[0, :, :width].real, spec[0, :, :width].imag
            table[:, 2], table[:, 3] = spec[1, :, :width].real, spec[1, :, :width].imag
            if g == 0:
                ends = (spec[0, :, 0].real, spec[1, :, 0].real, spec[0, :, width].real, spec[1, :, width].real)
            else:
                ends = tuple(
                    math.sqrt(2.0) * v
                    for v in (spec[0, :, 0].real, spec[0, :, 0].imag, spec[0, :, width].real, spec[0, :, width].imag)
                )
            for q in range(4):
                table[:, q, 0] = ends[q]
    lags = np.arange(LAGS)
    phase = 2 * np.pi * ((steps[:, None] * lags[None]) % (2 * width)) / (2 * width)
    lag = np.stack([2 * np.cos(phase), -2 * np.sin(phase)])
    lag[0, 0], lag[1, 0] = 1.0, (-1.0) ** lags
    bf16 = ml_dtypes.bfloat16
    forward_t = forward.transpose(0, 2, 1)
    forward_hi = forward_t.astype(bf16)
    forward_lo = (forward_t - forward_hi.astype(np.float64)).astype(bf16)
    bins_t = to_bins.transpose(0, 1, 3, 4, 2).reshape(2, groups, 4 * width, 4 * half).astype(bf16)
    lag_t = lag.reshape(2 * width, LAGS).T.astype(bf16)
    scale = residues / (2.0 * width * samples) / math.sqrt(samples)
    return forward_hi, forward_lo, bins_t, lag_t, scale


def real_dft(values):
    n = len(values)
    if n == 2:
        return [(values[0] + values[1], None), (values[0] - values[1], None)]
    even, odd = real_dft(values[0::2]), real_dft(values[1::2])
    out = [None] * (n // 2 + 1)
    for k in range(n // 4 + 1):
        (er, ei), (pr, pi) = even[k], odd[k]
        angle = -2.0 * math.pi * k / n
        c, s = math.cos(angle), math.sin(angle)
        if k == 0:
            out[0] = (er + pr, None)
            out[n // 2] = (er - pr, None)
            continue
        if 4 * k == n:
            out[k] = (er, -pr)
            continue
        if pi is None:
            tr, ti = pr * c, pr * s
        elif 8 * k == n:
            tr, ti = (pr + pi) * c, (pi - pr) * c
        else:
            tr, ti = pr * c - pi * s, pr * s + pi * c
        if ei is None:
            out[k] = (er + tr, ti)
            out[n // 2 - k] = (er - tr, ti)
        else:
            out[k] = (er + tr, ei + ti)
            out[n // 2 - k] = (er - tr, ti - ei)
    return out


def prepare_kernel(own, first_ref, second_ref, fhi_hbm, flo_hbm, bins_hbm, out_ref,
                   fhi, flo, bins, yhi, ylo, spec, wide, sems):
    windows, channels, samples = first_ref.shape
    width = LAGS
    residues = samples // width
    groups = residues // 2
    rows = 2 * windows * channels
    lanes = 2 * channels
    depth = windows * groups * 4
    copies = [
        pltpu.make_async_copy(src, dst, sems.at[i])
        for i, (src, dst) in enumerate(((fhi_hbm, fhi), (flo_hbm, flo), (bins_hbm, bins)))
    ]
    for copy in copies:
        copy.start()

    step = 16
    per_window = channels // step

    def split(value):
        high = value.astype(jnp.bfloat16)
        return high, (value - high.astype(jnp.float32)).astype(jnp.bfloat16)

    def transform(n, carry):
        w, c = n // per_window, n % per_window
        for which, ref in enumerate((first_ref, second_ref)):
            if own and which:
                continue
            block = ref[w, pl.ds(pl.multiple_of(c * step, step), step), :].astype(jnp.float32)
            terms = real_dft([block[:, a * width:(a + 1) * width] for a in range(residues)])
            for g in range(groups):
                if g == 0:
                    parts = (terms[0][0], terms[groups][0])
                else:
                    parts = terms[g]
                for side, part in enumerate(parts):
                    hi, lo = split(part)
                    for copy_to in ((0, 1) if own else (which,)):
                        row = pl.multiple_of(w * lanes + copy_to * channels + c * step, step)
                        yhi[g, pl.ds(row, step), side * width:(side + 1) * width] = hi
                        ylo[g, pl.ds(row, step), side * width:(side + 1) * width] = lo
        return carry

    lax.fori_loop(0, windows * per_window, transform, 0)
    copies[0].wait()
    copies[1].wait()
    nt = (((1,), (1,)), ((), ()))
    bands = (samples // 2) // BAND

    def forward(g, power):
        value = lax.dot_general(fhi[g], yhi[g], nt, preferred_element_type=jnp.float32)
        value += lax.dot_general(flo[g], yhi[g], nt, preferred_element_type=jnp.float32)
        value += lax.dot_general(fhi[g], ylo[g], nt, preferred_element_type=jnp.float32)
        spec[g] = value
        squared = (value * value).reshape(2 * width // bands, bands, rows)
        return power + squared.sum(0)

    power = lax.fori_loop(0, groups, forward, jnp.zeros((bands, rows), jnp.float32), unroll=4)
    gain = 1.0 / jnp.sqrt(power * (1.0 / BAND) + 1e-6)
    copies[2].wait()

    def to_bins(g, carry):
        white = (spec[g].reshape(2 * width // bands, bands, rows) * gain[None]).reshape(2 * width, rows)
        value = jnp.dot(bins[g], white.astype(jnp.bfloat16), preferred_element_type=jnp.float32)
        parts = [value[q * width:(q + 1) * width] for q in range(4)]
        if own:
            left = lax.broadcasted_iota(jnp.int32, (width, rows), 1) % lanes < channels
            ends = lax.broadcasted_iota(jnp.int32, (width, rows), 0) == 0
            turned = [parts[1], -parts[0], parts[3], -parts[2]]
            zero = jnp.zeros_like(parts[0])
            real = [parts[q] if q < 2 else jnp.where(ends, zero, parts[q]) for q in range(4)]
            imag = [jnp.where(ends, zero if q < 2 else parts[q], turned[q]) for q in range(4)]
            parts = [jnp.where(left, real[q], imag[q]) for q in range(4)]
        for q in range(4):
            for w in range(windows):
                start = w * (groups * 4) + g * 4 + q
                wide[pl.ds(start, width, stride=depth + 1), :] = parts[q][:, w * lanes:(w + 1) * lanes]
        return carry

    lax.fori_loop(0, groups, to_bins, 0, unroll=4)
    def narrow(k, carry):
        block = wide[pl.ds(k * (depth + 1), depth), :]
        out_ref[k] = (block.T if own else block).astype(jnp.bfloat16)
        return carry

    lax.fori_loop(0, width, narrow, 0, unroll=8)


def prepare(first, second, tables, own):
    windows, channels, samples = first.shape
    forward_hi, forward_lo, bins_t = tables
    width = LAGS
    groups = samples // width // 2
    rows = 2 * windows * channels
    depth = windows * groups * 4
    lanes = 2 * channels
    shape = (width, lanes, depth) if own else (width, depth, lanes)
    any_spec = pl.BlockSpec(memory_space=pl.ANY)
    vmem_spec = pl.BlockSpec(memory_space=pltpu.VMEM)
    flops = 2 * groups * rows * (3 * 4 * width * width + 8 * width * width)
    return pl.pallas_call(
        functools.partial(prepare_kernel, own),
        out_shape=jax.ShapeDtypeStruct(shape, jnp.bfloat16),
        in_specs=[vmem_spec, vmem_spec, any_spec, any_spec, any_spec],
        out_specs=vmem_spec,
        scratch_shapes=[
            pltpu.VMEM(forward_hi.shape, jnp.bfloat16),
            pltpu.VMEM(forward_lo.shape, jnp.bfloat16),
            pltpu.VMEM(bins_t.shape, jnp.bfloat16),
            pltpu.VMEM((groups, rows, 2 * width), jnp.bfloat16),
            pltpu.VMEM((groups, rows, 2 * width), jnp.bfloat16),
            pltpu.VMEM((groups, 2 * width, rows), jnp.float32),
            pltpu.VMEM((width * (depth + 1), lanes), jnp.float32),
            pltpu.SemaphoreType.DMA((3,)),
        ],
        compiler_params=pltpu.CompilerParams(vmem_limit_bytes=VMEM_LIMIT),
        cost_estimate=pl.CostEstimate(flops=flops, bytes_accessed=14 * 2**20, transcendentals=0),
        name="prepare_own" if own else "prepare_partners",
    )(first, second, forward_hi, forward_lo, bins_t)


def stack_kernel(chunks, per_chunk, per_out, own_ref, first_ref, second_ref, lag_ref, slot_ref, keep_ref, out_ref, *cross):
    step = pl.program_id(0)
    width = LAGS
    lanes = first_ref.shape[2]
    channels = lanes // 2

    @pl.when(step < chunks)
    def _():
        def one(n, carry):
            k = step * per_chunk + n
            partners = jnp.concatenate([first_ref[n], second_ref[n]], axis=1)
            value = jnp.dot(own_ref[n], partners, preferred_element_type=jnp.float32)
            for side in range(2):
                for part in range(2):
                    cross[side][pl.ds(part * width + k, channels, stride=2 * width + 1), :] = (
                        value[part * channels:(part + 1) * channels, side * lanes:(side + 1) * lanes]
                    )
            return carry

        lax.fori_loop(0, per_chunk, one, 0, unroll=8)

    @pl.when(step >= chunks)
    def _():
        def one(n, carry):
            i = (step - chunks) * per_out + n
            part = pl.ds(i * (2 * width + 1), 2 * width)
            block = jnp.concatenate([ref[part, :].astype(jnp.bfloat16) for ref in cross], axis=1)
            value = jnp.dot(lag_ref[...], block, preferred_element_type=jnp.float32).T
            for o in range(out_ref.shape[0]):
                out_ref[slot_ref[o], n] = value[o * channels:(o + 1) * channels] * keep_ref[o]
            return carry

        lax.fori_loop(0, per_out, one, 0, unroll=4)


def stack(own, first, second, lag_t, slots, keep):
    width, lanes, depth = own.shape
    channels = lanes // 2
    chunks, out_chunks = 4, 8
    per_chunk, per_out = width // chunks, channels // out_chunks
    block = lambda s: (jnp.minimum(s, chunks - 1), 0, 0)
    offsets = keep.shape[0]
    return pl.pallas_call(
        functools.partial(stack_kernel, chunks, per_chunk, per_out),
        grid=(chunks + out_chunks,),
        out_shape=jax.ShapeDtypeStruct((offsets, channels, channels, LAGS), jnp.float32),
        in_specs=[
            pl.BlockSpec((per_chunk, lanes, depth), block),
            pl.BlockSpec((per_chunk, depth, lanes), block),
            pl.BlockSpec((per_chunk, depth, lanes), block),
            pl.BlockSpec(lag_t.shape, lambda s: (0, 0)),
            pl.BlockSpec(memory_space=pltpu.SMEM),
            pl.BlockSpec(memory_space=pltpu.SMEM),
        ],
        out_specs=pl.BlockSpec(
            (offsets, per_out, channels, LAGS), lambda s: (0, jnp.maximum(s - chunks, 0), 0, 0)
        ),
        scratch_shapes=[pltpu.VMEM((channels * (2 * width + 1), lanes), jnp.float32)] * 2,
        compiler_params=pltpu.CompilerParams(
            vmem_limit_bytes=VMEM_LIMIT, dimension_semantics=("arbitrary",)
        ),
        name="stack_lags",
    )(own, first, second, lag_t, slots, keep)


def per_device(traces, live, reach):
    windows, channels, samples = traces.shape
    blocks = lax.axis_size("fibre")
    splits = lax.axis_size("freq")
    owned = OFF // splits
    place = lax.axis_index("freq")
    forward_hi, forward_lo, bins_t, lag_t, scale = build_tables(samples)
    forward_hi, forward_lo = jnp.asarray(forward_hi), jnp.asarray(forward_lo)
    masked = traces * live.astype(traces.dtype)[None, :, None]

    quads = blocks // owned
    half = owned // 2
    u = lax.axis_index("fibre") % owned
    core, pair = u % half, u // half

    def rank(q, pair, core, part):
        return (q * owned + pair * half + core) * splits + part

    def send(payload, route):
        pairs = []
        for q in range(quads):
            for p in range(2):
                for c in range(half):
                    for g in range(splits):
                        source = route(q, p, c, g)
                        if source[0] < quads:
                            pairs.append((rank(*source), rank(q, p, c, g)))
        return lax.ppermute(payload, ("fibre", "freq"), pairs)

    upper = send(masked, lambda q, p, c, g: (q + 1, p, c, g))
    own = prepare(masked, masked, (forward_hi, forward_lo, jnp.asarray(bins_t[1])), True)
    upper, own = lax.optimization_barrier((upper, own))
    core_payload = jnp.where((core == 1) & (place == 0), masked, upper)
    across_payload = jnp.where((pair == 1) & (place == 0), masked, upper)
    beside = send(core_payload, lambda q, p, c, g: (q + c * g, p, 1 - c, 1 - g if c else g))
    across = send(across_payload, lambda q, p, c, g: (q + p * g, 1 - p, c, g))
    here = jnp.where(place == 0, masked, upper)
    partner_tables = (forward_hi, forward_lo, jnp.asarray(bins_t[0]))
    first = prepare(here, beside, partner_tables, False)
    across, first = lax.optimization_barrier((across, first))
    across_beside = send(across, lambda q, p, c, g: (q, p, 1 - c, g))
    second = prepare(across, across_beside, partner_tables, False)
    slots = jnp.stack([0, 1 + 2 * core, 2, 3 - 2 * core]).astype(jnp.int32)
    offset_ids = place * owned + slots
    keep = jnp.where(offset_ids < reach[0], jnp.float32(scale), jnp.float32(0.0))
    return stack(own, first, second, jnp.asarray(lag_t), slots, keep)[None]


def solution(mesh):
    placed = (P(None, "fibre", None), P("fibre"), P("fibre"))
    return jax.shard_map(
        per_device,
        mesh=mesh,
        in_specs=placed,
        out_specs=P("fibre", "freq", None, None, None),
        check_vma=False,
    )
```

```python
import functools
import math

import jax
import jax.numpy as jnp
import ml_dtypes
import numpy as np
from jax import lax
from jax.experimental import pallas as pl
from jax.experimental.pallas import tpu as pltpu
from jax.sharding import PartitionSpec as P

BAND = 64
OFF = 8
LAGS = 128
VMEM_LIMIT = 36 * 1024 * 1024


def leak_spectrum(freqs, samples, window, shift, slots, period):
    steps = np.arange(window)
    tone = np.exp(2j * np.pi * ((freqs[:, None] * (steps - shift)[None]) % samples) / samples)
    bins = np.exp(-2j * np.pi * ((steps[:, None] * slots[None]) % period) / period)
    return tone @ bins


@functools.lru_cache(maxsize=None)
def build_tables(samples):
    width = LAGS
    residues = samples // width
    groups = residues // 2
    half = width // 2
    per_band = BAND // residues
    order = np.concatenate([np.arange(i, half, per_band) for i in range(per_band)])
    steps = np.arange(width)
    slots = np.arange(width + 1)
    forward = np.zeros((groups, 2 * width, 4 * half))
    to_bins = np.zeros((2, groups, 4 * half, 4, width))
    root = 1.0 / math.sqrt(2.0)
    re_a, im_a, re_b, im_b = (slice(i * half, (i + 1) * half) for i in range(4))
    for g in range(groups):
        freq_a = g + residues * order
        freq_b = (residues - g if g else groups) + residues * order
        wave_a = np.exp(-2j * np.pi * ((steps[:, None] * freq_a[None]) % samples) / samples)
        wave_b = np.exp(-2j * np.pi * ((steps[:, None] * freq_b[None]) % samples) / samples)
        top, low = forward[g, :width], forward[g, width:]
        top[:, re_a], top[:, im_a] = wave_a.real, wave_a.imag
        if g == 0:
            low[:, re_b], low[:, im_b] = wave_b.real, wave_b.imag
        else:
            low[:, re_a], low[:, im_a] = -wave_a.imag, wave_a.real
            top[:, re_b], top[:, im_b] = wave_b.real, wave_b.imag
            low[:, re_b], low[:, im_b] = wave_b.imag, -wave_b.real
        for side in range(2):
            window, shift = ((width, 0), (2 * width, half))[side]
            leak = functools.partial(
                leak_spectrum, samples=samples, window=window, shift=shift, slots=slots, period=2 * width
            )
            pos_a, neg_a, pos_b, neg_b = leak(freq_a), leak(-freq_a), leak(freq_b), leak(-freq_b)
            spec = np.zeros((2, 4 * half, width + 1), complex)
            if g == 0:
                zero = (freq_a == 0)[:, None]
                spec[0, re_a] = np.where(zero, pos_a, root * (pos_a + neg_a))
                spec[0, im_a] = np.where(zero, 0.0, root * 1j * (pos_a - neg_a))
                spec[1, re_b] = root * (pos_b + neg_b)
                spec[1, im_b] = root * 1j * (pos_b - neg_b)
            else:
                spec[0, re_a], spec[0, im_a] = root * pos_a, root * 1j * pos_a
                spec[0, re_b], spec[0, im_b] = root * neg_b, -root * 1j * neg_b
                spec[1, re_b], spec[1, im_b] = root * pos_b, root * 1j * pos_b
                spec[1, re_a], spec[1, im_a] = root * neg_a, -root * 1j * neg_a
            table = to_bins[side, g]
            table[:, 0], table[:, 1] = spec[0, :, :width].real, spec[0, :, :width].imag
            table[:, 2], table[:, 3] = spec[1, :, :width].real, spec[1, :, :width].imag
            if g == 0:
                ends = (spec[0, :, 0].real, spec[1, :, 0].real, spec[0, :, width].real, spec[1, :, width].real)
            else:
                ends = tuple(
                    math.sqrt(2.0) * v
                    for v in (spec[0, :, 0].real, spec[0, :, 0].imag, spec[0, :, width].real, spec[0, :, width].imag)
                )
            for q in range(4):
                table[:, q, 0] = ends[q]
    lags = np.arange(LAGS)
    phase = 2 * np.pi * ((steps[:, None] * lags[None]) % (2 * width)) / (2 * width)
    lag = np.stack([2 * np.cos(phase), -2 * np.sin(phase)])
    lag[0, 0], lag[1, 0] = 1.0, (-1.0) ** lags
    bf16 = ml_dtypes.bfloat16
    forward_t = forward.transpose(0, 2, 1)
    forward_hi = forward_t.astype(bf16)
    forward_lo = (forward_t - forward_hi.astype(np.float64)).astype(bf16)
    bins_t = to_bins.transpose(0, 1, 3, 4, 2).reshape(2, groups, 4 * width, 4 * half).astype(bf16)
    lag_t = lag.reshape(2 * width, LAGS).T.astype(bf16)
    scale = residues / (2.0 * width * samples) / math.sqrt(samples)
    return forward_hi, forward_lo, bins_t, lag_t, scale


def real_dft(values):
    n = len(values)
    if n == 2:
        return [(values[0] + values[1], None), (values[0] - values[1], None)]
    even, odd = real_dft(values[0::2]), real_dft(values[1::2])
    out = [None] * (n // 2 + 1)
    for k in range(n // 4 + 1):
        (er, ei), (pr, pi) = even[k], odd[k]
        angle = -2.0 * math.pi * k / n
        c, s = math.cos(angle), math.sin(angle)
        if k == 0:
            out[0] = (er + pr, None)
            out[n // 2] = (er - pr, None)
            continue
        if 4 * k == n:
            out[k] = (er, -pr)
            continue
        if pi is None:
            tr, ti = pr * c, pr * s
        elif 8 * k == n:
            tr, ti = (pr + pi) * c, (pi - pr) * c
        else:
            tr, ti = pr * c - pi * s, pr * s + pi * c
        if ei is None:
            out[k] = (er + tr, ti)
            out[n // 2 - k] = (er - tr, ti)
        else:
            out[k] = (er + tr, ei + ti)
            out[n // 2 - k] = (er - tr, ti - ei)
    return out


def prepare_kernel(own, windows, *refs):
    records, refs = refs[:-12], refs[-12:]
    fhi_hbm, flo_hbm, bins_hbm, out_ref, fhi, flo, bins, yhi, ylo, spec, wide, sems = refs
    channels, samples = records[0].shape
    width = LAGS
    residues = samples // width
    groups = residues // 2
    rows = 2 * windows * channels
    lanes = 2 * channels
    depth = windows * groups * 4
    copies = [
        pltpu.make_async_copy(src, dst, sems.at[i])
        for i, (src, dst) in enumerate(((fhi_hbm, fhi), (flo_hbm, flo), (bins_hbm, bins)))
    ]
    for copy in copies:
        copy.start()

    step = 16

    def split(value):
        high = value.astype(jnp.bfloat16)
        return high, (value - high.astype(jnp.float32)).astype(jnp.bfloat16)

    def transform(n, carry):
        for index, ref in enumerate(records):
            which, w = divmod(index, windows)
            block = ref[pl.ds(pl.multiple_of(n * step, step), step), :].astype(jnp.float32)
            terms = real_dft([block[:, a * width:(a + 1) * width] for a in range(residues)])
            for g in range(groups):
                if g == 0:
                    parts = (terms[0][0], terms[groups][0])
                else:
                    parts = terms[g]
                for side, part in enumerate(parts):
                    hi, lo = split(part)
                    for copy_to in ((0, 1) if own else (which,)):
                        row = pl.multiple_of(w * lanes + copy_to * channels + n * step, step)
                        yhi[g, pl.ds(row, step), side * width:(side + 1) * width] = hi
                        ylo[g, pl.ds(row, step), side * width:(side + 1) * width] = lo
        return carry

    lax.fori_loop(0, channels // step, transform, 0)
    copies[0].wait()
    copies[1].wait()
    nt = (((1,), (1,)), ((), ()))
    bands = (samples // 2) // BAND

    def forward(g, power):
        value = lax.dot_general(fhi[g], yhi[g], nt, preferred_element_type=jnp.float32)
        value += lax.dot_general(flo[g], yhi[g], nt, preferred_element_type=jnp.float32)
        value += lax.dot_general(fhi[g], ylo[g], nt, preferred_element_type=jnp.float32)
        spec[g] = value
        squared = (value * value).reshape(2 * width // bands, bands, rows)
        return power + squared.sum(0)

    power = lax.fori_loop(0, groups, forward, jnp.zeros((bands, rows), jnp.float32), unroll=4)
    gain = 1.0 / jnp.sqrt(power * (1.0 / BAND) + 1e-6)
    copies[2].wait()

    def to_bins(g, carry):
        white = (spec[g].reshape(2 * width // bands, bands, rows) * gain[None]).reshape(2 * width, rows)
        value = jnp.dot(bins[g], white.astype(jnp.bfloat16), preferred_element_type=jnp.float32)
        parts = [value[q * width:(q + 1) * width] for q in range(4)]
        if own:
            left = lax.broadcasted_iota(jnp.int32, (width, rows), 1) % lanes < channels
            ends = lax.broadcasted_iota(jnp.int32, (width, rows), 0) == 0
            turned = [parts[1], -parts[0], parts[3], -parts[2]]
            zero = jnp.zeros_like(parts[0])
            real = [parts[q] if q < 2 else jnp.where(ends, zero, parts[q]) for q in range(4)]
            imag = [jnp.where(ends, zero if q < 2 else parts[q], turned[q]) for q in range(4)]
            parts = [jnp.where(left, real[q], imag[q]) for q in range(4)]
        for q in range(4):
            for w in range(windows):
                start = w * (groups * 4) + g * 4 + q
                wide[pl.ds(start, width, stride=depth + 1), :] = parts[q][:, w * lanes:(w + 1) * lanes]
        return carry

    lax.fori_loop(0, groups, to_bins, 0, unroll=4)
    def narrow(k, carry):
        block = wide[pl.ds(k * (depth + 1), depth), :]
        out_ref[k] = (block.T if own else block).astype(jnp.bfloat16)
        return carry

    lax.fori_loop(0, width, narrow, 0, unroll=8)


def prepare(records, windows, tables, own):
    channels, samples = records[0].shape
    forward_hi, forward_lo, bins_t = tables
    width = LAGS
    groups = samples // width // 2
    rows = 2 * windows * channels
    depth = windows * groups * 4
    lanes = 2 * channels
    shape = (width, lanes, depth) if own else (width, depth, lanes)
    any_spec = pl.BlockSpec(memory_space=pl.ANY)
    vmem_spec = pl.BlockSpec(memory_space=pltpu.VMEM)
    flops = 2 * groups * rows * (3 * 4 * width * width + 8 * width * width)
    return pl.pallas_call(
        functools.partial(prepare_kernel, own, windows),
        out_shape=jax.ShapeDtypeStruct(shape, jnp.bfloat16),
        in_specs=[vmem_spec] * len(records) + [any_spec] * 3,
        out_specs=vmem_spec,
        scratch_shapes=[
            pltpu.VMEM(forward_hi.shape, jnp.bfloat16),
            pltpu.VMEM(forward_lo.shape, jnp.bfloat16),
            pltpu.VMEM(bins_t.shape, jnp.bfloat16),
            pltpu.VMEM((groups, rows, 2 * width), jnp.bfloat16),
            pltpu.VMEM((groups, rows, 2 * width), jnp.bfloat16),
            pltpu.VMEM((groups, 2 * width, rows), jnp.float32),
            pltpu.VMEM((width * (depth + 1), lanes), jnp.float32),
            pltpu.SemaphoreType.DMA((3,)),
        ],
        compiler_params=pltpu.CompilerParams(vmem_limit_bytes=VMEM_LIMIT),
        cost_estimate=pl.CostEstimate(flops=flops, bytes_accessed=14 * 2**20, transcendentals=0),
        name="prepare_own" if own else "prepare_partners",
    )(*records, forward_hi, forward_lo, bins_t)


def stack_kernel(chunks, per_chunk, per_out, own_ref, first_ref, second_ref, lag_ref, slot_ref, keep_ref, out_ref, *cross):
    step = pl.program_id(0)
    width = LAGS
    lanes = first_ref.shape[2]
    channels = lanes // 2

    @pl.when(step < chunks)
    def _():
        def one(n, carry):
            k = step * per_chunk + n
            partners = jnp.concatenate([first_ref[n], second_ref[n]], axis=1)
            value = jnp.dot(own_ref[n], partners, preferred_element_type=jnp.float32)
            for side in range(2):
                for part in range(2):
                    cross[side][pl.ds(part * width + k, channels, stride=2 * width + 1), :] = (
                        value[part * channels:(part + 1) * channels, side * lanes:(side + 1) * lanes]
                    )
            return carry

        lax.fori_loop(0, per_chunk, one, 0, unroll=8)

    @pl.when(step >= chunks)
    def _():
        def one(n, carry):
            i = (step - chunks) * per_out + n
            part = pl.ds(i * (2 * width + 1), 2 * width)
            block = jnp.concatenate([ref[part, :].astype(jnp.bfloat16) for ref in cross], axis=1)
            value = jnp.dot(lag_ref[...], block, preferred_element_type=jnp.float32).T
            for o in range(out_ref.shape[0]):
                out_ref[slot_ref[o], n] = value[o * channels:(o + 1) * channels] * keep_ref[o]
            return carry

        lax.fori_loop(0, per_out, one, 0, unroll=4)


def stack(own, first, second, lag_t, slots, keep):
    width, lanes, depth = own.shape
    channels = lanes // 2
    chunks, out_chunks = 4, 8
    per_chunk, per_out = width // chunks, channels // out_chunks
    block = lambda s: (jnp.minimum(s, chunks - 1), 0, 0)
    offsets = keep.shape[0]
    return pl.pallas_call(
        functools.partial(stack_kernel, chunks, per_chunk, per_out),
        grid=(chunks + out_chunks,),
        out_shape=jax.ShapeDtypeStruct((offsets, channels, channels, LAGS), jnp.float32),
        in_specs=[
            pl.BlockSpec((per_chunk, lanes, depth), block),
            pl.BlockSpec((per_chunk, depth, lanes), block),
            pl.BlockSpec((per_chunk, depth, lanes), block),
            pl.BlockSpec(lag_t.shape, lambda s: (0, 0)),
            pl.BlockSpec(memory_space=pltpu.SMEM),
            pl.BlockSpec(memory_space=pltpu.SMEM),
        ],
        out_specs=pl.BlockSpec(
            (offsets, per_out, channels, LAGS), lambda s: (0, jnp.maximum(s - chunks, 0), 0, 0)
        ),
        scratch_shapes=[pltpu.VMEM((channels * (2 * width + 1), lanes), jnp.float32)] * 2,
        compiler_params=pltpu.CompilerParams(
            vmem_limit_bytes=VMEM_LIMIT, dimension_semantics=("arbitrary",)
        ),
        name="stack_lags",
    )(own, first, second, lag_t, slots, keep)


def per_device(traces, live, reach):
    windows, channels, samples = traces.shape
    blocks = lax.axis_size("fibre")
    splits = lax.axis_size("freq")
    owned = OFF // splits
    place = lax.axis_index("freq")
    forward_hi, forward_lo, bins_t, lag_t, scale = build_tables(samples)
    forward_hi, forward_lo = jnp.asarray(forward_hi), jnp.asarray(forward_lo)
    alive = live.astype(traces.dtype)[:, None]
    masked = [traces[w] * alive for w in range(windows)]

    quads = blocks // owned
    half = owned // 2
    u = lax.axis_index("fibre") % owned
    core, pair = u % half, u // half

    def rank(q, pair, core, part):
        return (q * owned + pair * half + core) * splits + part

    def send(payload, route):
        pairs = []
        for q in range(quads):
            for p in range(2):
                for c in range(half):
                    for g in range(splits):
                        source = route(q, p, c, g)
                        if source[0] < quads:
                            pairs.append((rank(*source), rank(q, p, c, g)))
        return lax.ppermute(payload, ("fibre", "freq"), pairs)

    def from_neighbours(mine, upper):
        core_payload = jnp.where((core == 1) & (place == 0), mine, upper)
        across_payload = jnp.where((pair == 1) & (place == 0), mine, upper)
        beside = send(core_payload, lambda q, p, c, g: (q + c * g, p, 1 - c, 1 - g if c else g))
        across = send(across_payload, lambda q, p, c, g: (q + p * g, 1 - p, c, g))
        return jnp.where(place == 0, mine, upper), beside, across

    upper = [send(mine, lambda q, p, c, g: (q + 1, p, c, g)) for mine in masked]
    own = prepare(masked, windows, (forward_hi, forward_lo, jnp.asarray(bins_t[1])), True)
    upper[0], own = lax.optimization_barrier((upper[0], own))
    here, beside, across = map(list, zip(*(from_neighbours(mine, up) for mine, up in zip(masked, upper))))
    partner_tables = (forward_hi, forward_lo, jnp.asarray(bins_t[0]))
    across[0], beside[-1] = lax.optimization_barrier((across[0], beside[-1]))
    first = prepare(here + beside, windows, partner_tables, False)
    across[-1], first = lax.optimization_barrier((across[-1], first))
    across_beside = [send(block, lambda q, p, c, g: (q, p, 1 - c, g)) for block in across]
    second = prepare(across + across_beside, windows, partner_tables, False)
    slots = jnp.stack([0, 1 + 2 * core, 2, 3 - 2 * core]).astype(jnp.int32)
    offset_ids = place * owned + slots
    keep = jnp.where(offset_ids < reach[0], jnp.float32(scale), jnp.float32(0.0))
    return stack(own, first, second, jnp.asarray(lag_t), slots, keep)[None]


def solution(mesh):
    placed = (P(None, "fibre", None), P("fibre"), P("fibre"))
    return jax.shard_map(
        per_device,
        mesh=mesh,
        in_specs=placed,
        out_specs=P("fibre", "freq", None, None, None),
        check_vma=False,
    )
```

```python
import functools
import math

import jax
import jax.numpy as jnp
import ml_dtypes
import numpy as np
from jax import lax
from jax.experimental import pallas as pl
from jax.experimental.pallas import tpu as pltpu
from jax.sharding import PartitionSpec as P

BAND = 64
OFF = 8
LAGS = 128
VMEM_LIMIT = 50 * 2**20


def leak_spectrum(freqs, samples, window, shift, slots, period):
    steps = np.arange(window)
    tone = np.exp(2j * np.pi * ((freqs[:, None] * (steps - shift)[None]) % samples) / samples)
    bins = np.exp(-2j * np.pi * ((steps[:, None] * slots[None]) % period) / period)
    return tone @ bins


@functools.lru_cache(maxsize=None)
def build_tables(samples):
    width = LAGS
    residues = samples // width
    groups = residues // 2
    half = width // 2
    per_band = BAND // residues
    order = np.concatenate([np.arange(i, half, per_band) for i in range(per_band)])
    steps = np.arange(width)
    slots = np.arange(width + 1)
    forward = np.zeros((groups, 2 * width, 4 * half))
    to_bins = np.zeros((2, groups, 4 * half, 4, width))
    root = 1.0 / math.sqrt(2.0)
    re_a, im_a, re_b, im_b = (slice(i * half, (i + 1) * half) for i in range(4))
    for g in range(groups):
        freq_a = g + residues * order
        freq_b = (residues - g if g else groups) + residues * order
        wave_a = np.exp(-2j * np.pi * ((steps[:, None] * freq_a[None]) % samples) / samples)
        wave_b = np.exp(-2j * np.pi * ((steps[:, None] * freq_b[None]) % samples) / samples)
        top, low = forward[g, :width], forward[g, width:]
        top[:, re_a], top[:, im_a] = wave_a.real, wave_a.imag
        if g == 0:
            low[:, re_b], low[:, im_b] = wave_b.real, wave_b.imag
        else:
            low[:, re_a], low[:, im_a] = -wave_a.imag, wave_a.real
            top[:, re_b], top[:, im_b] = wave_b.real, wave_b.imag
            low[:, re_b], low[:, im_b] = wave_b.imag, -wave_b.real
        for side in range(2):
            window, shift = ((width, 0), (2 * width, half))[side]
            leak = functools.partial(
                leak_spectrum, samples=samples, window=window, shift=shift, slots=slots, period=2 * width
            )
            pos_a, neg_a, pos_b, neg_b = leak(freq_a), leak(-freq_a), leak(freq_b), leak(-freq_b)
            spec = np.zeros((2, 4 * half, width + 1), complex)
            if g == 0:
                zero = (freq_a == 0)[:, None]
                spec[0, re_a] = np.where(zero, pos_a, root * (pos_a + neg_a))
                spec[0, im_a] = np.where(zero, 0.0, root * 1j * (pos_a - neg_a))
                spec[1, re_b] = root * (pos_b + neg_b)
                spec[1, im_b] = root * 1j * (pos_b - neg_b)
            else:
                spec[0, re_a], spec[0, im_a] = root * pos_a, root * 1j * pos_a
                spec[0, re_b], spec[0, im_b] = root * neg_b, -root * 1j * neg_b
                spec[1, re_b], spec[1, im_b] = root * pos_b, root * 1j * pos_b
                spec[1, re_a], spec[1, im_a] = root * neg_a, -root * 1j * neg_a
            table = to_bins[side, g]
            table[:, 0], table[:, 1] = spec[0, :, :width].real, spec[0, :, :width].imag
            table[:, 2], table[:, 3] = spec[1, :, :width].real, spec[1, :, :width].imag
            if g == 0:
                ends = (spec[0, :, 0].real, spec[1, :, 0].real, spec[0, :, width].real, spec[1, :, width].real)
            else:
                ends = tuple(
                    math.sqrt(2.0) * v
                    for v in (spec[0, :, 0].real, spec[0, :, 0].imag, spec[0, :, width].real, spec[0, :, width].imag)
                )
            for q in range(4):
                table[:, q, 0] = ends[q]
    lags = np.arange(LAGS)
    phase = 2 * np.pi * ((steps[:, None] * lags[None]) % (2 * width)) / (2 * width)
    lag = np.stack([2 * np.cos(phase), -2 * np.sin(phase)])
    lag[0, 0], lag[1, 0] = 1.0, (-1.0) ** lags
    bf16 = ml_dtypes.bfloat16
    forward_t = forward.transpose(0, 2, 1)
    forward_hi = forward_t.astype(bf16)
    forward_lo = (forward_t - forward_hi.astype(np.float64)).astype(bf16)
    bins_t = to_bins.transpose(0, 1, 3, 4, 2).reshape(2, groups, 4 * width, 4 * half).astype(bf16)
    lag_t = lag.reshape(2 * width, LAGS).T.astype(bf16)
    scale = residues / (2.0 * width * samples) / math.sqrt(samples)
    return forward_hi, forward_lo, bins_t, lag_t, scale


def real_dft(values):
    n = len(values)
    if n == 2:
        return [(values[0] + values[1], None), (values[0] - values[1], None)]
    even, odd = real_dft(values[0::2]), real_dft(values[1::2])
    out = [None] * (n // 2 + 1)
    for k in range(n // 4 + 1):
        (er, ei), (pr, pi) = even[k], odd[k]
        angle = -2.0 * math.pi * k / n
        c, s = math.cos(angle), math.sin(angle)
        if k == 0:
            out[0] = (er + pr, None)
            out[n // 2] = (er - pr, None)
            continue
        if 4 * k == n:
            out[k] = (er, -pr)
            continue
        if pi is None:
            tr, ti = pr * c, pr * s
        elif 8 * k == n:
            tr, ti = (pr + pi) * c, (pi - pr) * c
        else:
            tr, ti = pr * c - pi * s, pr * s + pi * c
        if ei is None:
            out[k] = (er + tr, ti)
            out[n // 2 - k] = (er - tr, ti)
        else:
            out[k] = (er + tr, ei + ti)
            out[n // 2 - k] = (er - tr, ti - ei)
    return out


def whiten_into_bins(own, windows, records, copies, fhi, flo, bins, yhi, ylo, spec, wide):
    channels, samples = records[0].shape
    width = LAGS
    residues = samples // width
    groups = residues // 2
    rows = 2 * windows * channels
    lanes = 2 * channels
    stride = windows * groups * 4 + 1
    step = 16

    def split(value):
        high = value.astype(jnp.bfloat16)
        return high, (value - high.astype(jnp.float32)).astype(jnp.bfloat16)

    def transform(n, carry):
        for index, ref in enumerate(records):
            which, w = divmod(index, windows)
            block = ref[pl.ds(pl.multiple_of(n * step, step), step), :].astype(jnp.float32)
            terms = real_dft([block[:, a * width:(a + 1) * width] for a in range(residues)])
            for g in range(groups):
                parts = terms[g] if g else (terms[0][0], terms[groups][0])
                for side, part in enumerate(parts):
                    hi, lo = split(part)
                    for copy_to in ((0, 1) if own else (which,)):
                        row = pl.multiple_of(w * lanes + copy_to * channels + n * step, step)
                        yhi[g, pl.ds(row, step), side * width:(side + 1) * width] = hi
                        ylo[g, pl.ds(row, step), side * width:(side + 1) * width] = lo
        return carry

    lax.fori_loop(0, channels // step, transform, 0)
    copies[0].wait()
    copies[1].wait()
    nt = (((1,), (1,)), ((), ()))
    bands = (samples // 2) // BAND

    def forward(g, power):
        value = lax.dot_general(fhi[g], yhi[g], nt, preferred_element_type=jnp.float32)
        value += lax.dot_general(flo[g], yhi[g], nt, preferred_element_type=jnp.float32)
        value += lax.dot_general(fhi[g], ylo[g], nt, preferred_element_type=jnp.float32)
        spec[g] = value
        squared = (value * value).reshape(2 * width // bands, bands, rows)
        return power + squared.sum(0)

    power = lax.fori_loop(0, groups, forward, jnp.zeros((bands, rows), jnp.float32), unroll=4)
    gain = 1.0 / jnp.sqrt(power * (1.0 / BAND) + 1e-6)
    copies[2].wait()

    def to_bins(g, carry):
        white = (spec[g].reshape(2 * width // bands, bands, rows) * gain[None]).reshape(2 * width, rows)
        value = jnp.dot(bins[g], white.astype(jnp.bfloat16), preferred_element_type=jnp.float32)
        parts = [value[q * width:(q + 1) * width] for q in range(4)]
        if own:
            left = lax.broadcasted_iota(jnp.int32, (width, rows), 1) % lanes < channels
            ends = lax.broadcasted_iota(jnp.int32, (width, rows), 0) == 0
            turned = [parts[1], -parts[0], parts[3], -parts[2]]
            zero = jnp.zeros_like(parts[0])
            real = [parts[q] if q < 2 else jnp.where(ends, zero, parts[q]) for q in range(4)]
            imag = [jnp.where(ends, zero if q < 2 else parts[q], turned[q]) for q in range(4)]
            parts = [jnp.where(left, real[q], imag[q]) for q in range(4)]
        for q in range(4):
            for w in range(windows):
                start = w * (groups * 4) + g * 4 + q
                wide[pl.ds(start, width, stride=stride), :] = parts[q][:, w * lanes:(w + 1) * lanes]
        return carry

    lax.fori_loop(0, groups, to_bins, 0, unroll=4)


def start_tables(sources, targets, sems):
    copies = [
        pltpu.make_async_copy(source, target, sems.at[i])
        for i, (source, target) in enumerate(zip(sources, targets))
    ]
    for copy in copies:
        copy.start()
    return copies


def cross_bins(own_ref, wide, cross):
    width, lanes, depth = own_ref.shape
    channels = lanes // 2

    def one(k, carry):
        partners = wide[pl.ds(k * (depth + 1), depth), :].astype(jnp.bfloat16)
        value = jnp.dot(own_ref[k], partners, preferred_element_type=jnp.float32)
        for part in range(2):
            cross[pl.ds(part * width + k, channels, stride=2 * width + 1), :] = (
                value[part * channels:(part + 1) * channels]
            )
        return carry

    lax.fori_loop(0, width, one, 0, unroll=8)


def own_kernel(windows, *refs):
    records, (fhi_hbm, flo_hbm, bins_hbm, out_ref, *scratch) = refs[:windows], refs[windows:]
    *scratch, sems = scratch
    copies = start_tables((fhi_hbm, flo_hbm, bins_hbm), scratch[:3], sems)
    whiten_into_bins(True, windows, records, copies, *scratch)
    wide = scratch[-1]
    width, lanes, depth = out_ref.shape

    def narrow(k, carry):
        out_ref[k] = wide[pl.ds(k * (depth + 1), depth), :].T.astype(jnp.bfloat16)
        return carry

    lax.fori_loop(0, width, narrow, 0, unroll=8)


def first_kernel(windows, *refs):
    records, (*sources, out_ref), scratch = refs[:2 * windows], refs[2 * windows:2 * windows + 5], refs[2 * windows + 5:]
    fhi, flo, bins, own_ref, *work, cross, sems = scratch
    copies = start_tables(sources, scratch[:4], sems)
    whiten_into_bins(False, windows, records, copies, fhi, flo, bins, *work)
    copies[3].wait()
    cross_bins(own_ref, work[-1], cross)
    rows = 2 * own_ref.shape[0]

    def narrow(i, carry):
        out_ref[pl.ds(pl.multiple_of(i * rows, rows), rows), :] = (
            cross[pl.ds(i * (rows + 1), rows), :].astype(jnp.bfloat16)
        )
        return carry

    lax.fori_loop(0, out_ref.shape[0] // rows, narrow, 0, unroll=4)


def last_kernel(windows, *refs):
    records, refs = refs[:2 * windows], refs[2 * windows:]
    sources, (lag_ref, slot_ref, keep_ref, out_hbm), scratch = refs[:5], refs[5:9], refs[9:]
    fhi, flo, bins, own_ref, early_ref, *work, cross, stage, sems, out_sems = scratch
    copies = start_tables(sources, scratch[:5], sems)
    whiten_into_bins(False, windows, records, copies, fhi, flo, bins, *work)
    copies[3].wait()
    copies[4].wait()
    cross_bins(own_ref, work[-1], cross)
    rows = 2 * own_ref.shape[0]
    _, offsets, per_out, channels, _ = stage.shape
    chunks = channels // per_out

    def leave(chunk, slot):
        target = out_hbm.at[:, pl.ds(chunk * per_out, per_out)]
        return pltpu.make_async_copy(stage.at[slot], target, out_sems.at[slot])

    def two_chunks(t, carry):
        for slot in range(2):
            chunk = t * 2 + slot

            @pl.when(t > 0)
            def _():
                leave(chunk - 2, slot).wait()

            def one(n, inner):
                i = chunk * per_out + n
                early = early_ref[pl.ds(pl.multiple_of(i * rows, rows), rows), :]
                late = cross[pl.ds(i * (rows + 1), rows), :].astype(jnp.bfloat16)
                both = jnp.concatenate([early, late], axis=1)
                value = jnp.dot(lag_ref[...], both, preferred_element_type=jnp.float32).T
                for o in range(offsets):
                    stage[slot, slot_ref[o], n] = value[o * channels:(o + 1) * channels] * keep_ref[o]
                return inner

            lax.fori_loop(0, per_out, one, 0, unroll=4)
            leave(chunk, slot).start()
        return carry

    lax.fori_loop(0, chunks // 2, two_chunks, 0)
    for slot in range(2):
        leave(chunks - 2 + slot, slot).wait()


def call(kernel, name, windows, operands, tables, extra, out_shape, out_space, buffers=(), signals=()):
    channels, samples = operands[0].shape
    width = LAGS
    groups = samples // width // 2
    rows = 2 * windows * channels
    depth = windows * groups * 4
    lanes = 2 * channels
    any_spec = pl.BlockSpec(memory_space=pl.ANY)
    vmem_spec = pl.BlockSpec(memory_space=pltpu.VMEM)
    smem_spec = pl.BlockSpec(memory_space=pltpu.SMEM)
    small = [vmem_spec if v.ndim > 1 else smem_spec for v in extra]
    return pl.pallas_call(
        functools.partial(kernel, windows),
        out_shape=out_shape,
        in_specs=[vmem_spec] * len(operands) + [any_spec] * len(tables) + small,
        out_specs=pl.BlockSpec(memory_space=out_space),
        scratch_shapes=[pltpu.VMEM(t.shape, jnp.bfloat16) for t in tables] + [
            pltpu.VMEM((groups, rows, 2 * width), jnp.bfloat16),
            pltpu.VMEM((groups, rows, 2 * width), jnp.bfloat16),
            pltpu.VMEM((groups, 2 * width, rows), jnp.float32),
            pltpu.VMEM((width * (depth + 1), lanes), jnp.float32),
            *buffers,
            pltpu.SemaphoreType.DMA((len(tables),)),
            *signals,
        ],
        compiler_params=pltpu.CompilerParams(vmem_limit_bytes=VMEM_LIMIT),
        cost_estimate=pl.CostEstimate(
            flops=20 * groups * rows * 4 * width * width, bytes_accessed=14 * 2**20, transcendentals=0
        ),
        name=name,
    )(*operands, *tables, *extra)


def per_device(traces, live, reach):
    windows, channels, samples = traces.shape
    blocks = lax.axis_size("fibre")
    splits = lax.axis_size("freq")
    owned = OFF // splits
    place = lax.axis_index("freq")
    forward_hi, forward_lo, bins_t, lag_t, scale = build_tables(samples)
    forward_hi, forward_lo = jnp.asarray(forward_hi), jnp.asarray(forward_lo)
    alive = live.astype(traces.dtype)[:, None]
    masked = [traces[w] * alive for w in range(windows)]

    quads = blocks // owned
    half = owned // 2
    u = lax.axis_index("fibre") % owned
    core, pair = u % half, u // half

    def rank(q, pair, core, part):
        return (q * owned + pair * half + core) * splits + part

    def send(payload, route):
        pairs = []
        for q in range(quads):
            for p in range(2):
                for c in range(half):
                    for g in range(splits):
                        source = route(q, p, c, g)
                        if source[0] < quads:
                            pairs.append((rank(*source), rank(q, p, c, g)))
        return lax.ppermute(payload, ("fibre", "freq"), pairs)

    def from_neighbours(mine, upper):
        core_payload = jnp.where((core == 1) & (place == 0), mine, upper)
        across_payload = jnp.where((pair == 1) & (place == 0), mine, upper)
        beside = send(core_payload, lambda q, p, c, g: (q + c * g, p, 1 - c, 1 - g if c else g))
        across = send(across_payload, lambda q, p, c, g: (q + p * g, 1 - p, c, g))
        return jnp.where(place == 0, mine, upper), beside, across

    width = LAGS
    lanes = 2 * channels
    depth = windows * samples // width * 2
    crossed = pltpu.VMEM((channels * (2 * width + 1), lanes), jnp.float32)
    own_tables = (forward_hi, forward_lo, jnp.asarray(bins_t[1]))
    tables = (forward_hi, forward_lo, jnp.asarray(bins_t[0]))

    upper = [send(mine, lambda q, p, c, g: (q + 1, p, c, g)) for mine in masked]
    own = call(
        own_kernel, "own_bins", windows, masked, own_tables, (),
        jax.ShapeDtypeStruct((width, lanes, depth), jnp.bfloat16), pltpu.VMEM,
    )
    upper[0], own = lax.optimization_barrier((upper[0], own))
    here, beside, across = [], [], []
    for w in range(windows):
        if w:
            upper[w], beside[w - 1], across[w - 1] = lax.optimization_barrier(
                (upper[w], beside[w - 1], across[w - 1])
            )
        for known, new in zip((here, beside, across), from_neighbours(masked[w], upper[w])):
            known.append(new)
    early = call(
        first_kernel, "first_pair", windows, here + beside, (*tables, own), (),
        jax.ShapeDtypeStruct((channels * 2 * width, lanes), jnp.bfloat16), pltpu.VMEM, (crossed,),
    )
    *across, early = lax.optimization_barrier((*across, early))
    across_beside = [send(block, lambda q, p, c, g: (q, p, 1 - c, g)) for block in across]
    slots = jnp.stack([0, 1 + 2 * core, 2, 3 - 2 * core]).astype(jnp.int32)
    offset_ids = place * owned + slots
    keep = jnp.where(offset_ids < reach[0], jnp.float32(scale), jnp.float32(0.0))
    result = call(
        last_kernel, "second_pair", windows, across + across_beside, (*tables, own, early),
        (jnp.asarray(lag_t), slots, keep),
        jax.ShapeDtypeStruct((owned, channels, channels, LAGS), jnp.float32), pl.ANY,
        (crossed, pltpu.VMEM((2, owned, channels // 8, channels, LAGS), jnp.float32)), (pltpu.SemaphoreType.DMA((2,)),),
    )
    return result[None]


def solution(mesh):
    placed = (P(None, "fibre", None), P("fibre"), P("fibre"))
    return jax.shard_map(
        per_device,
        mesh=mesh,
        in_specs=placed,
        out_specs=P("fibre", "freq", None, None, None),
        check_vma=False,
    )
```

```python
import functools
import math

import jax
import jax.numpy as jnp
import ml_dtypes
import numpy as np
from jax import lax
from jax.experimental import pallas as pl
from jax.experimental.pallas import tpu as pltpu
from jax.sharding import PartitionSpec as P

BAND = 64
OFF = 8
LAGS = 128
VMEM_LIMIT = 50 * 2**20


def leak_spectrum(freqs, samples, window, shift, slots, period):
    steps = np.arange(window)
    tone = np.exp(2j * np.pi * ((freqs[:, None] * (steps - shift)[None]) % samples) / samples)
    bins = np.exp(-2j * np.pi * ((steps[:, None] * slots[None]) % period) / period)
    return tone @ bins


@functools.lru_cache(maxsize=None)
def build_tables(samples):
    width = LAGS
    residues = samples // width
    groups = residues // 2
    half = width // 2
    per_band = BAND // residues
    order = np.concatenate([np.arange(i, half, per_band) for i in range(per_band)])
    steps = np.arange(width)
    slots = np.arange(width + 1)
    forward = np.zeros((groups, 2 * width, 4 * half))
    to_bins = np.zeros((2, groups, 4 * half, 4, width))
    root = 1.0 / math.sqrt(2.0)
    re_a, im_a, re_b, im_b = (slice(i * half, (i + 1) * half) for i in range(4))
    for g in range(groups):
        freq_a = g + residues * order
        freq_b = (residues - g if g else groups) + residues * order
        wave_a = np.exp(-2j * np.pi * ((steps[:, None] * freq_a[None]) % samples) / samples)
        wave_b = np.exp(-2j * np.pi * ((steps[:, None] * freq_b[None]) % samples) / samples)
        top, low = forward[g, :width], forward[g, width:]
        top[:, re_a], top[:, im_a] = wave_a.real, wave_a.imag
        if g == 0:
            low[:, re_b], low[:, im_b] = wave_b.real, wave_b.imag
        else:
            low[:, re_a], low[:, im_a] = -wave_a.imag, wave_a.real
            top[:, re_b], top[:, im_b] = wave_b.real, wave_b.imag
            low[:, re_b], low[:, im_b] = wave_b.imag, -wave_b.real
        for side in range(2):
            window, shift = ((width, 0), (2 * width, half))[side]
            leak = functools.partial(
                leak_spectrum, samples=samples, window=window, shift=shift, slots=slots, period=2 * width
            )
            pos_a, neg_a, pos_b, neg_b = leak(freq_a), leak(-freq_a), leak(freq_b), leak(-freq_b)
            spec = np.zeros((2, 4 * half, width + 1), complex)
            if g == 0:
                zero = (freq_a == 0)[:, None]
                spec[0, re_a] = np.where(zero, pos_a, root * (pos_a + neg_a))
                spec[0, im_a] = np.where(zero, 0.0, root * 1j * (pos_a - neg_a))
                spec[1, re_b] = root * (pos_b + neg_b)
                spec[1, im_b] = root * 1j * (pos_b - neg_b)
            else:
                spec[0, re_a], spec[0, im_a] = root * pos_a, root * 1j * pos_a
                spec[0, re_b], spec[0, im_b] = root * neg_b, -root * 1j * neg_b
                spec[1, re_b], spec[1, im_b] = root * pos_b, root * 1j * pos_b
                spec[1, re_a], spec[1, im_a] = root * neg_a, -root * 1j * neg_a
            table = to_bins[side, g]
            table[:, 0], table[:, 1] = spec[0, :, :width].real, spec[0, :, :width].imag
            table[:, 2], table[:, 3] = spec[1, :, :width].real, spec[1, :, :width].imag
            if g == 0:
                ends = (spec[0, :, 0].real, spec[1, :, 0].real, spec[0, :, width].real, spec[1, :, width].real)
            else:
                ends = tuple(
                    math.sqrt(2.0) * v
                    for v in (spec[0, :, 0].real, spec[0, :, 0].imag, spec[0, :, width].real, spec[0, :, width].imag)
                )
            for q in range(4):
                table[:, q, 0] = ends[q]
    lags = np.arange(LAGS)
    phase = 2 * np.pi * ((steps[:, None] * lags[None]) % (2 * width)) / (2 * width)
    lag = np.stack([2 * np.cos(phase), -2 * np.sin(phase)])
    lag[0, 0], lag[1, 0] = 1.0, (-1.0) ** lags
    bf16 = ml_dtypes.bfloat16
    forward_t = forward.transpose(0, 2, 1)
    forward_hi = forward_t.astype(bf16)
    forward_lo = (forward_t - forward_hi.astype(np.float64)).astype(bf16)
    bins_t = to_bins.transpose(0, 1, 3, 4, 2).reshape(2, groups, 4 * width, 4 * half).astype(bf16)
    lag_t = lag.reshape(2 * width, LAGS).T.astype(bf16)
    scale = residues / (2.0 * width * samples) / math.sqrt(samples)
    return forward_hi, forward_lo, bins_t, lag_t, scale


def real_dft(values):
    n = len(values)
    if n == 2:
        return [(values[0] + values[1], None), (values[0] - values[1], None)]
    even, odd = real_dft(values[0::2]), real_dft(values[1::2])
    out = [None] * (n // 2 + 1)
    for k in range(n // 4 + 1):
        (er, ei), (pr, pi) = even[k], odd[k]
        angle = -2.0 * math.pi * k / n
        c, s = math.cos(angle), math.sin(angle)
        if k == 0:
            out[0] = (er + pr, None)
            out[n // 2] = (er - pr, None)
            continue
        if 4 * k == n:
            out[k] = (er, -pr)
            continue
        if pi is None:
            tr, ti = pr * c, pr * s
        elif 8 * k == n:
            tr, ti = (pr + pi) * c, (pi - pr) * c
        else:
            tr, ti = pr * c - pi * s, pr * s + pi * c
        if ei is None:
            out[k] = (er + tr, ti)
            out[n // 2 - k] = (er - tr, ti)
        else:
            out[k] = (er + tr, ei + ti)
            out[n // 2 - k] = (er - tr, ti - ei)
    return out


def whiten_into_bins(own, windows, records, copies, fhi, flo, bins, yhi, ylo, spec, wide):
    channels, samples = records[0].shape
    width = LAGS
    residues = samples // width
    groups = residues // 2
    rows = 2 * windows * channels
    lanes = 2 * channels
    stride = windows * groups * 4 + 1
    step = 16

    def split(value):
        high = value.astype(jnp.bfloat16)
        return high, (value - high.astype(jnp.float32)).astype(jnp.bfloat16)

    def transform(n, carry):
        for index, ref in enumerate(records):
            which, w = divmod(index, windows)
            block = ref[pl.ds(pl.multiple_of(n * step, step), step), :].astype(jnp.float32)
            terms = real_dft([block[:, a * width:(a + 1) * width] for a in range(residues)])
            for g in range(groups):
                parts = terms[g] if g else (terms[0][0], terms[groups][0])
                for side, part in enumerate(parts):
                    hi, lo = split(part)
                    for copy_to in ((0, 1) if own else (which,)):
                        row = pl.multiple_of(w * lanes + copy_to * channels + n * step, step)
                        yhi[g, pl.ds(row, step), side * width:(side + 1) * width] = hi
                        ylo[g, pl.ds(row, step), side * width:(side + 1) * width] = lo
        return carry

    lax.fori_loop(0, channels // step, transform, 0)
    copies[0].wait()
    copies[1].wait()
    nt = (((1,), (1,)), ((), ()))
    bands = (samples // 2) // BAND

    def forward(g, power):
        value = lax.dot_general(fhi[g], yhi[g], nt, preferred_element_type=jnp.float32)
        value += lax.dot_general(flo[g], yhi[g], nt, preferred_element_type=jnp.float32)
        value += lax.dot_general(fhi[g], ylo[g], nt, preferred_element_type=jnp.float32)
        spec[g] = value
        squared = (value * value).reshape(2 * width // bands, bands, rows)
        return power + squared.sum(0)

    power = lax.fori_loop(0, groups, forward, jnp.zeros((bands, rows), jnp.float32), unroll=8)
    gain = 1.0 / jnp.sqrt(power * (1.0 / BAND) + 1e-6)
    copies[2].wait()

    def to_bins(g, carry):
        white = (spec[g].reshape(2 * width // bands, bands, rows) * gain[None]).reshape(2 * width, rows)
        value = jnp.dot(bins[g], white.astype(jnp.bfloat16), preferred_element_type=jnp.float32)
        parts = [value[q * width:(q + 1) * width] for q in range(4)]
        if own:
            left = lax.broadcasted_iota(jnp.int32, (width, rows), 1) % lanes < channels
            ends = lax.broadcasted_iota(jnp.int32, (width, rows), 0) == 0
            turned = [parts[1], -parts[0], parts[3], -parts[2]]
            zero = jnp.zeros_like(parts[0])
            real = [parts[q] if q < 2 else jnp.where(ends, zero, parts[q]) for q in range(4)]
            imag = [jnp.where(ends, zero if q < 2 else parts[q], turned[q]) for q in range(4)]
            parts = [jnp.where(left, real[q], imag[q]) for q in range(4)]
        for q in range(4):
            for w in range(windows):
                start = w * (groups * 4) + g * 4 + q
                wide[pl.ds(start, width, stride=stride), :] = parts[q][:, w * lanes:(w + 1) * lanes]
        return carry

    lax.fori_loop(0, groups, to_bins, 0, unroll=8)


def start_tables(sources, targets, sems):
    copies = [
        pltpu.make_async_copy(source, target, sems.at[i])
        for i, (source, target) in enumerate(zip(sources, targets))
    ]
    for copy in copies:
        copy.start()
    return copies


def cross_bins(own_ref, wide, cross):
    width, lanes, depth = own_ref.shape
    channels = lanes // 2

    def one(k, carry):
        partners = wide[pl.ds(k * (depth + 1), depth), :].astype(jnp.bfloat16)
        value = jnp.dot(own_ref[k], partners, preferred_element_type=jnp.float32)
        for part in range(2):
            cross[pl.ds(part * width + k, channels, stride=2 * width + 1), :] = (
                value[part * channels:(part + 1) * channels]
            )
        return carry

    lax.fori_loop(0, width, one, 0, unroll=16)


def own_kernel(windows, *refs):
    records, (fhi_hbm, flo_hbm, bins_hbm, out_ref, *scratch) = refs[:windows], refs[windows:]
    *scratch, sems = scratch
    copies = start_tables((fhi_hbm, flo_hbm, bins_hbm), scratch[:3], sems)
    whiten_into_bins(True, windows, records, copies, *scratch)
    wide = scratch[-1]
    width, lanes, depth = out_ref.shape

    def narrow(k, carry):
        out_ref[k] = wide[pl.ds(k * (depth + 1), depth), :].T.astype(jnp.bfloat16)
        return carry

    lax.fori_loop(0, width, narrow, 0, unroll=8)


def first_kernel(windows, *refs):
    records, (*sources, out_ref), scratch = refs[:2 * windows], refs[2 * windows:2 * windows + 5], refs[2 * windows + 5:]
    fhi, flo, bins, own_ref, *work, cross, sems = scratch
    copies = start_tables(sources, scratch[:4], sems)
    whiten_into_bins(False, windows, records, copies, fhi, flo, bins, *work)
    copies[3].wait()
    cross_bins(own_ref, work[-1], cross)
    rows = 2 * own_ref.shape[0]

    def narrow(i, carry):
        out_ref[pl.ds(pl.multiple_of(i * rows, rows), rows), :] = (
            cross[pl.ds(i * (rows + 1), rows), :].astype(jnp.bfloat16)
        )
        return carry

    lax.fori_loop(0, out_ref.shape[0] // rows, narrow, 0, unroll=4)


def last_kernel(windows, *refs):
    records, refs = refs[:2 * windows], refs[2 * windows:]
    sources, (lag_ref, slot_ref, keep_ref, out_hbm), scratch = refs[:5], refs[5:9], refs[9:]
    fhi, flo, bins, own_ref, early_ref, *work, cross, stage, sems, out_sems = scratch
    copies = start_tables(sources, scratch[:5], sems)
    whiten_into_bins(False, windows, records, copies, fhi, flo, bins, *work)
    copies[3].wait()
    copies[4].wait()
    cross_bins(own_ref, work[-1], cross)
    rows = 2 * own_ref.shape[0]
    _, offsets, per_out, channels, _ = stage.shape
    chunks = channels // per_out

    def leave(chunk, slot):
        target = out_hbm.at[:, pl.ds(chunk * per_out, per_out)]
        return pltpu.make_async_copy(stage.at[slot], target, out_sems.at[slot])

    def two_chunks(t, carry):
        for slot in range(2):
            chunk = t * 2 + slot

            @pl.when(t > 0)
            def _():
                leave(chunk - 2, slot).wait()

            def one(n, inner):
                i = chunk * per_out + n
                early = early_ref[pl.ds(pl.multiple_of(i * rows, rows), rows), :]
                late = cross[pl.ds(i * (rows + 1), rows), :].astype(jnp.bfloat16)
                both = jnp.concatenate([early, late], axis=1)
                value = jnp.dot(lag_ref[...], both, preferred_element_type=jnp.float32).T
                for o in range(offsets):
                    stage[slot, slot_ref[o], n] = value[o * channels:(o + 1) * channels] * keep_ref[o]
                return inner

            lax.fori_loop(0, per_out, one, 0, unroll=8)
            leave(chunk, slot).start()
        return carry

    lax.fori_loop(0, chunks // 2, two_chunks, 0)
    for slot in range(2):
        leave(chunks - 2 + slot, slot).wait()


def call(kernel, name, windows, operands, tables, extra, out_shape, out_space, buffers=(), signals=()):
    channels, samples = operands[0].shape
    width = LAGS
    groups = samples // width // 2
    rows = 2 * windows * channels
    depth = windows * groups * 4
    lanes = 2 * channels
    any_spec = pl.BlockSpec(memory_space=pl.ANY)
    vmem_spec = pl.BlockSpec(memory_space=pltpu.VMEM)
    smem_spec = pl.BlockSpec(memory_space=pltpu.SMEM)
    small = [vmem_spec if v.ndim > 1 else smem_spec for v in extra]
    return pl.pallas_call(
        functools.partial(kernel, windows),
        out_shape=out_shape,
        in_specs=[vmem_spec] * len(operands) + [any_spec] * len(tables) + small,
        out_specs=pl.BlockSpec(memory_space=out_space),
        scratch_shapes=[pltpu.VMEM(t.shape, jnp.bfloat16) for t in tables] + [
            pltpu.VMEM((groups, rows, 2 * width), jnp.bfloat16),
            pltpu.VMEM((groups, rows, 2 * width), jnp.bfloat16),
            pltpu.VMEM((groups, 2 * width, rows), jnp.float32),
            pltpu.VMEM((width * (depth + 1), lanes), jnp.float32),
            *buffers,
            pltpu.SemaphoreType.DMA((len(tables),)),
            *signals,
        ],
        compiler_params=pltpu.CompilerParams(vmem_limit_bytes=VMEM_LIMIT),
        cost_estimate=pl.CostEstimate(
            flops=20 * groups * rows * 4 * width * width, bytes_accessed=14 * 2**20, transcendentals=0
        ),
        name=name,
    )(*operands, *tables, *extra)


def per_device(traces, live, reach):
    windows, channels, samples = traces.shape
    blocks = lax.axis_size("fibre")
    splits = lax.axis_size("freq")
    owned = OFF // splits
    place = lax.axis_index("freq")
    forward_hi, forward_lo, bins_t, lag_t, scale = build_tables(samples)
    forward_hi, forward_lo = jnp.asarray(forward_hi), jnp.asarray(forward_lo)
    masked = [jnp.where(live[:, None] > 0, traces[w], jnp.zeros((), traces.dtype)) for w in range(windows)]

    quads = blocks // owned
    half = owned // 2
    u = lax.axis_index("fibre") % owned
    core, pair = u % half, u // half

    def rank(q, pair, core, part):
        return (q * owned + pair * half + core) * splits + part

    def send(payload, route):
        pairs = []
        for q in range(quads):
            for p in range(2):
                for c in range(half):
                    for g in range(splits):
                        source = route(q, p, c, g)
                        if source[0] < quads:
                            pairs.append((rank(*source), rank(q, p, c, g)))
        return lax.ppermute(payload, ("fibre", "freq"), pairs)

    def from_neighbours(mine, upper):
        core_payload = jnp.where((core == 1) & (place == 0), mine, upper)
        across_payload = jnp.where((pair == 1) & (place == 0), mine, upper)
        beside = send(core_payload, lambda q, p, c, g: (q + c * g, p, 1 - c, 1 - g if c else g))
        across = send(across_payload, lambda q, p, c, g: (q + p * g, 1 - p, c, g))
        return jnp.where(place == 0, mine, upper), beside, across

    width = LAGS
    lanes = 2 * channels
    depth = windows * samples // width * 2
    crossed = pltpu.VMEM((channels * (2 * width + 1), lanes), jnp.float32)
    own_tables = (forward_hi, forward_lo, jnp.asarray(bins_t[1]))
    tables = (forward_hi, forward_lo, jnp.asarray(bins_t[0]))

    upper = [send(mine, lambda q, p, c, g: (q + 1, p, c, g)) for mine in masked]
    own = call(
        own_kernel, "own_bins", windows, masked, own_tables, (),
        jax.ShapeDtypeStruct((width, lanes, depth), jnp.bfloat16), pltpu.VMEM,
    )
    upper[0], own = lax.optimization_barrier((upper[0], own))
    here, beside, across = [], [], []
    for w in range(windows):
        if w:
            upper[w], beside[w - 1] = lax.optimization_barrier((upper[w], beside[w - 1]))
        for known, new in zip((here, beside, across), from_neighbours(masked[w], upper[w])):
            known.append(new)
    across[0], beside[-1] = lax.optimization_barrier((across[0], beside[-1]))
    early = call(
        first_kernel, "first_pair", windows, here + beside, (*tables, own), (),
        jax.ShapeDtypeStruct((channels * 2 * width, lanes), jnp.bfloat16), pltpu.VMEM, (crossed,),
    )
    *across, early = lax.optimization_barrier((*across, early))
    across_beside = [send(block, lambda q, p, c, g: (q, p, 1 - c, g)) for block in across]
    slots = jnp.stack([0, 1 + 2 * core, 2, 3 - 2 * core]).astype(jnp.int32)
    offset_ids = place * owned + slots
    keep = jnp.where(offset_ids < reach[0], jnp.float32(scale), jnp.float32(0.0))
    result = call(
        last_kernel, "second_pair", windows, across + across_beside, (*tables, own, early),
        (jnp.asarray(lag_t), slots, keep),
        jax.ShapeDtypeStruct((owned, channels, channels, LAGS), jnp.float32), pl.ANY,
        (crossed, pltpu.VMEM((2, owned, channels // 8, channels, LAGS), jnp.float32)), (pltpu.SemaphoreType.DMA((2,)),),
    )
    return result[None]


def solution(mesh):
    placed = (P(None, "fibre", None), P("fibre"), P("fibre"))
    return jax.shard_map(
        per_device,
        mesh=mesh,
        in_specs=placed,
        out_specs=P("fibre", "freq", None, None, None),
        check_vma=False,
    )
```

```python
import functools
import math

import jax
import jax.numpy as jnp
import ml_dtypes
import numpy as np
from jax import lax
from jax.experimental import pallas as pl
from jax.experimental.pallas import tpu as pltpu
from jax.sharding import PartitionSpec as P

BAND = 64
OFF = 8
LAGS = 128
VMEM_LIMIT = 50 * 2**20


def leak_spectrum(freqs, samples, window, shift, slots, period):
    steps = np.arange(window)
    tone = np.exp(2j * np.pi * ((freqs[:, None] * (steps - shift)[None]) % samples) / samples)
    bins = np.exp(-2j * np.pi * ((steps[:, None] * slots[None]) % period) / period)
    return tone @ bins


@functools.lru_cache(maxsize=None)
def build_tables(samples):
    width = LAGS
    residues = samples // width
    groups = residues // 2
    half = width // 2
    per_band = BAND // residues
    order = np.concatenate([np.arange(i, half, per_band) for i in range(per_band)])
    steps = np.arange(width)
    slots = np.arange(width + 1)
    forward = np.zeros((groups, 2 * width, 4 * half))
    to_bins = np.zeros((2, groups, 4 * half, 4, width))
    root = 1.0 / math.sqrt(2.0)
    re_a, im_a, re_b, im_b = (slice(i * half, (i + 1) * half) for i in range(4))
    for g in range(groups):
        freq_a = g + residues * order
        freq_b = (residues - g if g else groups) + residues * order
        wave_a = np.exp(-2j * np.pi * ((steps[:, None] * freq_a[None]) % samples) / samples)
        wave_b = np.exp(-2j * np.pi * ((steps[:, None] * freq_b[None]) % samples) / samples)
        top, low = forward[g, :width], forward[g, width:]
        top[:, re_a], top[:, im_a] = wave_a.real, wave_a.imag
        if g == 0:
            low[:, re_b], low[:, im_b] = wave_b.real, wave_b.imag
        else:
            low[:, re_a], low[:, im_a] = -wave_a.imag, wave_a.real
            top[:, re_b], top[:, im_b] = wave_b.real, wave_b.imag
            low[:, re_b], low[:, im_b] = wave_b.imag, -wave_b.real
        for side in range(2):
            window, shift = ((width, 0), (2 * width, half))[side]
            leak = functools.partial(
                leak_spectrum, samples=samples, window=window, shift=shift, slots=slots, period=2 * width
            )
            pos_a, neg_a, pos_b, neg_b = leak(freq_a), leak(-freq_a), leak(freq_b), leak(-freq_b)
            spec = np.zeros((2, 4 * half, width + 1), complex)
            if g == 0:
                zero = (freq_a == 0)[:, None]
                spec[0, re_a] = np.where(zero, pos_a, root * (pos_a + neg_a))
                spec[0, im_a] = np.where(zero, 0.0, root * 1j * (pos_a - neg_a))
                spec[1, re_b] = root * (pos_b + neg_b)
                spec[1, im_b] = root * 1j * (pos_b - neg_b)
            else:
                spec[0, re_a], spec[0, im_a] = root * pos_a, root * 1j * pos_a
                spec[0, re_b], spec[0, im_b] = root * neg_b, -root * 1j * neg_b
                spec[1, re_b], spec[1, im_b] = root * pos_b, root * 1j * pos_b
                spec[1, re_a], spec[1, im_a] = root * neg_a, -root * 1j * neg_a
            table = to_bins[side, g]
            table[:, 0], table[:, 1] = spec[0, :, :width].real, spec[0, :, :width].imag
            table[:, 2], table[:, 3] = spec[1, :, :width].real, spec[1, :, :width].imag
            if g == 0:
                ends = (spec[0, :, 0].real, spec[1, :, 0].real, spec[0, :, width].real, spec[1, :, width].real)
            else:
                ends = tuple(
                    math.sqrt(2.0) * v
                    for v in (spec[0, :, 0].real, spec[0, :, 0].imag, spec[0, :, width].real, spec[0, :, width].imag)
                )
            for q in range(4):
                table[:, q, 0] = ends[q]
    lags = np.arange(LAGS)
    phase = 2 * np.pi * ((steps[:, None] * lags[None]) % (2 * width)) / (2 * width)
    lag = np.stack([2 * np.cos(phase), -2 * np.sin(phase)])
    lag[0, 0], lag[1, 0] = 1.0, (-1.0) ** lags
    bf16 = ml_dtypes.bfloat16
    forward_t = forward.transpose(0, 2, 1)
    forward_hi = forward_t.astype(bf16)
    forward_lo = (forward_t - forward_hi.astype(np.float64)).astype(bf16)
    bins_t = to_bins.transpose(0, 1, 3, 4, 2).reshape(2, groups, 4 * width, 4 * half).astype(bf16)
    lag = lag.reshape(2 * width, LAGS).astype(bf16)
    scale = residues / (2.0 * width * samples) / math.sqrt(samples)
    return forward_hi, forward_lo, bins_t, lag, scale


def real_dft(values):
    n = len(values)
    if n == 2:
        return [(values[0] + values[1], None), (values[0] - values[1], None)]
    even, odd = real_dft(values[0::2]), real_dft(values[1::2])
    out = [None] * (n // 2 + 1)
    for k in range(n // 4 + 1):
        (er, ei), (pr, pi) = even[k], odd[k]
        angle = -2.0 * math.pi * k / n
        c, s = math.cos(angle), math.sin(angle)
        if k == 0:
            out[0] = (er + pr, None)
            out[n // 2] = (er - pr, None)
            continue
        if 4 * k == n:
            out[k] = (er, -pr)
            continue
        if pi is None:
            tr, ti = pr * c, pr * s
        elif 8 * k == n:
            tr, ti = (pr + pi) * c, (pi - pr) * c
        else:
            tr, ti = pr * c - pi * s, pr * s + pi * c
        if ei is None:
            out[k] = (er + tr, ti)
            out[n // 2 - k] = (er - tr, ti)
        else:
            out[k] = (er + tr, ei + ti)
            out[n // 2 - k] = (er - tr, ti - ei)
    return out


def whiten_into_bins(own, windows, records, copies, fhi, flo, bins, yhi, ylo, spec, wide):
    channels, samples = records[0].shape
    width = LAGS
    residues = samples // width
    groups = residues // 2
    rows = 2 * windows * channels
    lanes = 2 * channels
    stride = windows * groups * 4 + 1
    step = 16

    def split(value):
        high = value.astype(jnp.bfloat16)
        return high, (value - high.astype(jnp.float32)).astype(jnp.bfloat16)

    def transform(n, carry):
        for index, ref in enumerate(records):
            which, w = divmod(index, windows)
            block = ref[pl.ds(pl.multiple_of(n * step, step), step), :].astype(jnp.float32)
            terms = real_dft([block[:, a * width:(a + 1) * width] for a in range(residues)])
            for g in range(groups):
                parts = terms[g] if g else (terms[0][0], terms[groups][0])
                for side, part in enumerate(parts):
                    hi, lo = split(part)
                    for copy_to in ((0, 1) if own else (which,)):
                        row = pl.multiple_of(w * lanes + copy_to * channels + n * step, step)
                        yhi[g, pl.ds(row, step), side * width:(side + 1) * width] = hi
                        ylo[g, pl.ds(row, step), side * width:(side + 1) * width] = lo
        return carry

    lax.fori_loop(0, channels // step, transform, 0)
    copies[0].wait()
    copies[1].wait()
    nt = (((1,), (1,)), ((), ()))
    bands = (samples // 2) // BAND

    def forward(g, power):
        value = lax.dot_general(fhi[g], yhi[g], nt, preferred_element_type=jnp.float32)
        value += lax.dot_general(flo[g], yhi[g], nt, preferred_element_type=jnp.float32)
        value += lax.dot_general(fhi[g], ylo[g], nt, preferred_element_type=jnp.float32)
        spec[g] = value
        squared = (value * value).reshape(2 * width // bands, bands, rows)
        return power + squared.sum(0)

    power = lax.fori_loop(0, groups, forward, jnp.zeros((bands, rows), jnp.float32), unroll=8)
    gain = 1.0 / jnp.sqrt(power * (1.0 / BAND) + 1e-6)
    copies[2].wait()

    def to_bins(g, carry):
        white = (spec[g].reshape(2 * width // bands, bands, rows) * gain[None]).reshape(2 * width, rows)
        value = jnp.dot(bins[g], white.astype(jnp.bfloat16), preferred_element_type=jnp.float32)
        parts = [value[q * width:(q + 1) * width] for q in range(4)]
        if own:
            left = lax.broadcasted_iota(jnp.int32, (width, rows), 1) % lanes < channels
            ends = lax.broadcasted_iota(jnp.int32, (width, rows), 0) == 0
            turned = [parts[1], -parts[0], parts[3], -parts[2]]
            zero = jnp.zeros_like(parts[0])
            real = [parts[q] if q < 2 else jnp.where(ends, zero, parts[q]) for q in range(4)]
            imag = [jnp.where(ends, zero if q < 2 else parts[q], turned[q]) for q in range(4)]
            parts = [jnp.where(left, real[q], imag[q]) for q in range(4)]
        for q in range(4):
            for w in range(windows):
                start = w * (groups * 4) + g * 4 + q
                wide[pl.ds(start, width, stride=stride), :] = parts[q][:, w * lanes:(w + 1) * lanes]
        return carry

    lax.fori_loop(0, groups, to_bins, 0, unroll=8)


def start_tables(sources, targets, sems):
    copies = [
        pltpu.make_async_copy(source, target, sems.at[i])
        for i, (source, target) in enumerate(zip(sources, targets))
    ]
    for copy in copies:
        copy.start()
    return copies


def cross_bins(own_ref, wide, cross):
    width, lanes, depth = own_ref.shape
    channels = lanes // 2

    def one(k, carry):
        partners = wide[pl.ds(k * (depth + 1), depth), :].astype(jnp.bfloat16)
        value = jnp.dot(own_ref[k], partners, preferred_element_type=jnp.float32)
        for part in range(2):
            cross[pl.ds(part * width + k, channels, stride=2 * width + 1), :] = (
                value[part * channels:(part + 1) * channels]
            )
        return carry

    lax.fori_loop(0, width, one, 0, unroll=16)


def own_kernel(windows, *refs):
    records, (fhi_hbm, flo_hbm, bins_hbm, out_ref, *scratch) = refs[:windows], refs[windows:]
    *scratch, sems = scratch
    copies = start_tables((fhi_hbm, flo_hbm, bins_hbm), scratch[:3], sems)
    whiten_into_bins(True, windows, records, copies, *scratch)
    wide = scratch[-1]
    width, lanes, depth = out_ref.shape

    def narrow(k, carry):
        out_ref[k] = wide[pl.ds(k * (depth + 1), depth), :].T.astype(jnp.bfloat16)
        return carry

    lax.fori_loop(0, width, narrow, 0, unroll=8)


def first_kernel(windows, *refs):
    records, (*sources, out_ref), scratch = refs[:2 * windows], refs[2 * windows:2 * windows + 5], refs[2 * windows + 5:]
    fhi, flo, bins, own_ref, *work, cross, sems = scratch
    copies = start_tables(sources, scratch[:4], sems)
    whiten_into_bins(False, windows, records, copies, fhi, flo, bins, *work)
    copies[3].wait()
    cross_bins(own_ref, work[-1], cross)
    rows = 2 * own_ref.shape[0]

    def narrow(i, carry):
        out_ref[pl.ds(pl.multiple_of(i * rows, rows), rows), :] = (
            cross[pl.ds(i * (rows + 1), rows), :].astype(jnp.bfloat16)
        )
        return carry

    lax.fori_loop(0, out_ref.shape[0] // rows, narrow, 0, unroll=4)


def last_kernel(windows, *refs):
    records, refs = refs[:2 * windows], refs[2 * windows:]
    sources, (lag_ref, slot_ref, keep_ref, out_hbm), scratch = refs[:5], refs[5:9], refs[9:]
    fhi, flo, bins, own_ref, early_ref, *work, cross, stage, sems, out_sems = scratch
    copies = start_tables(sources, scratch[:5], sems)
    whiten_into_bins(False, windows, records, copies, fhi, flo, bins, *work)
    copies[3].wait()
    copies[4].wait()
    cross_bins(own_ref, work[-1], cross)
    rows = 2 * own_ref.shape[0]
    _, offsets, per_out, channels, _ = stage.shape
    chunks = channels // per_out

    def leave(chunk, slot):
        target = out_hbm.at[:, pl.ds(chunk * per_out, per_out)]
        return pltpu.make_async_copy(stage.at[slot], target, out_sems.at[slot])

    def two_chunks(t, carry):
        for slot in range(2):
            chunk = t * 2 + slot

            @pl.when(t > 0)
            def _():
                leave(chunk - 2, slot).wait()

            def one(n, inner):
                i = chunk * per_out + n
                early = early_ref[pl.ds(pl.multiple_of(i * rows, rows), rows), :]
                late = cross[pl.ds(i * (rows + 1), rows), :].astype(jnp.bfloat16)
                both = jnp.concatenate([early, late], axis=1)
                value = lax.dot_general(both, lag_ref[...], (((0,), (0,)), ((), ())), preferred_element_type=jnp.float32)
                for o in range(offsets):
                    stage[slot, slot_ref[o], n] = value[o * channels:(o + 1) * channels] * keep_ref[o]
                return inner

            lax.fori_loop(0, per_out, one, 0, unroll=8)
            leave(chunk, slot).start()
        return carry

    lax.fori_loop(0, chunks // 2, two_chunks, 0)
    for slot in range(2):
        leave(chunks - 2 + slot, slot).wait()


def call(kernel, name, windows, operands, tables, extra, out_shape, out_space, buffers=(), signals=()):
    channels, samples = operands[0].shape
    width = LAGS
    groups = samples // width // 2
    rows = 2 * windows * channels
    depth = windows * groups * 4
    lanes = 2 * channels
    any_spec = pl.BlockSpec(memory_space=pl.ANY)
    vmem_spec = pl.BlockSpec(memory_space=pltpu.VMEM)
    smem_spec = pl.BlockSpec(memory_space=pltpu.SMEM)
    small = [vmem_spec if v.ndim > 1 else smem_spec for v in extra]
    return pl.pallas_call(
        functools.partial(kernel, windows),
        out_shape=out_shape,
        in_specs=[vmem_spec] * len(operands) + [any_spec] * len(tables) + small,
        out_specs=pl.BlockSpec(memory_space=out_space),
        scratch_shapes=[pltpu.VMEM(t.shape, jnp.bfloat16) for t in tables] + [
            pltpu.VMEM((groups, rows, 2 * width), jnp.bfloat16),
            pltpu.VMEM((groups, rows, 2 * width), jnp.bfloat16),
            pltpu.VMEM((groups, 2 * width, rows), jnp.float32),
            pltpu.VMEM((width * (depth + 1), lanes), jnp.float32),
            *buffers,
            pltpu.SemaphoreType.DMA((len(tables),)),
            *signals,
        ],
        compiler_params=pltpu.CompilerParams(vmem_limit_bytes=VMEM_LIMIT),
        cost_estimate=pl.CostEstimate(
            flops=20 * groups * rows * 4 * width * width, bytes_accessed=14 * 2**20, transcendentals=0
        ),
        name=name,
    )(*operands, *tables, *extra)


def per_device(traces, live, reach):
    windows, channels, samples = traces.shape
    blocks = lax.axis_size("fibre")
    splits = lax.axis_size("freq")
    owned = OFF // splits
    place = lax.axis_index("freq")
    forward_hi, forward_lo, bins_t, lag, scale = build_tables(samples)
    forward_hi, forward_lo = jnp.asarray(forward_hi), jnp.asarray(forward_lo)
    masked = [jnp.where(live[:, None] > 0, traces[w], jnp.zeros((), traces.dtype)) for w in range(windows)]

    quads = blocks // owned
    half = owned // 2
    u = lax.axis_index("fibre") % owned
    core, pair = u % half, u // half

    def rank(q, pair, core, part):
        return (q * owned + pair * half + core) * splits + part

    def send(payload, route):
        pairs = []
        for q in range(quads):
            for p in range(2):
                for c in range(half):
                    for g in range(splits):
                        source = route(q, p, c, g)
                        if source[0] < quads:
                            pairs.append((rank(*source), rank(q, p, c, g)))
        return lax.ppermute(payload, ("fibre", "freq"), pairs)

    def from_neighbours(mine, upper):
        core_payload = jnp.where((core == 1) & (place == 0), mine, upper)
        across_payload = jnp.where((pair == 1) & (place == 0), mine, upper)
        beside = send(core_payload, lambda q, p, c, g: (q + c * g, p, 1 - c, 1 - g if c else g))
        across = send(across_payload, lambda q, p, c, g: (q + p * g, 1 - p, c, g))
        return jnp.where(place == 0, mine, upper), beside, across

    width = LAGS
    lanes = 2 * channels
    depth = windows * samples // width * 2
    crossed = pltpu.VMEM((channels * (2 * width + 1), lanes), jnp.float32)
    own_tables = (forward_hi, forward_lo, jnp.asarray(bins_t[1]))
    tables = (forward_hi, forward_lo, jnp.asarray(bins_t[0]))

    above = lambda q, p, c, g: (quads if p and c and not g else q + 1, p, c, g)
    upper = [send(mine, above) for mine in masked]
    upper[0], *mine = lax.optimization_barrier((upper[0], *masked))
    own = call(
        own_kernel, "own_bins", windows, mine, own_tables, (),
        jax.ShapeDtypeStruct((width, lanes, depth), jnp.bfloat16), pltpu.VMEM,
    )
    here, beside, across = [], [], []
    for w in range(windows):
        if w:
            upper[w], beside[w - 1], own = lax.optimization_barrier((upper[w], beside[w - 1], own))
        for known, new in zip((here, beside, across), from_neighbours(masked[w], upper[w])):
            known.append(new)
    across[0], beside[-1] = lax.optimization_barrier((across[0], beside[-1]))
    early = call(
        first_kernel, "first_pair", windows, here + beside, (*tables, own), (),
        jax.ShapeDtypeStruct((channels * 2 * width, lanes), jnp.bfloat16), pltpu.VMEM, (crossed,),
    )
    *across, early = lax.optimization_barrier((*across, early))
    across_beside = [send(block, lambda q, p, c, g: (q, p, 1 - c, g)) for block in across]
    slots = jnp.stack([0, 1 + 2 * core, 2, 3 - 2 * core]).astype(jnp.int32)
    offset_ids = place * owned + slots
    keep = jnp.where(offset_ids < reach[0], jnp.float32(scale), jnp.float32(0.0))
    result = call(
        last_kernel, "second_pair", windows, across + across_beside, (*tables, own, early),
        (jnp.asarray(lag), slots, keep),
        jax.ShapeDtypeStruct((owned, channels, channels, LAGS), jnp.float32), pl.ANY,
        (crossed, pltpu.VMEM((2, owned, channels // 8, channels, LAGS), jnp.float32)), (pltpu.SemaphoreType.DMA((2,)),),
    )
    return result[None]


def solution(mesh):
    placed = (P(None, "fibre", None), P("fibre"), P("fibre"))
    return jax.shard_map(
        per_device,
        mesh=mesh,
        in_specs=placed,
        out_specs=P("fibre", "freq", None, None, None),
        check_vma=False,
    )
```

```python
import functools
import math

import jax
import jax.numpy as jnp
import ml_dtypes
import numpy as np
from jax import lax
from jax.experimental import pallas as pl
from jax.experimental.pallas import tpu as pltpu
from jax.sharding import PartitionSpec as P

BAND = 64
OFF = 8
LAGS = 128
VMEM_LIMIT = 50 * 2**20


def leak_spectrum(freqs, samples, window, shift, slots, period):
    steps = np.arange(window)
    tone = np.exp(2j * np.pi * ((freqs[:, None] * (steps - shift)[None]) % samples) / samples)
    bins = np.exp(-2j * np.pi * ((steps[:, None] * slots[None]) % period) / period)
    return tone @ bins


@functools.lru_cache(maxsize=None)
def build_tables(samples):
    width = LAGS
    residues = samples // width
    groups = residues // 2
    half = width // 2
    per_band = BAND // residues
    order = np.concatenate([np.arange(i, half, per_band) for i in range(per_band)])
    steps = np.arange(width)
    slots = np.arange(width + 1)
    forward = np.zeros((groups, 2 * width, 4 * half))
    to_bins = np.zeros((2, groups, 4 * half, 4, width))
    root = 1.0 / math.sqrt(2.0)
    re_a, im_a, re_b, im_b = (slice(i * half, (i + 1) * half) for i in range(4))
    for g in range(groups):
        freq_a = g + residues * order
        freq_b = (residues - g if g else groups) + residues * order
        wave_a = np.exp(-2j * np.pi * ((steps[:, None] * freq_a[None]) % samples) / samples)
        wave_b = np.exp(-2j * np.pi * ((steps[:, None] * freq_b[None]) % samples) / samples)
        top, low = forward[g, :width], forward[g, width:]
        top[:, re_a], top[:, im_a] = wave_a.real, wave_a.imag
        if g == 0:
            low[:, re_b], low[:, im_b] = wave_b.real, wave_b.imag
        else:
            low[:, re_a], low[:, im_a] = -wave_a.imag, wave_a.real
            top[:, re_b], top[:, im_b] = wave_b.real, wave_b.imag
            low[:, re_b], low[:, im_b] = wave_b.imag, -wave_b.real
        for side in range(2):
            window, shift = ((width, 0), (2 * width, half))[side]
            leak = functools.partial(
                leak_spectrum, samples=samples, window=window, shift=shift, slots=slots, period=2 * width
            )
            pos_a, neg_a, pos_b, neg_b = leak(freq_a), leak(-freq_a), leak(freq_b), leak(-freq_b)
            spec = np.zeros((2, 4 * half, width + 1), complex)
            if g == 0:
                zero = (freq_a == 0)[:, None]
                spec[0, re_a] = np.where(zero, pos_a, root * (pos_a + neg_a))
                spec[0, im_a] = np.where(zero, 0.0, root * 1j * (pos_a - neg_a))
                spec[1, re_b] = root * (pos_b + neg_b)
                spec[1, im_b] = root * 1j * (pos_b - neg_b)
            else:
                spec[0, re_a], spec[0, im_a] = root * pos_a, root * 1j * pos_a
                spec[0, re_b], spec[0, im_b] = root * neg_b, -root * 1j * neg_b
                spec[1, re_b], spec[1, im_b] = root * pos_b, root * 1j * pos_b
                spec[1, re_a], spec[1, im_a] = root * neg_a, -root * 1j * neg_a
            table = to_bins[side, g]
            table[:, 0], table[:, 1] = spec[0, :, :width].real, spec[0, :, :width].imag
            table[:, 2], table[:, 3] = spec[1, :, :width].real, spec[1, :, :width].imag
            if g == 0:
                ends = (spec[0, :, 0].real, spec[1, :, 0].real, spec[0, :, width].real, spec[1, :, width].real)
            else:
                ends = tuple(
                    math.sqrt(2.0) * v
                    for v in (spec[0, :, 0].real, spec[0, :, 0].imag, spec[0, :, width].real, spec[0, :, width].imag)
                )
            for q in range(4):
                table[:, q, 0] = ends[q]
    lags = np.arange(LAGS)
    phase = 2 * np.pi * ((steps[:, None] * lags[None]) % (2 * width)) / (2 * width)
    lag = np.stack([2 * np.cos(phase), -2 * np.sin(phase)])
    lag[0, 0], lag[1, 0] = 1.0, (-1.0) ** lags
    bf16 = ml_dtypes.bfloat16
    forward_t = forward.transpose(0, 2, 1)
    forward_hi = forward_t.astype(bf16)
    forward_lo = (forward_t - forward_hi.astype(np.float64)).astype(bf16)
    bins_t = to_bins.transpose(0, 1, 3, 4, 2).reshape(2, groups, 4 * width, 4 * half).astype(bf16)
    lag = lag.reshape(2 * width, LAGS).T.astype(bf16)
    scale = residues / (2.0 * width * samples) / math.sqrt(samples)
    return forward_hi, forward_lo, bins_t, lag, scale


def real_dft(values):
    n = len(values)
    if n == 2:
        return [(values[0] + values[1], None), (values[0] - values[1], None)]
    even, odd = real_dft(values[0::2]), real_dft(values[1::2])
    out = [None] * (n // 2 + 1)
    for k in range(n // 4 + 1):
        (er, ei), (pr, pi) = even[k], odd[k]
        angle = -2.0 * math.pi * k / n
        c, s = math.cos(angle), math.sin(angle)
        if k == 0:
            out[0] = (er + pr, None)
            out[n // 2] = (er - pr, None)
            continue
        if 4 * k == n:
            out[k] = (er, -pr)
            continue
        if pi is None:
            tr, ti = pr * c, pr * s
        elif 8 * k == n:
            tr, ti = (pr + pi) * c, (pi - pr) * c
        else:
            tr, ti = pr * c - pi * s, pr * s + pi * c
        if ei is None:
            out[k] = (er + tr, ti)
            out[n // 2 - k] = (er - tr, ti)
        else:
            out[k] = (er + tr, ei + ti)
            out[n // 2 - k] = (er - tr, ti - ei)
    return out


def whiten(own, windows, records, copies, fhi, flo, yhi, ylo, spec):
    channels, samples = records[0].shape
    width = LAGS
    residues = samples // width
    groups = residues // 2
    rows = 2 * windows * channels
    lanes = 2 * channels
    step = 16

    def split(value):
        high = value.astype(jnp.bfloat16)
        return high, (value - high.astype(jnp.float32)).astype(jnp.bfloat16)

    def transform(n, carry):
        for index, ref in enumerate(records):
            which, w = divmod(index, windows)
            block = ref[pl.ds(pl.multiple_of(n * step, step), step), :].astype(jnp.float32)
            terms = real_dft([block[:, a * width:(a + 1) * width] for a in range(residues)])
            for g in range(groups):
                parts = terms[g] if g else (terms[0][0], terms[groups][0])
                for side, part in enumerate(parts):
                    hi, lo = split(part)
                    for copy_to in ((0, 1) if own else (which,)):
                        row = pl.multiple_of(w * lanes + copy_to * channels + n * step, step)
                        yhi[g, pl.ds(row, step), side * width:(side + 1) * width] = hi
                        ylo[g, pl.ds(row, step), side * width:(side + 1) * width] = lo
        return carry

    lax.fori_loop(0, channels // step, transform, 0)
    copies[0].wait()
    copies[1].wait()
    nt = (((1,), (1,)), ((), ()))
    bands = (samples // 2) // BAND

    def forward(g, power):
        value = lax.dot_general(fhi[g], yhi[g], nt, preferred_element_type=jnp.float32)
        value += lax.dot_general(flo[g], yhi[g], nt, preferred_element_type=jnp.float32)
        value += lax.dot_general(fhi[g], ylo[g], nt, preferred_element_type=jnp.float32)
        spec[g] = value
        squared = (value * value).reshape(2 * width // bands, bands, rows)
        return power + squared.sum(0)

    power = lax.fori_loop(0, groups, forward, jnp.zeros((bands, rows), jnp.float32), unroll=8)
    gain = 1.0 / jnp.sqrt(power * (1.0 / BAND) + 1e-6)

    def white(g):
        value = spec[g].reshape(2 * width // bands, bands, rows) * gain[None]
        return value.reshape(2 * width, rows).astype(jnp.bfloat16)

    return white


def fill_bins(own, windows, white, bins, wide):
    groups, parts, _ = bins.shape
    width, lanes = parts // 4, wide.shape[1]
    rows, channels = windows * lanes, lanes // 2
    stride = windows * groups * 4 + 1

    def to_bins(g, carry):
        value = jnp.dot(bins[g], white(g), preferred_element_type=jnp.float32)
        parts = [value[q * width:(q + 1) * width] for q in range(4)]
        if own:
            left = lax.broadcasted_iota(jnp.int32, (width, rows), 1) % lanes < channels
            ends = lax.broadcasted_iota(jnp.int32, (width, rows), 0) == 0
            turned = [parts[1], -parts[0], parts[3], -parts[2]]
            zero = jnp.zeros_like(parts[0])
            real = [parts[q] if q < 2 else jnp.where(ends, zero, parts[q]) for q in range(4)]
            imag = [jnp.where(ends, zero if q < 2 else parts[q], turned[q]) for q in range(4)]
            parts = [jnp.where(left, real[q], imag[q]) for q in range(4)]
        for q in range(4):
            for w in range(windows):
                start = w * (groups * 4) + g * 4 + q
                wide[pl.ds(start, width, stride=stride), :] = parts[q][:, w * lanes:(w + 1) * lanes]
        return carry

    lax.fori_loop(0, groups, to_bins, 0, unroll=8)


def start_tables(sources, targets, sems):
    copies = [
        pltpu.make_async_copy(source, target, sems.at[i])
        for i, (source, target) in enumerate(zip(sources, targets))
    ]
    for copy in copies:
        copy.start()
    return copies


def cross_bins(own_ref, wide, cross):
    width, lanes, depth = own_ref.shape
    channels = lanes // 2

    def one(k, carry):
        partners = wide[pl.ds(k * (depth + 1), depth), :].astype(jnp.bfloat16)
        value = jnp.dot(own_ref[k], partners, preferred_element_type=jnp.float32)
        for part in range(2):
            cross[pl.ds(part * width + k, channels, stride=2 * width + 1), :] = (
                value[part * channels:(part + 1) * channels]
            )
        return carry

    lax.fori_loop(0, width, one, 0, unroll=16)


def own_spectra_kernel(windows, *refs):
    records, (fhi_hbm, flo_hbm, out_ref, fhi, flo, yhi, ylo, spec, sems) = refs[:windows], refs[windows:]
    copies = start_tables((fhi_hbm, flo_hbm), (fhi, flo), sems)
    white = whiten(True, windows, records, copies, fhi, flo, yhi, ylo, spec)

    def write(g, carry):
        out_ref[g] = white(g)
        return carry

    lax.fori_loop(0, out_ref.shape[0], write, 0, unroll=4)


def own_bins_kernel(windows, white_ref, bins, out_ref, wide):
    fill_bins(True, windows, lambda g: white_ref[g], bins, wide)
    width, lanes, depth = out_ref.shape

    def narrow(k, carry):
        out_ref[k] = wide[pl.ds(k * (depth + 1), depth), :].T.astype(jnp.bfloat16)
        return carry

    lax.fori_loop(0, width, narrow, 0, unroll=8)


def first_kernel(windows, *refs):
    records, (*sources, out_ref), scratch = refs[:2 * windows], refs[2 * windows:2 * windows + 5], refs[2 * windows + 5:]
    fhi, flo, bins, own_ref, *work, wide, cross, sems = scratch
    copies = start_tables(sources, scratch[:4], sems)
    white = whiten(False, windows, records, copies, fhi, flo, *work)
    copies[2].wait()
    fill_bins(False, windows, white, bins, wide)
    copies[3].wait()
    cross_bins(own_ref, wide, cross)
    rows = 2 * own_ref.shape[0]

    def narrow(i, carry):
        out_ref[pl.ds(pl.multiple_of(i * rows, rows), rows), :] = (
            cross[pl.ds(i * (rows + 1), rows), :].astype(jnp.bfloat16)
        )
        return carry

    lax.fori_loop(0, out_ref.shape[0] // rows, narrow, 0, unroll=4)


def last_kernel(windows, *refs):
    records, refs = refs[:2 * windows], refs[2 * windows:]
    sources, (lag_ref, slot_ref, keep_ref, out_hbm), scratch = refs[:5], refs[5:9], refs[9:]
    fhi, flo, bins, own_ref, early_ref, *work, wide, cross, stage, sems, out_sems = scratch
    copies = start_tables(sources, scratch[:5], sems)
    white = whiten(False, windows, records, copies, fhi, flo, *work)
    copies[2].wait()
    fill_bins(False, windows, white, bins, wide)
    copies[3].wait()
    copies[4].wait()
    cross_bins(own_ref, wide, cross)
    rows = 2 * own_ref.shape[0]
    _, offsets, per_out, channels, _ = stage.shape
    chunks = channels // per_out

    def leave(chunk, slot):
        target = out_hbm.at[:, pl.ds(chunk * per_out, per_out)]
        return pltpu.make_async_copy(stage.at[slot], target, out_sems.at[slot])

    def two_chunks(t, carry):
        for slot in range(2):
            chunk = t * 2 + slot

            @pl.when(t > 0)
            def _():
                leave(chunk - 2, slot).wait()

            def one(n, inner):
                i = chunk * per_out + n
                early = early_ref[pl.ds(pl.multiple_of(i * rows, rows), rows), :]
                late = cross[pl.ds(i * (rows + 1), rows), :].astype(jnp.bfloat16)
                both = jnp.concatenate([early, late], axis=1)
                value = jnp.dot(lag_ref[...], both, preferred_element_type=jnp.float32).T
                for o in range(offsets):
                    stage[slot, slot_ref[o], n] = value[o * channels:(o + 1) * channels] * keep_ref[o]
                return inner

            lax.fori_loop(0, per_out, one, 0, unroll=8)
            leave(chunk, slot).start()
        return carry

    lax.fori_loop(0, chunks // 2, two_chunks, 0)
    for slot in range(2):
        leave(chunks - 2 + slot, slot).wait()


def call(kernel, name, windows, operands, tables, extra, out_shape, out_space, buffers=(), signals=()):
    channels, samples = operands[0].shape
    width = LAGS
    groups = samples // width // 2
    rows = 2 * windows * channels
    depth = windows * groups * 4
    lanes = 2 * channels
    any_spec = pl.BlockSpec(memory_space=pl.ANY)
    vmem_spec = pl.BlockSpec(memory_space=pltpu.VMEM)
    smem_spec = pl.BlockSpec(memory_space=pltpu.SMEM)
    small = [vmem_spec if v.ndim > 1 else smem_spec for v in extra]
    return pl.pallas_call(
        functools.partial(kernel, windows),
        out_shape=out_shape,
        in_specs=[vmem_spec] * len(operands) + [any_spec] * len(tables) + small,
        out_specs=pl.BlockSpec(memory_space=out_space),
        scratch_shapes=[pltpu.VMEM(t.shape, jnp.bfloat16) for t in tables] + [
            pltpu.VMEM((groups, rows, 2 * width), jnp.bfloat16),
            pltpu.VMEM((groups, rows, 2 * width), jnp.bfloat16),
            pltpu.VMEM((groups, 2 * width, rows), jnp.float32),
            *buffers,
            pltpu.SemaphoreType.DMA((len(tables),)),
            *signals,
        ],
        compiler_params=pltpu.CompilerParams(vmem_limit_bytes=VMEM_LIMIT),
        cost_estimate=pl.CostEstimate(
            flops=20 * groups * rows * 4 * width * width, bytes_accessed=14 * 2**20, transcendentals=0
        ),
        name=name,
    )(*operands, *tables, *extra)


def per_device(traces, live, reach):
    windows, channels, samples = traces.shape
    blocks = lax.axis_size("fibre")
    splits = lax.axis_size("freq")
    owned = OFF // splits
    place = lax.axis_index("freq")
    forward_hi, forward_lo, bins_t, lag, scale = build_tables(samples)
    forward_hi, forward_lo = jnp.asarray(forward_hi), jnp.asarray(forward_lo)
    masked = [jnp.where(live[:, None] > 0, traces[w], jnp.zeros((), traces.dtype)) for w in range(windows)]

    quads = blocks // owned
    half = owned // 2
    u = lax.axis_index("fibre") % owned
    core, pair = u % half, u // half

    def rank(q, pair, core, part):
        return (q * owned + pair * half + core) * splits + part

    def send(payload, route):
        pairs = []
        for q in range(quads):
            for p in range(2):
                for c in range(half):
                    for g in range(splits):
                        source = route(q, p, c, g)
                        if source[0] < quads:
                            pairs.append((rank(*source), rank(q, p, c, g)))
        return lax.ppermute(payload, ("fibre", "freq"), pairs)

    def from_neighbours(mine, upper):
        core_payload = jnp.where((core == 1) & (place == 0), mine, upper)
        across_payload = jnp.where((pair == 1) & (place == 0), mine, upper)
        beside = send(core_payload, lambda q, p, c, g: (q + c * g, p, 1 - c, 1 - g if c else g))
        across = send(across_payload, lambda q, p, c, g: (q + p * g, 1 - p, c, g))
        return jnp.where(place == 0, mine, upper), beside, across

    width = LAGS
    lanes = 2 * channels
    depth = windows * samples // width * 2
    crossed = pltpu.VMEM((channels * (2 * width + 1), lanes), jnp.float32)
    wide = pltpu.VMEM((width * (depth + 1), lanes), jnp.float32)
    tables = (forward_hi, forward_lo, jnp.asarray(bins_t[0]))

    above = lambda q, p, c, g: (quads if p and c and not g else q + 1, p, c, g)
    upper = [send(mine, above) for mine in masked]
    groups = samples // width // 2
    own_white = call(
        own_spectra_kernel, "own_spectra", windows, masked, (forward_hi, forward_lo), (),
        jax.ShapeDtypeStruct((groups, 2 * width, windows * lanes), jnp.bfloat16), pltpu.VMEM,
    )
    upper[0], own_white = lax.optimization_barrier((upper[0], own_white))
    own = pl.pallas_call(
        functools.partial(own_bins_kernel, windows),
        out_shape=jax.ShapeDtypeStruct((width, lanes, depth), jnp.bfloat16),
        in_specs=[pl.BlockSpec(memory_space=pltpu.VMEM)] * 2,
        out_specs=pl.BlockSpec(memory_space=pltpu.VMEM),
        scratch_shapes=[wide],
        compiler_params=pltpu.CompilerParams(vmem_limit_bytes=VMEM_LIMIT),
        cost_estimate=pl.CostEstimate(
            flops=8 * groups * windows * lanes * 4 * width * width, bytes_accessed=10 * 2**20, transcendentals=0
        ),
        name="own_bins",
    )(own_white, jnp.asarray(bins_t[1]))
    here, beside, across = [], [], []
    for w in range(windows):
        if w:
            upper[w], beside[w - 1], own = lax.optimization_barrier((upper[w], beside[w - 1], own))
        for known, new in zip((here, beside, across), from_neighbours(masked[w], upper[w])):
            known.append(new)
    across[0], beside[-1] = lax.optimization_barrier((across[0], beside[-1]))
    early = call(
        first_kernel, "first_pair", windows, here + beside, (*tables, own), (),
        jax.ShapeDtypeStruct((channels * 2 * width, lanes), jnp.bfloat16), pltpu.VMEM, (wide, crossed),
    )
    *across, early = lax.optimization_barrier((*across, early))
    across_beside = [send(block, lambda q, p, c, g: (q, p, 1 - c, g)) for block in across]
    slots = jnp.stack([0, 1 + 2 * core, 2, 3 - 2 * core]).astype(jnp.int32)
    offset_ids = place * owned + slots
    keep = jnp.where(offset_ids < reach[0], jnp.float32(scale), jnp.float32(0.0))
    result = call(
        last_kernel, "second_pair", windows, across + across_beside, (*tables, own, early),
        (jnp.asarray(lag), slots, keep),
        jax.ShapeDtypeStruct((owned, channels, channels, LAGS), jnp.float32), pl.ANY,
        (wide, crossed, pltpu.VMEM((2, owned, channels // 8, channels, LAGS), jnp.float32)), (pltpu.SemaphoreType.DMA((2,)),),
    )
    return result[None]


def solution(mesh):
    placed = (P(None, "fibre", None), P("fibre"), P("fibre"))
    return jax.shard_map(
        per_device,
        mesh=mesh,
        in_specs=placed,
        out_specs=P("fibre", "freq", None, None, None),
        check_vma=False,
    )
```

```python
import functools
import math

import jax
import jax.numpy as jnp
import ml_dtypes
import numpy as np
from jax import lax
from jax.experimental import pallas as pl
from jax.experimental.pallas import tpu as pltpu
from jax.sharding import PartitionSpec as P

BAND = 64
OFF = 8
LAGS = 128


def leak_spectrum(freqs, samples, window, shift, slots, period):
    steps = np.arange(window)
    tone = np.exp(2j * np.pi * ((freqs[:, None] * (steps - shift)[None]) % samples) / samples)
    bins = np.exp(-2j * np.pi * ((steps[:, None] * slots[None]) % period) / period)
    return tone @ bins


@functools.lru_cache(maxsize=None)
def build_tables(samples):
    width = LAGS
    residues = samples // width
    groups = residues // 2
    half = width // 2
    per_band = BAND // residues
    order = np.concatenate([np.arange(i, half, per_band) for i in range(per_band)])
    steps = np.arange(width)
    slots = np.arange(width + 1)
    forward = np.zeros((groups, 2 * width, 4 * half))
    to_bins = np.zeros((2, groups, 4 * half, 4, width))
    root = 1.0 / math.sqrt(2.0)
    re_a, im_a, re_b, im_b = (slice(i * half, (i + 1) * half) for i in range(4))
    for g in range(groups):
        freq_a = g + residues * order
        freq_b = (residues - g if g else groups) + residues * order
        wave_a = np.exp(-2j * np.pi * ((steps[:, None] * freq_a[None]) % samples) / samples)
        wave_b = np.exp(-2j * np.pi * ((steps[:, None] * freq_b[None]) % samples) / samples)
        top, low = forward[g, :width], forward[g, width:]
        top[:, re_a], top[:, im_a] = wave_a.real, wave_a.imag
        if g == 0:
            low[:, re_b], low[:, im_b] = wave_b.real, wave_b.imag
        else:
            low[:, re_a], low[:, im_a] = -wave_a.imag, wave_a.real
            top[:, re_b], top[:, im_b] = wave_b.real, wave_b.imag
            low[:, re_b], low[:, im_b] = wave_b.imag, -wave_b.real
        for side in range(2):
            window, shift = ((width, 0), (2 * width, half))[side]
            leak = functools.partial(
                leak_spectrum, samples=samples, window=window, shift=shift, slots=slots, period=2 * width
            )
            pos_a, neg_a, pos_b, neg_b = leak(freq_a), leak(-freq_a), leak(freq_b), leak(-freq_b)
            spec = np.zeros((2, 4 * half, width + 1), complex)
            if g == 0:
                zero = (freq_a == 0)[:, None]
                spec[0, re_a] = np.where(zero, pos_a, root * (pos_a + neg_a))
                spec[0, im_a] = np.where(zero, 0.0, root * 1j * (pos_a - neg_a))
                spec[1, re_b] = root * (pos_b + neg_b)
                spec[1, im_b] = root * 1j * (pos_b - neg_b)
            else:
                spec[0, re_a], spec[0, im_a] = root * pos_a, root * 1j * pos_a
                spec[0, re_b], spec[0, im_b] = root * neg_b, -root * 1j * neg_b
                spec[1, re_b], spec[1, im_b] = root * pos_b, root * 1j * pos_b
                spec[1, re_a], spec[1, im_a] = root * neg_a, -root * 1j * neg_a
            table = to_bins[side, g]
            table[:, 0], table[:, 1] = spec[0, :, :width].real, spec[0, :, :width].imag
            table[:, 2], table[:, 3] = spec[1, :, :width].real, spec[1, :, :width].imag
            if g == 0:
                ends = (spec[0, :, 0].real, spec[1, :, 0].real, spec[0, :, width].real, spec[1, :, width].real)
            else:
                ends = tuple(
                    math.sqrt(2.0) * v
                    for v in (spec[0, :, 0].real, spec[0, :, 0].imag, spec[0, :, width].real, spec[0, :, width].imag)
                )
            for q in range(4):
                table[:, q, 0] = ends[q]
    lags = np.arange(LAGS)
    phase = 2 * np.pi * ((steps[:, None] * lags[None]) % (2 * width)) / (2 * width)
    lag = np.stack([2 * np.cos(phase), -2 * np.sin(phase)])
    lag[0, 0], lag[1, 0] = 1.0, (-1.0) ** lags
    bf16 = ml_dtypes.bfloat16
    forward_t = forward.transpose(0, 2, 1)
    forward_hi = forward_t.astype(bf16)
    forward_lo = (forward_t - forward_hi.astype(np.float64)).astype(bf16)
    bins_t = to_bins.transpose(0, 1, 3, 4, 2).reshape(2, groups, 4 * width, 4 * half).astype(bf16)
    lag = lag.reshape(2 * width, LAGS).T.astype(bf16)
    scale = residues / (2.0 * width * samples) / math.sqrt(samples)
    return forward_hi, forward_lo, bins_t, lag, scale


def real_dft(values):
    n = len(values)
    if n == 2:
        return [(values[0] + values[1], None), (values[0] - values[1], None)]
    even, odd = real_dft(values[0::2]), real_dft(values[1::2])
    out = [None] * (n // 2 + 1)
    for k in range(n // 4 + 1):
        (er, ei), (pr, pi) = even[k], odd[k]
        angle = -2.0 * math.pi * k / n
        c, s = math.cos(angle), math.sin(angle)
        if k == 0:
            out[0] = (er + pr, None)
            out[n // 2] = (er - pr, None)
            continue
        if 4 * k == n:
            out[k] = (er, -pr)
            continue
        if pi is None:
            tr, ti = pr * c, pr * s
        elif 8 * k == n:
            tr, ti = (pr + pi) * c, (pi - pr) * c
        else:
            tr, ti = pr * c - pi * s, pr * s + pi * c
        if ei is None:
            out[k] = (er + tr, ti)
            out[n // 2 - k] = (er - tr, ti)
        else:
            out[k] = (er + tr, ei + ti)
            out[n // 2 - k] = (er - tr, ti - ei)
    return out


def whiten(copies_of, records, copies, fhi, flo, yhi, ylo, spec):
    channels, samples = records[0].shape
    width = LAGS
    residues = samples // width
    groups = residues // 2
    rows = len(records) * copies_of * channels
    tiles = rows // width
    step = 16

    def split(value):
        high = value.astype(jnp.bfloat16)
        return high, (value - high.astype(jnp.float32)).astype(jnp.bfloat16)

    def transform(n, carry):
        for index, ref in enumerate(records):
            block = ref[pl.ds(pl.multiple_of(n * step, step), step), :].astype(jnp.float32)
            terms = real_dft([block[:, a * width:(a + 1) * width] for a in range(residues)])
            for g in range(groups):
                parts = terms[g] if g else (terms[0][0], terms[groups][0])
                for side, part in enumerate(parts):
                    hi, lo = split(part)
                    for copy_to in range(copies_of):
                        row = pl.multiple_of((index * copies_of + copy_to) * channels + n * step, step)
                        yhi[g, pl.ds(row, step), side * width:(side + 1) * width] = hi
                        ylo[g, pl.ds(row, step), side * width:(side + 1) * width] = lo
        return carry

    lax.fori_loop(0, channels // step, transform, 0)
    copies[0].wait()
    copies[1].wait()
    nt = (((1,), (1,)), ((), ()))
    bands = (samples // 2) // BAND

    def place(g, tile):
        return pl.ds(pl.multiple_of((g * tiles + tile) * 2 * width, 2 * width), 2 * width)

    def forward(g, power):
        value = lax.dot_general(fhi[g], yhi[g], nt, preferred_element_type=jnp.float32)
        value += lax.dot_general(flo[g], yhi[g], nt, preferred_element_type=jnp.float32)
        value += lax.dot_general(fhi[g], ylo[g], nt, preferred_element_type=jnp.float32)
        for tile in range(tiles):
            spec[place(g, tile), :] = value[:, tile * width:(tile + 1) * width]
        squared = (value * value).reshape(2 * width // bands, bands, rows)
        return power + squared.sum(0)

    power = lax.fori_loop(0, groups, forward, jnp.zeros((bands, rows), jnp.float32), unroll=8)
    gain = 1.0 / jnp.sqrt(power * (1.0 / BAND) + 1e-6)

    def white(g):
        value = jnp.concatenate([spec[place(g, tile), :] for tile in range(tiles)], axis=1)
        value = value.reshape(2 * width // bands, bands, rows) * gain[None]
        return value.reshape(2 * width, rows).astype(jnp.bfloat16)

    return white


def start_copies(sources, targets, sems):
    copies = [
        pltpu.make_async_copy(source, target, sems.at[i])
        for i, (source, target) in enumerate(zip(sources, targets))
    ]
    for copy in copies:
        copy.start()
    return copies


def write_out(chunks, fill, stage, out_hbm, sems):
    per_chunk = stage.shape[0] // chunks
    copies = []
    for chunk in range(chunks):
        def one(n, carry):
            stage[chunk * per_chunk + n] = fill(chunk * per_chunk + n)
            return carry

        lax.fori_loop(0, per_chunk, one, 0, unroll=8)
        part = pl.ds(chunk * per_chunk, per_chunk)
        copies.append(pltpu.make_async_copy(stage.at[part], out_hbm.at[part], sems.at[chunk]))
        copies[-1].start()
    for copy in copies:
        copy.wait()


def own_spectra_kernel(windows, *refs):
    records, (fhi_hbm, flo_hbm, out_ref, fhi, flo, yhi, ylo, spec, sems) = refs[:windows], refs[windows:]
    copies = start_copies((fhi_hbm, flo_hbm), (fhi, flo), sems)
    white = whiten(2, records, copies, fhi, flo, yhi, ylo, spec)

    def write(g, carry):
        out_ref[g] = white(g)
        return carry

    lax.fori_loop(0, out_ref.shape[0], write, 0, unroll=4)


def own_bins_kernel(windows, white_ref, bins_hbm, out_hbm, bins, wide, stage, sems, out_sems):
    groups, rows, _ = bins.shape
    width, lanes, depth = stage.shape
    chunks = sems.shape[0]
    per_chunk = groups // chunks
    parts = [pl.ds(chunk * per_chunk, per_chunk) for chunk in range(chunks)]
    copies = start_copies([bins_hbm.at[p] for p in parts], [bins.at[p] for p in parts], sems)
    left = lax.broadcasted_iota(jnp.int32, (width, windows * lanes), 1) % lanes < lanes // 2
    ends = lax.broadcasted_iota(jnp.int32, (width, windows * lanes), 0) == 0
    for chunk in range(chunks):
        copies[chunk].wait()
        for g in range(chunk * per_chunk, (chunk + 1) * per_chunk):
            value = jnp.dot(bins[g], white_ref[g], preferred_element_type=jnp.float32)
            parts = [value[q * width:(q + 1) * width] for q in range(4)]
            turned = [parts[1], -parts[0], parts[3], -parts[2]]
            zero = jnp.zeros_like(parts[0])
            for q in range(4):
                real = parts[q] if q < 2 else jnp.where(ends, zero, parts[q])
                imag = jnp.where(ends, zero if q < 2 else parts[q], turned[q])
                both = jnp.where(left, real, imag)
                for w in range(windows):
                    start = w * (groups * 4) + g * 4 + q
                    wide[pl.ds(start, width, stride=depth + 1), :] = both[:, w * lanes:(w + 1) * lanes]

    def turn(k):
        return wide[pl.ds(k * (depth + 1), depth), :].T.astype(jnp.bfloat16)

    write_out(out_sems.shape[0], turn, stage, out_hbm, out_sems)


def fill_bins(white, bins, wide):
    groups, rows, _ = bins.shape
    width = rows // 4

    def to_bins(g, carry):
        value = jnp.dot(bins[g], white(g), preferred_element_type=jnp.float32)
        for q in range(4):
            for tile, ref in enumerate(wide):
                ref[pl.ds(g * 4 + q, width, stride=groups * 4 + 1), :] = (
                    value[q * width:(q + 1) * width, tile * width:(tile + 1) * width]
                )
        return carry

    lax.fori_loop(0, groups, to_bins, 0, unroll=8)


def partner_bins(wide, k, depth):
    part = pl.ds(k * (depth + 1), depth)
    return jnp.concatenate([ref[part, :].astype(jnp.bfloat16) for ref in wide], axis=0)


def pair_kernel(windows, *refs):
    records, sources, refs = refs[:2 * windows], refs[2 * windows:2 * windows + 3], refs[2 * windows + 3:]
    out_hbm, fhi, flo, bins, yhi, ylo, spec, *wide, stage, sems, out_sems = refs
    copies = start_copies(sources, (fhi, flo, bins), sems)
    white = whiten(1, records, copies, fhi, flo, yhi, ylo, spec)
    copies[2].wait()
    fill_bins(white, bins, wide)
    depth = stage.shape[1] // windows
    write_out(out_sems.shape[0], lambda k: partner_bins(wide, k, depth), stage, out_hbm, out_sems)


def last_kernel(windows, earlier, *refs):
    records, refs = refs[:2 * windows], refs[2 * windows:]
    count, pairs = 4 + earlier, 1 + earlier
    sources, (lag_ref, slot_ref, keep_ref, out_hbm), scratch = refs[:count], refs[count:count + 4], refs[count + 4:]
    loaded, (yhi, ylo, *scratch) = scratch[:count], scratch[count:]
    wide, cross, (stage, sems, out_sems) = scratch[:windows], scratch[windows:windows + pairs], scratch[windows + pairs:]
    fhi, flo, bins, own_ref, *early = loaded
    copies = start_copies(sources, loaded, sems)
    white = whiten(1, records, copies, fhi, flo, yhi, ylo, cross[0])
    copies[2].wait()
    fill_bins(white, bins, wide)
    for copy in copies[3:]:
        copy.wait()
    width, lanes, _ = own_ref.shape
    channels = lanes // 2
    depth = bins.shape[0] * 4

    def one_bin(k, carry):
        block = jnp.concatenate([ref[k] for ref in early] + [partner_bins(wide, k, depth)], axis=1)
        value = jnp.dot(own_ref[k], block, preferred_element_type=jnp.float32)
        for tile, ref in enumerate(cross):
            for part in range(2):
                ref[pl.ds(part * width + k, channels, stride=2 * width + 1), :] = (
                    value[part * channels:(part + 1) * channels, tile * lanes:(tile + 1) * lanes]
                )
        return carry

    lax.fori_loop(0, width, one_bin, 0, unroll=16)
    rows = 2 * width
    _, offsets, per_out, channels, _ = stage.shape
    chunks = channels // per_out

    def leave(chunk, slot):
        target = out_hbm.at[:, pl.ds(chunk * per_out, per_out)]
        return pltpu.make_async_copy(stage.at[slot], target, out_sems.at[slot])

    def two_chunks(t, carry):
        for slot in range(2):
            chunk = t * 2 + slot

            @pl.when(t > 0)
            def _():
                leave(chunk - 2, slot).wait()

            def one(n, inner):
                i = chunk * per_out + n
                block = jnp.concatenate(
                    [ref[pl.ds(i * (rows + 1), rows), :].astype(jnp.bfloat16) for ref in cross], axis=1
                )
                value = jnp.dot(lag_ref[...], block, preferred_element_type=jnp.float32).T
                for o in range(offsets):
                    stage[slot, slot_ref[o], n] = value[o * channels:(o + 1) * channels] * keep_ref[o]
                return inner

            lax.fori_loop(0, per_out, one, 0, unroll=8)
            leave(chunk, slot).start()
        return carry

    lax.fori_loop(0, chunks // 2, two_chunks, 0)
    for slot in range(2):
        leave(chunks - 2 + slot, slot).wait()


def call(kernel, name, operands, streamed, small, out_shape, out_space, scratch, flops, limit=50):
    vmem_spec = pl.BlockSpec(memory_space=pltpu.VMEM)
    smem_spec = pl.BlockSpec(memory_space=pltpu.SMEM)
    return pl.pallas_call(
        kernel,
        out_shape=out_shape,
        in_specs=[vmem_spec] * len(operands)
        + [pl.BlockSpec(memory_space=pl.ANY)] * len(streamed)
        + [vmem_spec if v.ndim > 1 else smem_spec for v in small],
        out_specs=pl.BlockSpec(memory_space=out_space),
        scratch_shapes=scratch,
        compiler_params=pltpu.CompilerParams(vmem_limit_bytes=limit * 2**20),
        cost_estimate=pl.CostEstimate(flops=flops, bytes_accessed=14 * 2**20, transcendentals=0),
        name=name,
    )(*operands, *streamed, *small)


def per_device(traces, live, reach):
    windows, channels, samples = traces.shape
    blocks = lax.axis_size("fibre")
    splits = lax.axis_size("freq")
    owned = OFF // splits
    place = lax.axis_index("freq")
    forward_hi, forward_lo, bins_t, lag, scale = build_tables(samples)
    forward_hi, forward_lo = jnp.asarray(forward_hi), jnp.asarray(forward_lo)
    masked = [jnp.where(live[:, None] > 0, traces[w], jnp.zeros((), traces.dtype)) for w in range(windows)]

    quads = blocks // owned
    half = owned // 2
    u = lax.axis_index("fibre") % owned
    core, pair = u % half, u // half

    def rank(q, pair, core, part):
        return (q * owned + pair * half + core) * splits + part

    def send(payload, route):
        pairs = []
        for q in range(quads):
            for p in range(2):
                for c in range(half):
                    for g in range(splits):
                        source = route(q, p, c, g)
                        if source[0] < quads:
                            pairs.append((rank(*source), rank(q, p, c, g)))
        return lax.ppermute(payload, ("fibre", "freq"), pairs)

    def from_neighbours(mine, upper):
        core_payload = jnp.where((core == 1) & (place == 0), mine, upper)
        across_payload = jnp.where((pair == 1) & (place == 0), mine, upper)
        beside = send(core_payload, lambda q, p, c, g: (q + c * g, p, 1 - c, 1 - g if c else g))
        across = send(across_payload, lambda q, p, c, g: (q + p * g, 1 - p, c, g))
        return jnp.where(place == 0, mine, upper), beside, across

    width = LAGS
    lanes = 2 * channels
    groups = samples // width // 2
    depth = 4 * groups
    pairs = 2
    bf16, f32 = jnp.bfloat16, jnp.float32
    dma = pltpu.SemaphoreType.DMA
    table_shapes = [pltpu.VMEM(t.shape, bf16) for t in (forward_hi, forward_lo, bins_t[0])]
    own_table, partner_table = jnp.asarray(bins_t[1]), jnp.asarray(bins_t[0])
    split_shapes = [pltpu.VMEM((groups, 2 * lanes, 2 * width), bf16)] * 2
    spec_shape = pltpu.VMEM((groups * 2 * lanes // width * 2 * width, width), f32)
    wide_shapes = [pltpu.VMEM((width * (depth + 1), lanes), f32)] * windows
    work = 16 * groups * 2 * lanes * 4 * width * width

    above = lambda q, p, c, g: (quads if p and c and not g else q + 1, p, c, g)
    upper = [send(mine, above) for mine in masked]
    own_white = call(
        functools.partial(own_spectra_kernel, windows), "own_spectra", masked, (forward_hi, forward_lo), (),
        jax.ShapeDtypeStruct((groups, 2 * width, windows * lanes), bf16), pltpu.VMEM,
        table_shapes[:2] + split_shapes + [spec_shape, dma((2,))], work // 2,
    )
    upper[0], own_white = lax.optimization_barrier((upper[0], own_white))
    own_shape = (width, lanes, windows * depth)
    own = call(
        functools.partial(own_bins_kernel, windows), "own_bins", [own_white], [own_table], (),
        jax.ShapeDtypeStruct(own_shape, bf16), pl.ANY,
        [table_shapes[2], pltpu.VMEM((width * (windows * depth + 1), lanes), f32), pltpu.VMEM(own_shape, bf16),
         dma((4,)), dma((4,))], work // 2,
    )
    here, beside, across = [], [], []
    for w in range(windows):
        if w:
            upper[w], beside[w - 1], own = lax.optimization_barrier((upper[w], beside[w - 1], own))
        for known, new in zip((here, beside, across), from_neighbours(masked[w], upper[w])):
            known.append(new)
    across[0], beside[-1] = lax.optimization_barrier((across[0], beside[-1]))
    shape = (width, windows * depth, lanes)
    first = call(
        functools.partial(pair_kernel, windows), "first_pair", [r for both in zip(here, beside) for r in both],
        (forward_hi, forward_lo, partner_table), (), jax.ShapeDtypeStruct(shape, bf16), pl.ANY,
        table_shapes + split_shapes + [spec_shape] + wide_shapes
        + [pltpu.VMEM(shape, bf16), dma((3,)), dma((4,))], work,
    )
    across[-1], first = lax.optimization_barrier((across[-1], first))
    across_beside = [send(block, lambda q, p, c, g: (q, p, 1 - c, g)) for block in across]
    early = [first]
    slots = jnp.stack([0, 1 + 2 * core, 2, 3 - 2 * core]).astype(jnp.int32)
    offset_ids = place * owned + slots
    keep = jnp.where(offset_ids < reach[0], jnp.float32(scale), jnp.float32(0.0))
    result = call(
        functools.partial(last_kernel, windows, len(early)), "second_pair",
        [r for both in zip(across, across_beside) for r in both],
        (forward_hi, forward_lo, partner_table, own, *early), (jnp.asarray(lag), slots, keep),
        jax.ShapeDtypeStruct((owned, channels, channels, LAGS), f32), pl.ANY,
        table_shapes + [pltpu.VMEM(own_shape, bf16)] + [pltpu.VMEM(e.shape, bf16) for e in early]
        + split_shapes + wide_shapes + [pltpu.VMEM((channels * (2 * width + 1), lanes), f32)] * pairs
        + [pltpu.VMEM((2, owned, channels // 8, channels, LAGS), f32), dma((4 + len(early),)), dma((2,))],
        2 * work,
    )
    return result[None]


def solution(mesh):
    placed = (P(None, "fibre", None), P("fibre"), P("fibre"))
    return jax.shard_map(
        per_device,
        mesh=mesh,
        in_specs=placed,
        out_specs=P("fibre", "freq", None, None, None),
        check_vma=False,
    )
```

```python
import functools
import math

import jax
import jax.numpy as jnp
import ml_dtypes
import numpy as np
from jax import lax
from jax.experimental import pallas as pl
from jax.experimental.pallas import tpu as pltpu
from jax.sharding import PartitionSpec as P

BAND = 64
OFF = 8
LAGS = 128


def leak_spectrum(freqs, samples, window, shift, slots, period):
    steps = np.arange(window)
    tone = np.exp(2j * np.pi * ((freqs[:, None] * (steps - shift)[None]) % samples) / samples)
    bins = np.exp(-2j * np.pi * ((steps[:, None] * slots[None]) % period) / period)
    return tone @ bins


@functools.lru_cache(maxsize=None)
def build_tables(samples):
    width = LAGS
    residues = samples // width
    groups = residues // 2
    half = width // 2
    per_band = BAND // residues
    order = np.concatenate([np.arange(i, half, per_band) for i in range(per_band)])
    steps = np.arange(width)
    slots = np.arange(width + 1)
    forward = np.zeros((groups, 2 * width, 4 * half))
    to_bins = np.zeros((2, groups, 4 * half, 4, width))
    root = 1.0 / math.sqrt(2.0)
    re_a, im_a, re_b, im_b = (slice(i * half, (i + 1) * half) for i in range(4))
    for g in range(groups):
        freq_a = g + residues * order
        freq_b = (residues - g if g else groups) + residues * order
        wave_a = np.exp(-2j * np.pi * ((steps[:, None] * freq_a[None]) % samples) / samples)
        wave_b = np.exp(-2j * np.pi * ((steps[:, None] * freq_b[None]) % samples) / samples)
        top, low = forward[g, :width], forward[g, width:]
        top[:, re_a], top[:, im_a] = wave_a.real, wave_a.imag
        if g == 0:
            low[:, re_b], low[:, im_b] = wave_b.real, wave_b.imag
        else:
            low[:, re_a], low[:, im_a] = -wave_a.imag, wave_a.real
            top[:, re_b], top[:, im_b] = wave_b.real, wave_b.imag
            low[:, re_b], low[:, im_b] = wave_b.imag, -wave_b.real
        for side in range(2):
            window, shift = ((width, 0), (2 * width, half))[side]
            leak = functools.partial(
                leak_spectrum, samples=samples, window=window, shift=shift, slots=slots, period=2 * width
            )
            pos_a, neg_a, pos_b, neg_b = leak(freq_a), leak(-freq_a), leak(freq_b), leak(-freq_b)
            spec = np.zeros((2, 4 * half, width + 1), complex)
            if g == 0:
                zero = (freq_a == 0)[:, None]
                spec[0, re_a] = np.where(zero, pos_a, root * (pos_a + neg_a))
                spec[0, im_a] = np.where(zero, 0.0, root * 1j * (pos_a - neg_a))
                spec[1, re_b] = root * (pos_b + neg_b)
                spec[1, im_b] = root * 1j * (pos_b - neg_b)
            else:
                spec[0, re_a], spec[0, im_a] = root * pos_a, root * 1j * pos_a
                spec[0, re_b], spec[0, im_b] = root * neg_b, -root * 1j * neg_b
                spec[1, re_b], spec[1, im_b] = root * pos_b, root * 1j * pos_b
                spec[1, re_a], spec[1, im_a] = root * neg_a, -root * 1j * neg_a
            table = to_bins[side, g]
            table[:, 0], table[:, 1] = spec[0, :, :width].real, spec[0, :, :width].imag
            table[:, 2], table[:, 3] = spec[1, :, :width].real, spec[1, :, :width].imag
            if g == 0:
                ends = (spec[0, :, 0].real, spec[1, :, 0].real, spec[0, :, width].real, spec[1, :, width].real)
            else:
                ends = tuple(
                    math.sqrt(2.0) * v
                    for v in (spec[0, :, 0].real, spec[0, :, 0].imag, spec[0, :, width].real, spec[0, :, width].imag)
                )
            for q in range(4):
                table[:, q, 0] = ends[q]
    lags = np.arange(LAGS)
    phase = 2 * np.pi * ((steps[:, None] * lags[None]) % (2 * width)) / (2 * width)
    lag = np.stack([2 * np.cos(phase), -2 * np.sin(phase)])
    lag[0, 0], lag[1, 0] = 1.0, (-1.0) ** lags
    bf16 = ml_dtypes.bfloat16
    forward_t = forward.transpose(0, 2, 1)
    forward_hi = forward_t.astype(bf16)
    forward_lo = (forward_t - forward_hi.astype(np.float64)).astype(bf16)
    bins_t = to_bins.transpose(0, 1, 3, 4, 2).reshape(2, groups, 4 * width, 4 * half).astype(bf16)
    lag = lag.reshape(2 * width, LAGS).T.astype(bf16)
    scale = residues / (2.0 * width * samples) / math.sqrt(samples)
    return forward_hi, forward_lo, bins_t, lag, scale


def real_dft(values):
    n = len(values)
    if n == 2:
        return [(values[0] + values[1], None), (values[0] - values[1], None)]
    even, odd = real_dft(values[0::2]), real_dft(values[1::2])
    out = [None] * (n // 2 + 1)
    for k in range(n // 4 + 1):
        (er, ei), (pr, pi) = even[k], odd[k]
        angle = -2.0 * math.pi * k / n
        c, s = math.cos(angle), math.sin(angle)
        if k == 0:
            out[0] = (er + pr, None)
            out[n // 2] = (er - pr, None)
            continue
        if 4 * k == n:
            out[k] = (er, -pr)
            continue
        if pi is None:
            tr, ti = pr * c, pr * s
        elif 8 * k == n:
            tr, ti = (pr + pi) * c, (pi - pr) * c
        else:
            tr, ti = pr * c - pi * s, pr * s + pi * c
        if ei is None:
            out[k] = (er + tr, ti)
            out[n // 2 - k] = (er - tr, ti)
        else:
            out[k] = (er + tr, ei + ti)
            out[n // 2 - k] = (er - tr, ti - ei)
    return out


def whiten(copies_of, records, copies, fhi, flo, yhi, ylo, spec):
    channels, samples = records[0].shape
    width = LAGS
    residues = samples // width
    groups = residues // 2
    rows = len(records) * copies_of * channels
    tiles = rows // width
    step = 16

    def split(value):
        high = value.astype(jnp.bfloat16)
        return high, (value - high.astype(jnp.float32)).astype(jnp.bfloat16)

    def transform(n, carry):
        for index, ref in enumerate(records):
            block = ref[pl.ds(pl.multiple_of(n * step, step), step), :].astype(jnp.float32)
            terms = real_dft([block[:, a * width:(a + 1) * width] for a in range(residues)])
            for g in range(groups):
                parts = terms[g] if g else (terms[0][0], terms[groups][0])
                for side, part in enumerate(parts):
                    hi, lo = split(part)
                    for copy_to in range(copies_of):
                        row = pl.multiple_of((index * copies_of + copy_to) * channels + n * step, step)
                        yhi[g, pl.ds(row, step), side * width:(side + 1) * width] = hi
                        ylo[g, pl.ds(row, step), side * width:(side + 1) * width] = lo
        return carry

    lax.fori_loop(0, channels // step, transform, 0)
    copies[0].wait()
    copies[1].wait()
    nt = (((1,), (1,)), ((), ()))
    bands = (samples // 2) // BAND

    def place(g, tile):
        return pl.ds(pl.multiple_of((g * tiles + tile) * 2 * width, 2 * width), 2 * width)

    def forward(g, power):
        value = lax.dot_general(fhi[g], yhi[g], nt, preferred_element_type=jnp.float32)
        value += lax.dot_general(flo[g], yhi[g], nt, preferred_element_type=jnp.float32)
        value += lax.dot_general(fhi[g], ylo[g], nt, preferred_element_type=jnp.float32)
        for tile in range(tiles):
            spec[place(g, tile), :] = value[:, tile * width:(tile + 1) * width]
        squared = (value * value).reshape(2 * width // bands, bands, rows)
        return power + squared.sum(0)

    power = lax.fori_loop(0, groups, forward, jnp.zeros((bands, rows), jnp.float32), unroll=8)
    gain = 1.0 / jnp.sqrt(power * (1.0 / BAND) + 1e-6)

    def white(g):
        value = jnp.concatenate([spec[place(g, tile), :] for tile in range(tiles)], axis=1)
        value = value.reshape(2 * width // bands, bands, rows) * gain[None]
        return value.reshape(2 * width, rows).astype(jnp.bfloat16)

    return white


def start_copies(sources, targets, sems):
    copies = [
        pltpu.make_async_copy(source, target, sems.at[i])
        for i, (source, target) in enumerate(zip(sources, targets))
    ]
    for copy in copies:
        copy.start()
    return copies


def write_out(chunks, fill, stage, out_hbm, sems):
    per_chunk = stage.shape[0] // chunks
    copies = []
    for chunk in range(chunks):
        def one(n, carry):
            stage[chunk * per_chunk + n] = fill(chunk * per_chunk + n)
            return carry

        lax.fori_loop(0, per_chunk, one, 0, unroll=8)
        part = pl.ds(chunk * per_chunk, per_chunk)
        copies.append(pltpu.make_async_copy(stage.at[part], out_hbm.at[part], sems.at[chunk]))
        copies[-1].start()
    for copy in copies:
        copy.wait()


def mask_kernel(traces_ref, live_ref, *out_refs):
    channels = live_ref.shape[1]
    square = (channels, channels)
    same = lax.broadcasted_iota(jnp.int32, square, 0) == lax.broadcasted_iota(jnp.int32, square, 1)
    live = jnp.broadcast_to((live_ref[...] > 0).astype(jnp.float32), square)
    pick = jnp.where(same, live, 0.0).astype(jnp.bfloat16)
    for w, out_ref in enumerate(out_refs):
        value = jnp.dot(pick, traces_ref[w], preferred_element_type=jnp.float32)
        out_ref[...] = value.astype(jnp.bfloat16)


def own_spectra_kernel(windows, *refs):
    records, (fhi_hbm, flo_hbm, out_ref, fhi, flo, yhi, ylo, spec, sems) = refs[:windows], refs[windows:]
    copies = start_copies((fhi_hbm, flo_hbm), (fhi, flo), sems)
    white = whiten(2, records, copies, fhi, flo, yhi, ylo, spec)

    def write(g, carry):
        out_ref[g] = white(g)
        return carry

    lax.fori_loop(0, out_ref.shape[0], write, 0, unroll=4)


def own_bins_kernel(windows, white_ref, bins_hbm, out_hbm, bins, wide, stage, sems, out_sems):
    groups, rows, _ = bins.shape
    width, lanes, depth = stage.shape
    chunks = sems.shape[0]
    per_chunk = groups // chunks
    parts = [pl.ds(chunk * per_chunk, per_chunk) for chunk in range(chunks)]
    copies = start_copies([bins_hbm.at[p] for p in parts], [bins.at[p] for p in parts], sems)
    left = lax.broadcasted_iota(jnp.int32, (width, windows * lanes), 1) % lanes < lanes // 2
    ends = lax.broadcasted_iota(jnp.int32, (width, windows * lanes), 0) == 0
    for chunk in range(chunks):
        copies[chunk].wait()
        for g in range(chunk * per_chunk, (chunk + 1) * per_chunk):
            value = jnp.dot(bins[g], white_ref[g], preferred_element_type=jnp.float32)
            parts = [value[q * width:(q + 1) * width] for q in range(4)]
            turned = [parts[1], -parts[0], parts[3], -parts[2]]
            zero = jnp.zeros_like(parts[0])
            for q in range(4):
                real = parts[q] if q < 2 else jnp.where(ends, zero, parts[q])
                imag = jnp.where(ends, zero if q < 2 else parts[q], turned[q])
                both = jnp.where(left, real, imag)
                for w in range(windows):
                    start = w * (groups * 4) + g * 4 + q
                    wide[pl.ds(start, width, stride=depth + 1), :] = both[:, w * lanes:(w + 1) * lanes]

    def turn(k):
        return wide[pl.ds(k * (depth + 1), depth), :].T.astype(jnp.bfloat16)

    write_out(out_sems.shape[0], turn, stage, out_hbm, out_sems)


def fill_bins(white, bins, wide):
    groups, rows, _ = bins.shape
    width = rows // 4

    def to_bins(g, carry):
        value = jnp.dot(bins[g], white(g), preferred_element_type=jnp.float32)
        for q in range(4):
            for tile, ref in enumerate(wide):
                ref[pl.ds(g * 4 + q, width, stride=groups * 4 + 1), :] = (
                    value[q * width:(q + 1) * width, tile * width:(tile + 1) * width]
                )
        return carry

    lax.fori_loop(0, groups, to_bins, 0, unroll=8)


def partner_bins(wide, k, depth):
    part = pl.ds(k * (depth + 1), depth)
    return jnp.concatenate([ref[part, :].astype(jnp.bfloat16) for ref in wide], axis=0)


def pair_kernel(windows, *refs):
    records, sources, refs = refs[:2 * windows], refs[2 * windows:2 * windows + 3], refs[2 * windows + 3:]
    out_hbm, fhi, flo, bins, yhi, ylo, spec, *wide, stage, sems, out_sems = refs
    copies = start_copies(sources, (fhi, flo, bins), sems)
    white = whiten(1, records, copies, fhi, flo, yhi, ylo, spec)
    copies[2].wait()
    fill_bins(white, bins, wide)
    depth = stage.shape[1] // windows
    write_out(out_sems.shape[0], lambda k: partner_bins(wide, k, depth), stage, out_hbm, out_sems)


def last_kernel(windows, earlier, *refs):
    records, refs = refs[:2 * windows], refs[2 * windows:]
    count, pairs = 4 + earlier, 1 + earlier
    sources, (lag_ref, slot_ref, keep_ref, out_hbm), scratch = refs[:count], refs[count:count + 4], refs[count + 4:]
    loaded, (yhi, ylo, *scratch) = scratch[:count], scratch[count:]
    wide, cross, (stage, sems, out_sems) = scratch[:windows], scratch[windows:windows + pairs], scratch[windows + pairs:]
    fhi, flo, bins, own_ref, *early = loaded
    copies = start_copies(sources, loaded, sems)
    white = whiten(1, records, copies, fhi, flo, yhi, ylo, cross[0])
    copies[2].wait()
    fill_bins(white, bins, wide)
    for copy in copies[3:]:
        copy.wait()
    width, lanes, _ = own_ref.shape
    channels = lanes // 2
    depth = bins.shape[0] * 4

    def one_bin(k, carry):
        block = jnp.concatenate([ref[k] for ref in early] + [partner_bins(wide, k, depth)], axis=1)
        value = jnp.dot(own_ref[k], block, preferred_element_type=jnp.float32)
        for tile, ref in enumerate(cross):
            for part in range(2):
                ref[pl.ds(part * width + k, channels, stride=2 * width + 1), :] = (
                    value[part * channels:(part + 1) * channels, tile * lanes:(tile + 1) * lanes]
                )
        return carry

    lax.fori_loop(0, width, one_bin, 0, unroll=16)
    rows = 2 * width
    _, offsets, per_out, channels, _ = stage.shape
    chunks = channels // per_out

    def leave(chunk, slot):
        target = out_hbm.at[:, pl.ds(chunk * per_out, per_out)]
        return pltpu.make_async_copy(stage.at[slot], target, out_sems.at[slot])

    def two_chunks(t, carry):
        for slot in range(2):
            chunk = t * 2 + slot

            @pl.when(t > 0)
            def _():
                leave(chunk - 2, slot).wait()

            def one(n, inner):
                i = chunk * per_out + n
                block = jnp.concatenate(
                    [ref[pl.ds(i * (rows + 1), rows), :].astype(jnp.bfloat16) for ref in cross], axis=1
                )
                value = jnp.dot(lag_ref[...], block, preferred_element_type=jnp.float32).T
                for o in range(offsets):
                    stage[slot, slot_ref[o], n] = value[o * channels:(o + 1) * channels] * keep_ref[o]
                return inner

            lax.fori_loop(0, per_out, one, 0, unroll=8)
            leave(chunk, slot).start()
        return carry

    lax.fori_loop(0, chunks // 2, two_chunks, 0)
    for slot in range(2):
        leave(chunks - 2 + slot, slot).wait()


def call(kernel, name, operands, streamed, small, out_shape, out_space, scratch, flops, limit=50):
    vmem_spec = pl.BlockSpec(memory_space=pltpu.VMEM)
    smem_spec = pl.BlockSpec(memory_space=pltpu.SMEM)
    return pl.pallas_call(
        kernel,
        out_shape=out_shape,
        in_specs=[vmem_spec] * len(operands)
        + [pl.BlockSpec(memory_space=pl.ANY)] * len(streamed)
        + [vmem_spec if v.ndim > 1 else smem_spec for v in small],
        out_specs=pl.BlockSpec(memory_space=out_space),
        scratch_shapes=scratch,
        compiler_params=pltpu.CompilerParams(vmem_limit_bytes=limit * 2**20),
        cost_estimate=pl.CostEstimate(flops=flops, bytes_accessed=14 * 2**20, transcendentals=0),
        name=name,
    )(*operands, *streamed, *small)


def per_device(traces, live, reach):
    windows, channels, samples = traces.shape
    blocks = lax.axis_size("fibre")
    splits = lax.axis_size("freq")
    owned = OFF // splits
    place = lax.axis_index("freq")
    forward_hi, forward_lo, bins_t, lag, scale = build_tables(samples)
    forward_hi, forward_lo = jnp.asarray(forward_hi), jnp.asarray(forward_lo)
    masked = list(pl.pallas_call(
        mask_kernel,
        out_shape=[jax.ShapeDtypeStruct((channels, samples), traces.dtype)] * windows,
        in_specs=[pl.BlockSpec(memory_space=pltpu.VMEM)] * 2,
        out_specs=[pl.BlockSpec(memory_space=pltpu.VMEM)] * windows,
        compiler_params=pltpu.CompilerParams(vmem_limit_bytes=61 * 2**20),
        name="mask_dead",
    )(traces, live[None, :]))

    quads = blocks // owned
    half = owned // 2
    u = lax.axis_index("fibre") % owned
    core, pair = u % half, u // half

    def rank(q, pair, core, part):
        return (q * owned + pair * half + core) * splits + part

    def send(payload, route):
        pairs = []
        for q in range(quads):
            for p in range(2):
                for c in range(half):
                    for g in range(splits):
                        source = route(q, p, c, g)
                        if source[0] < quads:
                            pairs.append((rank(*source), rank(q, p, c, g)))
        return lax.ppermute(payload, ("fibre", "freq"), pairs)

    def to_core(mine, upper):
        payload = jnp.where((core == 1) & (place == 0), mine, upper)
        return send(payload, lambda q, p, c, g: (q + c * g, p, 1 - c, 1 - g if c else g))

    def to_pair(mine, upper):
        payload = jnp.where((pair == 1) & (place == 0), mine, upper)
        return send(payload, lambda q, p, c, g: (q + p * g, 1 - p, c, g))

    width = LAGS
    lanes = 2 * channels
    groups = samples // width // 2
    depth = 4 * groups
    pairs = 2
    bf16, f32 = jnp.bfloat16, jnp.float32
    dma = pltpu.SemaphoreType.DMA
    table_shapes = [pltpu.VMEM(t.shape, bf16) for t in (forward_hi, forward_lo, bins_t[0])]
    own_table, partner_table = jnp.asarray(bins_t[1]), jnp.asarray(bins_t[0])
    split_shapes = [pltpu.VMEM((groups, 2 * lanes, 2 * width), bf16)] * 2
    spec_shape = pltpu.VMEM((groups * 2 * lanes // width * 2 * width, width), f32)
    wide_shapes = [pltpu.VMEM((width * (depth + 1), lanes), f32)] * windows
    work = 16 * groups * 2 * lanes * 4 * width * width

    above = lambda q, p, c, g: (quads if p and c and not g else q + 1, p, c, g)
    upper = [send(mine, above) for mine in masked]
    own_white = call(
        functools.partial(own_spectra_kernel, windows), "own_spectra", masked, (forward_hi, forward_lo), (),
        jax.ShapeDtypeStruct((groups, 2 * width, windows * lanes), bf16), pltpu.VMEM,
        table_shapes[:2] + split_shapes + [spec_shape, dma((2,))], work // 2,
    )
    upper[0], own_white = lax.optimization_barrier((upper[0], own_white))
    own_shape = (width, lanes, windows * depth)
    own = call(
        functools.partial(own_bins_kernel, windows), "own_bins", [own_white], [own_table], (),
        jax.ShapeDtypeStruct(own_shape, bf16), pl.ANY,
        [table_shapes[2], pltpu.VMEM((width * (windows * depth + 1), lanes), f32), pltpu.VMEM(own_shape, bf16),
         dma((4,)), dma((4,))], work // 2,
    )
    slots = jnp.stack([0, 1 + 2 * core, 2, 3 - 2 * core]).astype(jnp.int32)
    offset_ids = place * owned + slots
    keep = jnp.where(offset_ids < reach[0], jnp.float32(scale), jnp.float32(0.0))
    here, beside, across = [], [], []
    for w in range(windows):
        if w:
            upper[w], own, slots, keep = lax.optimization_barrier((upper[w], own, slots, keep))
        beside.append(to_core(masked[w], upper[w]))
        if w:
            upper[w], beside[w - 1] = lax.optimization_barrier((upper[w], beside[w - 1]))
        across.append(to_pair(masked[w], upper[w]))
        here.append(jnp.where(place == 0, masked[w], upper[w]))
    across[0], beside[-1] = lax.optimization_barrier((across[0], beside[-1]))
    shape = (width, windows * depth, lanes)
    first = call(
        functools.partial(pair_kernel, windows), "first_pair", [r for both in zip(here, beside) for r in both],
        (forward_hi, forward_lo, partner_table), (), jax.ShapeDtypeStruct(shape, bf16), pl.ANY,
        table_shapes + split_shapes + [spec_shape] + wide_shapes
        + [pltpu.VMEM(shape, bf16), dma((3,)), dma((4,))], work,
    )
    across[-1], first = lax.optimization_barrier((across[-1], first))
    across_beside = [send(block, lambda q, p, c, g: (q, p, 1 - c, g)) for block in across]
    early = [first]
    result = call(
        functools.partial(last_kernel, windows, len(early)), "second_pair",
        [r for both in zip(across, across_beside) for r in both],
        (forward_hi, forward_lo, partner_table, own, *early), (jnp.asarray(lag), slots, keep),
        jax.ShapeDtypeStruct((owned, channels, channels, LAGS), f32), pl.ANY,
        table_shapes + [pltpu.VMEM(own_shape, bf16)] + [pltpu.VMEM(e.shape, bf16) for e in early]
        + split_shapes + wide_shapes + [pltpu.VMEM((channels * (2 * width + 1), lanes), f32)] * pairs
        + [pltpu.VMEM((2, owned, channels // 8, channels, LAGS), f32), dma((4 + len(early),)), dma((2,))],
        2 * work,
    )
    return result[None]


def solution(mesh):
    placed = (P(None, "fibre", None), P("fibre"), P("fibre"))
    return jax.shard_map(
        per_device,
        mesh=mesh,
        in_specs=placed,
        out_specs=P("fibre", "freq", None, None, None),
        check_vma=False,
    )
```

```python
import functools
import math

import jax
import jax.numpy as jnp
import ml_dtypes
import numpy as np
from jax import lax
from jax.experimental import pallas as pl
from jax.experimental.pallas import tpu as pltpu
from jax.sharding import PartitionSpec as P

BAND = 64
OFF = 8
LAGS = 128


def leak_spectrum(freqs, samples, window, shift, slots, period):
    steps = np.arange(window)
    tone = np.exp(2j * np.pi * ((freqs[:, None] * (steps - shift)[None]) % samples) / samples)
    bins = np.exp(-2j * np.pi * ((steps[:, None] * slots[None]) % period) / period)
    return tone @ bins


@functools.lru_cache(maxsize=None)
def build_tables(samples):
    width = LAGS
    residues = samples // width
    groups = residues // 2
    half = width // 2
    per_band = BAND // residues
    order = np.concatenate([np.arange(i, half, per_band) for i in range(per_band)])
    steps = np.arange(width)
    slots = np.arange(width + 1)
    forward = np.zeros((groups, 2 * width, 4 * half))
    to_bins = np.zeros((2, groups, 4 * half, 4, width))
    root = 1.0 / math.sqrt(2.0)
    re_a, im_a, re_b, im_b = (slice(i * half, (i + 1) * half) for i in range(4))
    for g in range(groups):
        freq_a = g + residues * order
        freq_b = (residues - g if g else groups) + residues * order
        wave_a = np.exp(-2j * np.pi * ((steps[:, None] * freq_a[None]) % samples) / samples)
        wave_b = np.exp(-2j * np.pi * ((steps[:, None] * freq_b[None]) % samples) / samples)
        top, low = forward[g, :width], forward[g, width:]
        top[:, re_a], top[:, im_a] = wave_a.real, wave_a.imag
        if g == 0:
            low[:, re_b], low[:, im_b] = wave_b.real, wave_b.imag
        else:
            low[:, re_a], low[:, im_a] = -wave_a.imag, wave_a.real
            top[:, re_b], top[:, im_b] = wave_b.real, wave_b.imag
            low[:, re_b], low[:, im_b] = wave_b.imag, -wave_b.real
        for side in range(2):
            window, shift = ((width, 0), (2 * width, half))[side]
            leak = functools.partial(
                leak_spectrum, samples=samples, window=window, shift=shift, slots=slots, period=2 * width
            )
            pos_a, neg_a, pos_b, neg_b = leak(freq_a), leak(-freq_a), leak(freq_b), leak(-freq_b)
            spec = np.zeros((2, 4 * half, width + 1), complex)
            if g == 0:
                zero = (freq_a == 0)[:, None]
                spec[0, re_a] = np.where(zero, pos_a, root * (pos_a + neg_a))
                spec[0, im_a] = np.where(zero, 0.0, root * 1j * (pos_a - neg_a))
                spec[1, re_b] = root * (pos_b + neg_b)
                spec[1, im_b] = root * 1j * (pos_b - neg_b)
            else:
                spec[0, re_a], spec[0, im_a] = root * pos_a, root * 1j * pos_a
                spec[0, re_b], spec[0, im_b] = root * neg_b, -root * 1j * neg_b
                spec[1, re_b], spec[1, im_b] = root * pos_b, root * 1j * pos_b
                spec[1, re_a], spec[1, im_a] = root * neg_a, -root * 1j * neg_a
            table = to_bins[side, g]
            table[:, 0], table[:, 1] = spec[0, :, :width].real, spec[0, :, :width].imag
            table[:, 2], table[:, 3] = spec[1, :, :width].real, spec[1, :, :width].imag
            if g == 0:
                ends = (spec[0, :, 0].real, spec[1, :, 0].real, spec[0, :, width].real, spec[1, :, width].real)
            else:
                ends = tuple(
                    math.sqrt(2.0) * v
                    for v in (spec[0, :, 0].real, spec[0, :, 0].imag, spec[0, :, width].real, spec[0, :, width].imag)
                )
            for q in range(4):
                table[:, q, 0] = ends[q]
    lags = np.arange(LAGS)
    phase = 2 * np.pi * ((steps[:, None] * lags[None]) % (2 * width)) / (2 * width)
    lag = np.stack([2 * np.cos(phase), -2 * np.sin(phase)])
    lag[0, 0], lag[1, 0] = 1.0, (-1.0) ** lags
    bf16 = ml_dtypes.bfloat16
    forward_t = forward.transpose(0, 2, 1)
    forward_hi = forward_t.astype(bf16)
    forward_lo = (forward_t - forward_hi.astype(np.float64)).astype(bf16)
    bins_t = to_bins.transpose(0, 1, 3, 4, 2).reshape(2, groups, 4 * width, 4 * half).astype(bf16)
    lag = lag.reshape(2 * width, LAGS).T.astype(bf16)
    scale = residues / (2.0 * width * samples) / math.sqrt(samples)
    return forward_hi, forward_lo, bins_t, lag, scale


def real_dft(values):
    n = len(values)
    if n == 2:
        return [(values[0] + values[1], None), (values[0] - values[1], None)]
    even, odd = real_dft(values[0::2]), real_dft(values[1::2])
    out = [None] * (n // 2 + 1)
    for k in range(n // 4 + 1):
        (er, ei), (pr, pi) = even[k], odd[k]
        angle = -2.0 * math.pi * k / n
        c, s = math.cos(angle), math.sin(angle)
        if k == 0:
            out[0] = (er + pr, None)
            out[n // 2] = (er - pr, None)
            continue
        if 4 * k == n:
            out[k] = (er, -pr)
            continue
        if pi is None:
            tr, ti = pr * c, pr * s
        elif 8 * k == n:
            tr, ti = (pr + pi) * c, (pi - pr) * c
        else:
            tr, ti = pr * c - pi * s, pr * s + pi * c
        if ei is None:
            out[k] = (er + tr, ti)
            out[n // 2 - k] = (er - tr, ti)
        else:
            out[k] = (er + tr, ei + ti)
            out[n // 2 - k] = (er - tr, ti - ei)
    return out


def whiten(copies_of, records, copies, fhi, flo, yhi, ylo, spec):
    channels, samples = records[0].shape
    width = LAGS
    residues = samples // width
    groups = residues // 2
    rows = len(records) * copies_of * channels
    tiles = rows // width
    step = 16

    def split(value):
        high = value.astype(jnp.bfloat16)
        return high, (value - high.astype(jnp.float32)).astype(jnp.bfloat16)

    def transform(n, carry):
        for index, ref in enumerate(records):
            block = ref[pl.ds(pl.multiple_of(n * step, step), step), :].astype(jnp.float32)
            terms = real_dft([block[:, a * width:(a + 1) * width] for a in range(residues)])
            for g in range(groups):
                parts = terms[g] if g else (terms[0][0], terms[groups][0])
                for side, part in enumerate(parts):
                    hi, lo = split(part)
                    for copy_to in range(copies_of):
                        row = pl.multiple_of((index * copies_of + copy_to) * channels + n * step, step)
                        yhi[g, pl.ds(row, step), side * width:(side + 1) * width] = hi
                        ylo[g, pl.ds(row, step), side * width:(side + 1) * width] = lo
        return carry

    lax.fori_loop(0, channels // step, transform, 0)
    copies[0].wait()
    copies[1].wait()
    nt = (((1,), (1,)), ((), ()))
    bands = (samples // 2) // BAND

    def place(g, tile):
        return pl.ds(pl.multiple_of((g * tiles + tile) * 2 * width, 2 * width), 2 * width)

    def forward(g, power):
        value = lax.dot_general(fhi[g], yhi[g], nt, preferred_element_type=jnp.float32)
        value += lax.dot_general(flo[g], yhi[g], nt, preferred_element_type=jnp.float32)
        value += lax.dot_general(fhi[g], ylo[g], nt, preferred_element_type=jnp.float32)
        for tile in range(tiles):
            spec[place(g, tile), :] = value[:, tile * width:(tile + 1) * width]
        squared = (value * value).reshape(2 * width // bands, bands, rows)
        return power + squared.sum(0)

    power = lax.fori_loop(0, groups, forward, jnp.zeros((bands, rows), jnp.float32), unroll=8)
    gain = 1.0 / jnp.sqrt(power * (1.0 / BAND) + 1e-6)

    def white(g):
        value = jnp.concatenate([spec[place(g, tile), :] for tile in range(tiles)], axis=1)
        value = value.reshape(2 * width // bands, bands, rows) * gain[None]
        return value.reshape(2 * width, rows)

    return white


def start_copies(sources, targets, sems):
    copies = [
        pltpu.make_async_copy(source, target, sems.at[i])
        for i, (source, target) in enumerate(zip(sources, targets))
    ]
    for copy in copies:
        copy.start()
    return copies


def write_out(chunks, fill, stage, out_hbm, sems):
    per_chunk = stage.shape[0] // chunks
    copies = []
    for chunk in range(chunks):
        def one(n, carry):
            stage[chunk * per_chunk + n] = fill(chunk * per_chunk + n)
            return carry

        lax.fori_loop(0, per_chunk, one, 0, unroll=8)
        part = pl.ds(chunk * per_chunk, per_chunk)
        copies.append(pltpu.make_async_copy(stage.at[part], out_hbm.at[part], sems.at[chunk]))
        copies[-1].start()
    for copy in copies:
        copy.wait()


def spectra_kernel(windows, copies_of, *refs):
    records, (fhi_hbm, flo_hbm, out_ref, fhi, flo, yhi, ylo, spec, sems) = refs[:windows], refs[windows:]
    copies = start_copies((fhi_hbm, flo_hbm), (fhi, flo), sems)
    white = whiten(copies_of, records, copies, fhi, flo, yhi, ylo, spec)

    def write(g, carry):
        out_ref[g] = white(g).astype(jnp.bfloat16)
        return carry

    lax.fori_loop(0, out_ref.shape[0], write, 0, unroll=4)


def own_bins_kernel(windows, white_ref, bins_hbm, out_hbm, bins, wide, stage, sems, out_sems):
    groups, rows, _ = bins.shape
    width, lanes, depth = stage.shape
    chunks = sems.shape[0]
    per_chunk = groups // chunks
    parts = [pl.ds(chunk * per_chunk, per_chunk) for chunk in range(chunks)]
    copies = start_copies([bins_hbm.at[p] for p in parts], [bins.at[p] for p in parts], sems)
    left = lax.broadcasted_iota(jnp.int32, (width, windows * lanes), 1) % lanes < lanes // 2
    ends = lax.broadcasted_iota(jnp.int32, (width, windows * lanes), 0) == 0
    for chunk in range(chunks):
        copies[chunk].wait()
        for g in range(chunk * per_chunk, (chunk + 1) * per_chunk):
            value = jnp.dot(bins[g], white_ref[g], preferred_element_type=jnp.float32)
            parts = [value[q * width:(q + 1) * width] for q in range(4)]
            turned = [parts[1], -parts[0], parts[3], -parts[2]]
            zero = jnp.zeros_like(parts[0])
            for q in range(4):
                real = parts[q] if q < 2 else jnp.where(ends, zero, parts[q])
                imag = jnp.where(ends, zero if q < 2 else parts[q], turned[q])
                both = jnp.where(left, real, imag)
                for w in range(windows):
                    start = w * (groups * 4) + g * 4 + q
                    wide[pl.ds(start, width, stride=depth + 1), :] = both[:, w * lanes:(w + 1) * lanes]

    def turn(k):
        return wide[pl.ds(k * (depth + 1), depth), :].T.astype(jnp.bfloat16)

    write_out(out_sems.shape[0], turn, stage, out_hbm, out_sems)


def fill_bins(white, bins, wide):
    groups, rows, _ = bins.shape
    width = rows // 4

    def to_bins(g, carry):
        value = jnp.dot(bins[g], white(g).astype(jnp.bfloat16), preferred_element_type=jnp.float32)
        for q in range(4):
            for tile, ref in enumerate(wide):
                ref[pl.ds(g * 4 + q, width, stride=groups * 4 + 1), :] = (
                    value[q * width:(q + 1) * width, tile * width:(tile + 1) * width]
                )
        return carry

    lax.fori_loop(0, groups, to_bins, 0, unroll=8)


def partner_bins(wide, k, depth):
    part = pl.ds(k * (depth + 1), depth)
    return jnp.concatenate([ref[part, :].astype(jnp.bfloat16) for ref in wide], axis=0)


def pair_kernel(windows, *refs):
    records, here, sources, refs = refs[:windows], refs[windows], refs[windows + 1:windows + 4], refs[windows + 4:]
    out_hbm, fhi, flo, bins, yhi, ylo, spec, *wide, stage, sems, out_sems = refs
    copies = start_copies(sources, (fhi, flo, bins), sems)
    white = whiten(1, records, copies, fhi, flo, yhi, ylo, spec)
    copies[2].wait()
    _, rows, lanes = here.shape
    left = lax.broadcasted_iota(jnp.int32, (rows, lanes), 1) < lanes // 2

    def both(g):
        one, two = here[g].astype(jnp.float32), white(g)
        first = jnp.where(left, one, pltpu.roll(two, lanes // 2, 1))
        second = jnp.where(left, pltpu.roll(one, lanes // 2, 1), two)
        return jnp.concatenate([first, second], axis=1)

    fill_bins(both, bins, wide)
    depth = stage.shape[1] // windows
    write_out(out_sems.shape[0], lambda k: partner_bins(wide, k, depth), stage, out_hbm, out_sems)


def last_kernel(windows, earlier, *refs):
    records, refs = refs[:2 * windows], refs[2 * windows:]
    count, pairs = 4 + earlier, 1 + earlier
    sources, (lag_ref, slot_ref, keep_ref, out_hbm), scratch = refs[:count], refs[count:count + 4], refs[count + 4:]
    loaded, (yhi, ylo, *scratch) = scratch[:count], scratch[count:]
    wide, cross, (stage, sems, out_sems) = scratch[:windows], scratch[windows:windows + pairs], scratch[windows + pairs:]
    fhi, flo, bins, own_ref, *early = loaded
    copies = start_copies(sources, loaded, sems)
    white = whiten(1, records, copies, fhi, flo, yhi, ylo, cross[0])
    copies[2].wait()
    fill_bins(white, bins, wide)
    for copy in copies[3:]:
        copy.wait()
    width, lanes, _ = own_ref.shape
    channels = lanes // 2
    depth = bins.shape[0] * 4

    def one_bin(k, carry):
        block = jnp.concatenate([ref[k] for ref in early] + [partner_bins(wide, k, depth)], axis=1)
        value = jnp.dot(own_ref[k], block, preferred_element_type=jnp.float32)
        for tile, ref in enumerate(cross):
            for part in range(2):
                ref[pl.ds(part * width + k, channels, stride=2 * width + 1), :] = (
                    value[part * channels:(part + 1) * channels, tile * lanes:(tile + 1) * lanes]
                )
        return carry

    lax.fori_loop(0, width, one_bin, 0, unroll=16)
    rows = 2 * width
    _, offsets, per_out, channels, _ = stage.shape
    chunks = channels // per_out

    def leave(chunk, slot):
        target = out_hbm.at[:, pl.ds(chunk * per_out, per_out)]
        return pltpu.make_async_copy(stage.at[slot], target, out_sems.at[slot])

    def two_chunks(t, carry):
        for slot in range(2):
            chunk = t * 2 + slot

            @pl.when(t > 0)
            def _():
                leave(chunk - 2, slot).wait()

            def one(n, inner):
                i = chunk * per_out + n
                block = jnp.concatenate(
                    [ref[pl.ds(i * (rows + 1), rows), :].astype(jnp.bfloat16) for ref in cross], axis=1
                )
                value = jnp.dot(lag_ref[...], block, preferred_element_type=jnp.float32).T
                for o in range(offsets):
                    stage[slot, slot_ref[o], n] = value[o * channels:(o + 1) * channels] * keep_ref[o]
                return inner

            lax.fori_loop(0, per_out, one, 0, unroll=8)
            leave(chunk, slot).start()
        return carry

    lax.fori_loop(0, chunks // 2, two_chunks, 0)
    for slot in range(2):
        leave(chunks - 2 + slot, slot).wait()


def call(kernel, name, operands, streamed, small, out_shape, out_space, scratch, flops, limit=50):
    vmem_spec = pl.BlockSpec(memory_space=pltpu.VMEM)
    smem_spec = pl.BlockSpec(memory_space=pltpu.SMEM)
    return pl.pallas_call(
        kernel,
        out_shape=out_shape,
        in_specs=[vmem_spec] * len(operands)
        + [pl.BlockSpec(memory_space=pl.ANY)] * len(streamed)
        + [vmem_spec if v.ndim > 1 else smem_spec for v in small],
        out_specs=pl.BlockSpec(memory_space=out_space),
        scratch_shapes=scratch,
        compiler_params=pltpu.CompilerParams(vmem_limit_bytes=limit * 2**20),
        cost_estimate=pl.CostEstimate(flops=flops, bytes_accessed=14 * 2**20, transcendentals=0),
        name=name,
    )(*operands, *streamed, *small)


def per_device(traces, live, reach):
    windows, channels, samples = traces.shape
    blocks = lax.axis_size("fibre")
    splits = lax.axis_size("freq")
    owned = OFF // splits
    place = lax.axis_index("freq")
    forward_hi, forward_lo, bins_t, lag, scale = build_tables(samples)
    forward_hi, forward_lo = jnp.asarray(forward_hi), jnp.asarray(forward_lo)
    masked = [jnp.where(live[:, None] > 0, traces[w], jnp.zeros((), traces.dtype)) for w in range(windows)]

    quads = blocks // owned
    half = owned // 2
    u = lax.axis_index("fibre") % owned
    core, pair = u % half, u // half

    def rank(q, pair, core, part):
        return (q * owned + pair * half + core) * splits + part

    def send(payload, route):
        pairs = []
        for q in range(quads):
            for p in range(2):
                for c in range(half):
                    for g in range(splits):
                        source = route(q, p, c, g)
                        if source[0] < quads:
                            pairs.append((rank(*source), rank(q, p, c, g)))
        return lax.ppermute(payload, ("fibre", "freq"), pairs)

    def from_neighbours(mine, upper):
        core_payload = jnp.where((core == 1) & (place == 0), mine, upper)
        across_payload = jnp.where((pair == 1) & (place == 0), mine, upper)
        beside = send(core_payload, lambda q, p, c, g: (q + c * g, p, 1 - c, 1 - g if c else g))
        across = send(across_payload, lambda q, p, c, g: (q + p * g, 1 - p, c, g))
        return jnp.where(place == 0, mine, upper), beside, across

    width = LAGS
    lanes = 2 * channels
    groups = samples // width // 2
    depth = 4 * groups
    pairs = 2
    bf16, f32 = jnp.bfloat16, jnp.float32
    dma = pltpu.SemaphoreType.DMA
    table_shapes = [pltpu.VMEM(t.shape, bf16) for t in (forward_hi, forward_lo, bins_t[0])]
    own_table, partner_table = jnp.asarray(bins_t[1]), jnp.asarray(bins_t[0])
    split_shapes = [pltpu.VMEM((groups, 2 * lanes, 2 * width), bf16)] * 2
    spec_shape = pltpu.VMEM((groups * 2 * lanes // width * 2 * width, width), f32)
    wide_shapes = [pltpu.VMEM((width * (depth + 1), lanes), f32)] * windows
    work = 16 * groups * 2 * lanes * 4 * width * width

    above = lambda q, p, c, g: (quads if p and c and not g else q + 1, p, c, g)
    upper = [send(mine, above) for mine in masked]
    own_white = call(
        functools.partial(spectra_kernel, windows, 2), "own_spectra", masked, (forward_hi, forward_lo), (),
        jax.ShapeDtypeStruct((groups, 2 * width, windows * lanes), bf16), pltpu.VMEM,
        table_shapes[:2] + split_shapes + [spec_shape, dma((2,))], work // 2,
    )
    upper[0], own_white = lax.optimization_barrier((upper[0], own_white))
    own_shape = (width, lanes, windows * depth)
    own = call(
        functools.partial(own_bins_kernel, windows), "own_bins", [own_white], [own_table], (),
        jax.ShapeDtypeStruct(own_shape, bf16), pl.ANY,
        [table_shapes[2], pltpu.VMEM((width * (windows * depth + 1), lanes), f32), pltpu.VMEM(own_shape, bf16),
         dma((4,)), dma((4,))], work // 2,
    )
    slots = jnp.stack([0, 1 + 2 * core, 2, 3 - 2 * core]).astype(jnp.int32)
    offset_ids = place * owned + slots
    keep = jnp.where(offset_ids < reach[0], jnp.float32(scale), jnp.float32(0.0))
    here, beside, across = [], [], []
    for w in range(windows):
        if w:
            upper[w], beside[w - 1], own, slots, keep = lax.optimization_barrier(
                (upper[w], beside[w - 1], own, slots, keep)
            )
        for known, new in zip((here, beside, across), from_neighbours(masked[w], upper[w])):
            known.append(new)
    across[0], beside[-1] = lax.optimization_barrier((across[0], beside[-1]))
    shape = (width, windows * depth, lanes)
    half_split = [pltpu.VMEM((groups, lanes, 2 * width), bf16)] * 2
    half_spec = pltpu.VMEM((groups * lanes // width * 2 * width, width), f32)
    here_white = call(
        functools.partial(spectra_kernel, windows, 1), "here_spectra", here, (forward_hi, forward_lo), (),
        jax.ShapeDtypeStruct((groups, 2 * width, lanes), bf16), pltpu.VMEM,
        table_shapes[:2] + half_split + [half_spec, dma((2,))], work // 4,
    )
    first = call(
        functools.partial(pair_kernel, windows), "first_pair", [*beside, here_white],
        (forward_hi, forward_lo, partner_table), (), jax.ShapeDtypeStruct(shape, bf16), pl.ANY,
        table_shapes + half_split + [half_spec] + wide_shapes
        + [pltpu.VMEM(shape, bf16), dma((3,)), dma((4,))], work,
    )
    across[-1], first = lax.optimization_barrier((across[-1], first))
    across_beside = [send(block, lambda q, p, c, g: (q, p, 1 - c, g)) for block in across]
    early = [first]
    result = call(
        functools.partial(last_kernel, windows, len(early)), "second_pair",
        [r for both in zip(across, across_beside) for r in both],
        (forward_hi, forward_lo, partner_table, own, *early), (jnp.asarray(lag), slots, keep),
        jax.ShapeDtypeStruct((owned, channels, channels, LAGS), f32), pl.ANY,
        table_shapes + [pltpu.VMEM(own_shape, bf16)] + [pltpu.VMEM(e.shape, bf16) for e in early]
        + split_shapes + wide_shapes + [pltpu.VMEM((channels * (2 * width + 1), lanes), f32)] * pairs
        + [pltpu.VMEM((2, owned, channels // 8, channels, LAGS), f32), dma((4 + len(early),)), dma((2,))],
        2 * work,
    )
    return result[None]


def solution(mesh):
    placed = (P(None, "fibre", None), P("fibre"), P("fibre"))
    return jax.shard_map(
        per_device,
        mesh=mesh,
        in_specs=placed,
        out_specs=P("fibre", "freq", None, None, None),
        check_vma=False,
    )
```

```python
import functools
import math

import jax
import jax.numpy as jnp
import ml_dtypes
import numpy as np
from jax import lax
from jax.experimental import pallas as pl
from jax.experimental.pallas import tpu as pltpu
from jax.sharding import PartitionSpec as P

BAND = 64
OFF = 8
LAGS = 128


def leak_spectrum(freqs, samples, window, shift, slots, period):
    steps = np.arange(window)
    tone = np.exp(2j * np.pi * ((freqs[:, None] * (steps - shift)[None]) % samples) / samples)
    bins = np.exp(-2j * np.pi * ((steps[:, None] * slots[None]) % period) / period)
    return tone @ bins


@functools.lru_cache(maxsize=None)
def build_tables(samples):
    width = LAGS
    residues = samples // width
    groups = residues // 2
    half = width // 2
    per_band = BAND // residues
    order = np.concatenate([np.arange(i, half, per_band) for i in range(per_band)])
    steps = np.arange(width)
    slots = np.arange(width + 1)
    forward = np.zeros((groups, 2 * width, 4 * half))
    to_bins = np.zeros((2, groups, 4 * half, 4, width))
    root = 1.0 / math.sqrt(2.0)
    re_a, im_a, re_b, im_b = (slice(i * half, (i + 1) * half) for i in range(4))
    for g in range(groups):
        freq_a = g + residues * order
        freq_b = (residues - g if g else groups) + residues * order
        wave_a = np.exp(-2j * np.pi * ((steps[:, None] * freq_a[None]) % samples) / samples)
        wave_b = np.exp(-2j * np.pi * ((steps[:, None] * freq_b[None]) % samples) / samples)
        top, low = forward[g, :width], forward[g, width:]
        top[:, re_a], top[:, im_a] = wave_a.real, wave_a.imag
        if g == 0:
            low[:, re_b], low[:, im_b] = wave_b.real, wave_b.imag
        else:
            low[:, re_a], low[:, im_a] = -wave_a.imag, wave_a.real
            top[:, re_b], top[:, im_b] = wave_b.real, wave_b.imag
            low[:, re_b], low[:, im_b] = wave_b.imag, -wave_b.real
        for side in range(2):
            window, shift = ((width, 0), (2 * width, half))[side]
            leak = functools.partial(
                leak_spectrum, samples=samples, window=window, shift=shift, slots=slots, period=2 * width
            )
            pos_a, neg_a, pos_b, neg_b = leak(freq_a), leak(-freq_a), leak(freq_b), leak(-freq_b)
            spec = np.zeros((2, 4 * half, width + 1), complex)
            if g == 0:
                zero = (freq_a == 0)[:, None]
                spec[0, re_a] = np.where(zero, pos_a, root * (pos_a + neg_a))
                spec[0, im_a] = np.where(zero, 0.0, root * 1j * (pos_a - neg_a))
                spec[1, re_b] = root * (pos_b + neg_b)
                spec[1, im_b] = root * 1j * (pos_b - neg_b)
            else:
                spec[0, re_a], spec[0, im_a] = root * pos_a, root * 1j * pos_a
                spec[0, re_b], spec[0, im_b] = root * neg_b, -root * 1j * neg_b
                spec[1, re_b], spec[1, im_b] = root * pos_b, root * 1j * pos_b
                spec[1, re_a], spec[1, im_a] = root * neg_a, -root * 1j * neg_a
            table = to_bins[side, g]
            table[:, 0], table[:, 1] = spec[0, :, :width].real, spec[0, :, :width].imag
            table[:, 2], table[:, 3] = spec[1, :, :width].real, spec[1, :, :width].imag
            if g == 0:
                ends = (spec[0, :, 0].real, spec[1, :, 0].real, spec[0, :, width].real, spec[1, :, width].real)
            else:
                ends = tuple(
                    math.sqrt(2.0) * v
                    for v in (spec[0, :, 0].real, spec[0, :, 0].imag, spec[0, :, width].real, spec[0, :, width].imag)
                )
            for q in range(4):
                table[:, q, 0] = ends[q]
    lags = np.arange(LAGS)
    phase = 2 * np.pi * ((steps[:, None] * lags[None]) % (2 * width)) / (2 * width)
    lag = np.stack([2 * np.cos(phase), -2 * np.sin(phase)])
    lag[0, 0], lag[1, 0] = 1.0, (-1.0) ** lags
    bf16 = ml_dtypes.bfloat16
    forward_t = forward.transpose(0, 2, 1)
    forward_hi = forward_t.astype(bf16)
    forward_lo = (forward_t - forward_hi.astype(np.float64)).astype(bf16)
    bins_t = to_bins.transpose(0, 1, 3, 4, 2).reshape(2, groups, 4 * width, 4 * half).astype(bf16)
    lag = lag.reshape(2 * width, LAGS).T.astype(bf16)
    scale = residues / (2.0 * width * samples) / math.sqrt(samples)
    return forward_hi, forward_lo, bins_t, lag, scale


def real_dft(values):
    n = len(values)
    if n == 2:
        return [(values[0] + values[1], None), (values[0] - values[1], None)]
    even, odd = real_dft(values[0::2]), real_dft(values[1::2])
    out = [None] * (n // 2 + 1)
    for k in range(n // 4 + 1):
        (er, ei), (pr, pi) = even[k], odd[k]
        angle = -2.0 * math.pi * k / n
        c, s = math.cos(angle), math.sin(angle)
        if k == 0:
            out[0] = (er + pr, None)
            out[n // 2] = (er - pr, None)
            continue
        if 4 * k == n:
            out[k] = (er, -pr)
            continue
        if pi is None:
            tr, ti = pr * c, pr * s
        elif 8 * k == n:
            tr, ti = (pr + pi) * c, (pi - pr) * c
        else:
            tr, ti = pr * c - pi * s, pr * s + pi * c
        if ei is None:
            out[k] = (er + tr, ti)
            out[n // 2 - k] = (er - tr, ti)
        else:
            out[k] = (er + tr, ei + ti)
            out[n // 2 - k] = (er - tr, ti - ei)
    return out


def whiten(copies_of, records, copies, fhi, flo, yhi, ylo, spec, later=()):
    channels, samples = records[0].shape
    width = LAGS
    residues = samples // width
    groups = residues // 2
    rows = len(records) * copies_of * channels
    tiles = rows // width
    step = 16

    def split(value):
        high = value.astype(jnp.bfloat16)
        return high, (value - high.astype(jnp.float32)).astype(jnp.bfloat16)

    def transform(n, carry):
        for index, ref in enumerate(records):
            block = ref[pl.ds(pl.multiple_of(n * step, step), step), :].astype(jnp.float32)
            terms = real_dft([block[:, a * width:(a + 1) * width] for a in range(residues)])
            for g in range(groups):
                parts = terms[g] if g else (terms[0][0], terms[groups][0])
                for side, part in enumerate(parts):
                    hi, lo = split(part)
                    for copy_to in range(copies_of):
                        row = pl.multiple_of((index * copies_of + copy_to) * channels + n * step, step)
                        yhi[g, pl.ds(row, step), side * width:(side + 1) * width] = hi
                        ylo[g, pl.ds(row, step), side * width:(side + 1) * width] = lo
        return carry

    lax.fori_loop(0, channels // step, transform, 0)
    copies[0].wait()
    copies[1].wait()
    for copy in later:
        copy.start()
    nt = (((1,), (1,)), ((), ()))
    bands = (samples // 2) // BAND

    def place(g, tile):
        return pl.ds(pl.multiple_of((g * tiles + tile) * 2 * width, 2 * width), 2 * width)

    def forward(g, power):
        value = lax.dot_general(fhi[g], yhi[g], nt, preferred_element_type=jnp.float32)
        value += lax.dot_general(flo[g], yhi[g], nt, preferred_element_type=jnp.float32)
        value += lax.dot_general(fhi[g], ylo[g], nt, preferred_element_type=jnp.float32)
        for tile in range(tiles):
            spec[place(g, tile), :] = value[:, tile * width:(tile + 1) * width]
        squared = (value * value).reshape(2 * width // bands, bands, rows)
        return power + squared.sum(0)

    power = lax.fori_loop(0, groups, forward, jnp.zeros((bands, rows), jnp.float32), unroll=8)
    gain = 1.0 / jnp.sqrt(power * (1.0 / BAND) + 1e-6)

    def white(g):
        value = jnp.concatenate([spec[place(g, tile), :] for tile in range(tiles)], axis=1)
        value = value.reshape(2 * width // bands, bands, rows) * gain[None]
        return value.reshape(2 * width, rows).astype(jnp.bfloat16)

    return white


def make_copies(sources, targets, sems):
    return [
        pltpu.make_async_copy(source, target, sems.at[i])
        for i, (source, target) in enumerate(zip(sources, targets))
    ]


def start_copies(sources, targets, sems):
    copies = make_copies(sources, targets, sems)
    for copy in copies:
        copy.start()
    return copies


def write_out(chunks, fill, stage, out_hbm, sems):
    per_chunk = stage.shape[0] // chunks
    copies = []
    for chunk in range(chunks):
        def one(n, carry):
            stage[chunk * per_chunk + n] = fill(chunk * per_chunk + n)
            return carry

        lax.fori_loop(0, per_chunk, one, 0, unroll=8)
        part = pl.ds(chunk * per_chunk, per_chunk)
        copies.append(pltpu.make_async_copy(stage.at[part], out_hbm.at[part], sems.at[chunk]))
        copies[-1].start()
    for copy in copies:
        copy.wait()


def own_spectra_kernel(windows, *refs):
    records, (fhi_hbm, flo_hbm, out_ref, fhi, flo, yhi, ylo, spec, sems) = refs[:windows], refs[windows:]
    copies = start_copies((fhi_hbm, flo_hbm), (fhi, flo), sems)
    white = whiten(2, records, copies, fhi, flo, yhi, ylo, spec)

    def write(g, carry):
        out_ref[g] = white(g)
        return carry

    lax.fori_loop(0, out_ref.shape[0], write, 0, unroll=4)


def own_bins_kernel(windows, white_ref, bins_hbm, out_hbm, bins, wide, stage, sems, out_sems):
    groups, rows, _ = bins.shape
    width, lanes, depth = stage.shape
    chunks = sems.shape[0]
    per_chunk = groups // chunks
    parts = [pl.ds(chunk * per_chunk, per_chunk) for chunk in range(chunks)]
    copies = start_copies([bins_hbm.at[p] for p in parts], [bins.at[p] for p in parts], sems)
    left = lax.broadcasted_iota(jnp.int32, (width, windows * lanes), 1) % lanes < lanes // 2
    ends = lax.broadcasted_iota(jnp.int32, (width, windows * lanes), 0) == 0
    for chunk in range(chunks):
        copies[chunk].wait()
        for g in range(chunk * per_chunk, (chunk + 1) * per_chunk):
            value = jnp.dot(bins[g], white_ref[g], preferred_element_type=jnp.float32)
            parts = [value[q * width:(q + 1) * width] for q in range(4)]
            turned = [parts[1], -parts[0], parts[3], -parts[2]]
            zero = jnp.zeros_like(parts[0])
            for q in range(4):
                real = parts[q] if q < 2 else jnp.where(ends, zero, parts[q])
                imag = jnp.where(ends, zero if q < 2 else parts[q], turned[q])
                both = jnp.where(left, real, imag)
                for w in range(windows):
                    start = w * (groups * 4) + g * 4 + q
                    wide[pl.ds(start, width, stride=depth + 1), :] = both[:, w * lanes:(w + 1) * lanes]

    def turn(k):
        return wide[pl.ds(k * (depth + 1), depth), :].T.astype(jnp.bfloat16)

    write_out(out_sems.shape[0], turn, stage, out_hbm, out_sems)


def fill_bins(white, bins, wide):
    groups, rows, _ = bins.shape
    width = rows // 4

    def to_bins(g, carry):
        value = jnp.dot(bins[g], white(g), preferred_element_type=jnp.float32)
        for q in range(4):
            for tile, ref in enumerate(wide):
                ref[pl.ds(g * 4 + q, width, stride=groups * 4 + 1), :] = (
                    value[q * width:(q + 1) * width, tile * width:(tile + 1) * width]
                )
        return carry

    lax.fori_loop(0, groups, to_bins, 0, unroll=8)


def partner_bins(wide, k, depth):
    part = pl.ds(k * (depth + 1), depth)
    return jnp.concatenate([ref[part, :].astype(jnp.bfloat16) for ref in wide], axis=0)


def pair_kernel(windows, *refs):
    records, sources, refs = refs[:2 * windows], refs[2 * windows:2 * windows + 3], refs[2 * windows + 3:]
    out_hbm, fhi, flo, bins, yhi, ylo, spec, *wide, stage, sems, out_sems = refs
    copies = make_copies(sources, (fhi, flo, bins), sems)
    copies[0].start()
    copies[1].start()
    white = whiten(1, records, copies, fhi, flo, yhi, ylo, spec, copies[2:])
    copies[2].wait()
    fill_bins(white, bins, wide)
    depth = stage.shape[1] // windows
    write_out(out_sems.shape[0], lambda k: partner_bins(wide, k, depth), stage, out_hbm, out_sems)


def last_kernel(windows, earlier, *refs):
    records, refs = refs[:2 * windows], refs[2 * windows:]
    count, pairs = 4 + earlier, 1 + earlier
    sources, (lag_ref, slot_ref, keep_ref, out_hbm), scratch = refs[:count], refs[count:count + 4], refs[count + 4:]
    loaded, (yhi, ylo, *scratch) = scratch[:count], scratch[count:]
    wide, cross, (stage, sems, out_sems) = scratch[:windows], scratch[windows:windows + pairs], scratch[windows + pairs:]
    fhi, flo, bins, own_ref, *early = loaded
    tables = make_copies(sources[:3], loaded[:3], sems)
    tables[0].start()
    tables[1].start()
    splits = (sems.shape[0] - 3) // (1 + earlier)
    per_split = own_ref.shape[0] // splits
    chunks = []
    for split in range(splits):
        part = pl.ds(split * per_split, per_split)
        chunks.append([
            pltpu.make_async_copy(source.at[part], target.at[part], sems.at[3 + split * (1 + earlier) + i])
            for i, (source, target) in enumerate(zip(sources[3:], loaded[3:]))
        ])
    white = whiten(1, records, tables, fhi, flo, yhi, ylo, cross[0], [tables[2]] + chunks[0])
    tables[2].wait()
    for chunk in chunks[1:]:
        for copy in chunk:
            copy.start()
    fill_bins(white, bins, wide)
    width, lanes, _ = own_ref.shape
    channels = lanes // 2
    depth = bins.shape[0] * 4

    def one_bin(k, carry):
        block = jnp.concatenate([ref[k] for ref in early] + [partner_bins(wide, k, depth)], axis=1)
        value = jnp.dot(own_ref[k], block, preferred_element_type=jnp.float32)
        for tile, ref in enumerate(cross):
            for part in range(2):
                ref[pl.ds(part * width + k, channels, stride=2 * width + 1), :] = (
                    value[part * channels:(part + 1) * channels, tile * lanes:(tile + 1) * lanes]
                )
        return carry

    for split, chunk in enumerate(chunks):
        for copy in chunk:
            copy.wait()
        lax.fori_loop(split * per_split, (split + 1) * per_split, one_bin, 0, unroll=16)
    rows = 2 * width
    _, offsets, per_out, channels, _ = stage.shape
    out_chunks = channels // per_out

    def leave(chunk, slot):
        target = out_hbm.at[:, pl.ds(chunk * per_out, per_out)]
        return pltpu.make_async_copy(stage.at[slot], target, out_sems.at[slot])

    def two_chunks(t, carry):
        for slot in range(2):
            chunk = t * 2 + slot

            @pl.when(t > 0)
            def _():
                leave(chunk - 2, slot).wait()

            def one(n, inner):
                i = chunk * per_out + n
                block = jnp.concatenate(
                    [ref[pl.ds(i * (rows + 1), rows), :].astype(jnp.bfloat16) for ref in cross], axis=1
                )
                value = jnp.dot(lag_ref[...], block, preferred_element_type=jnp.float32).T
                for o in range(offsets):
                    stage[slot, slot_ref[o], n] = value[o * channels:(o + 1) * channels] * keep_ref[o]
                return inner

            lax.fori_loop(0, per_out, one, 0, unroll=8)
            leave(chunk, slot).start()
        return carry

    lax.fori_loop(0, out_chunks // 2, two_chunks, 0)
    for slot in range(2):
        leave(out_chunks - 2 + slot, slot).wait()


def call(kernel, name, operands, streamed, small, out_shape, out_space, scratch, flops, limit=50):
    vmem_spec = pl.BlockSpec(memory_space=pltpu.VMEM)
    smem_spec = pl.BlockSpec(memory_space=pltpu.SMEM)
    return pl.pallas_call(
        kernel,
        out_shape=out_shape,
        in_specs=[vmem_spec] * len(operands)
        + [pl.BlockSpec(memory_space=pl.ANY)] * len(streamed)
        + [vmem_spec if v.ndim > 1 else smem_spec for v in small],
        out_specs=pl.BlockSpec(memory_space=out_space),
        scratch_shapes=scratch,
        compiler_params=pltpu.CompilerParams(vmem_limit_bytes=limit * 2**20),
        cost_estimate=pl.CostEstimate(flops=flops, bytes_accessed=14 * 2**20, transcendentals=0),
        name=name,
    )(*operands, *streamed, *small)


def per_device(traces, live, reach):
    windows, channels, samples = traces.shape
    blocks = lax.axis_size("fibre")
    splits = lax.axis_size("freq")
    owned = OFF // splits
    place = lax.axis_index("freq")
    forward_hi, forward_lo, bins_t, lag, scale = build_tables(samples)
    forward_hi, forward_lo = jnp.asarray(forward_hi), jnp.asarray(forward_lo)
    masked = [jnp.where(live[:, None] > 0, traces[w], jnp.zeros((), traces.dtype)) for w in range(windows)]

    quads = blocks // owned
    half = owned // 2
    u = lax.axis_index("fibre") % owned
    core, pair = u % half, u // half

    def rank(q, pair, core, part):
        return (q * owned + pair * half + core) * splits + part

    def send(payload, route):
        pairs = []
        for q in range(quads):
            for p in range(2):
                for c in range(half):
                    for g in range(splits):
                        source = route(q, p, c, g)
                        if source[0] < quads:
                            pairs.append((rank(*source), rank(q, p, c, g)))
        return lax.ppermute(payload, ("fibre", "freq"), pairs)

    def from_neighbours(mine, upper):
        core_payload = jnp.where((core == 1) & (place == 0), mine, upper)
        across_payload = jnp.where((pair == 1) & (place == 0), mine, upper)
        beside = send(core_payload, lambda q, p, c, g: (q + c * g, p, 1 - c, 1 - g if c else g))
        across = send(across_payload, lambda q, p, c, g: (q + p * g, 1 - p, c, g))
        return jnp.where(place == 0, mine, upper), beside, across

    width = LAGS
    lanes = 2 * channels
    groups = samples // width // 2
    depth = 4 * groups
    pairs = 2
    bf16, f32 = jnp.bfloat16, jnp.float32
    dma = pltpu.SemaphoreType.DMA
    table_shapes = [pltpu.VMEM(t.shape, bf16) for t in (forward_hi, forward_lo, bins_t[0])]
    own_table, partner_table = jnp.asarray(bins_t[1]), jnp.asarray(bins_t[0])
    split_shapes = [pltpu.VMEM((groups, 2 * lanes, 2 * width), bf16)] * 2
    spec_shape = pltpu.VMEM((groups * 2 * lanes // width * 2 * width, width), f32)
    wide_shapes = [pltpu.VMEM((width * (depth + 1), lanes), f32)] * windows
    work = 16 * groups * 2 * lanes * 4 * width * width

    above = lambda q, p, c, g: (quads if p and c and not g else q + 1, p, c, g)
    upper = [send(mine, above) for mine in masked]
    own_white = call(
        functools.partial(own_spectra_kernel, windows), "own_spectra", masked, (forward_hi, forward_lo), (),
        jax.ShapeDtypeStruct((groups, 2 * width, windows * lanes), bf16), pltpu.VMEM,
        table_shapes[:2] + split_shapes + [spec_shape, dma((2,))], work // 2,
    )
    upper[0], own_white = lax.optimization_barrier((upper[0], own_white))
    own_shape = (width, lanes, windows * depth)
    own = call(
        functools.partial(own_bins_kernel, windows), "own_bins", [own_white], [own_table], (),
        jax.ShapeDtypeStruct(own_shape, bf16), pl.ANY,
        [table_shapes[2], pltpu.VMEM((width * (windows * depth + 1), lanes), f32), pltpu.VMEM(own_shape, bf16),
         dma((4,)), dma((4,))], work // 2,
    )
    here, beside, across = [], [], []
    for w in range(windows):
        if w:
            upper[w], beside[w - 1], own = lax.optimization_barrier((upper[w], beside[w - 1], own))
        for known, new in zip((here, beside, across), from_neighbours(masked[w], upper[w])):
            known.append(new)
    across[0], beside[-1] = lax.optimization_barrier((across[0], beside[-1]))
    shape = (width, windows * depth, lanes)
    first = call(
        functools.partial(pair_kernel, windows), "first_pair", [r for both in zip(here, beside) for r in both],
        (forward_hi, forward_lo, partner_table), (), jax.ShapeDtypeStruct(shape, bf16), pl.ANY,
        table_shapes + split_shapes + [spec_shape] + wide_shapes
        + [pltpu.VMEM(shape, bf16), dma((3,)), dma((4,))], work,
    )
    across[-1], first = lax.optimization_barrier((across[-1], first))
    across_beside = [send(block, lambda q, p, c, g: (q, p, 1 - c, g)) for block in across]
    early = [first]
    slots = jnp.stack([0, 1 + 2 * core, 2, 3 - 2 * core]).astype(jnp.int32)
    offset_ids = place * owned + slots
    keep = jnp.where(offset_ids < reach[0], jnp.float32(scale), jnp.float32(0.0))
    result = call(
        functools.partial(last_kernel, windows, len(early)), "second_pair",
        [r for both in zip(across, across_beside) for r in both],
        (forward_hi, forward_lo, partner_table, own, *early), (jnp.asarray(lag), slots, keep),
        jax.ShapeDtypeStruct((owned, channels, channels, LAGS), f32), pl.ANY,
        table_shapes + [pltpu.VMEM(own_shape, bf16)] + [pltpu.VMEM(e.shape, bf16) for e in early]
        + split_shapes + wide_shapes + [pltpu.VMEM((channels * (2 * width + 1), lanes), f32)] * pairs
        + [pltpu.VMEM((2, owned, channels // 8, channels, LAGS), f32), dma((3 + 4 * (1 + len(early)),)), dma((2,))],
        2 * work,
    )
    return result[None]


def solution(mesh):
    placed = (P(None, "fibre", None), P("fibre"), P("fibre"))
    return jax.shard_map(
        per_device,
        mesh=mesh,
        in_specs=placed,
        out_specs=P("fibre", "freq", None, None, None),
        check_vma=False,
    )
```

```python
import functools
import math

import jax
import jax.numpy as jnp
import ml_dtypes
import numpy as np
from jax import lax
from jax.experimental import pallas as pl
from jax.experimental.pallas import tpu as pltpu
from jax.sharding import PartitionSpec as P

BAND = 64
OFF = 8
LAGS = 128


def leak_spectrum(freqs, samples, window, shift, slots, period):
    steps = np.arange(window)
    tone = np.exp(2j * np.pi * ((freqs[:, None] * (steps - shift)[None]) % samples) / samples)
    bins = np.exp(-2j * np.pi * ((steps[:, None] * slots[None]) % period) / period)
    return tone @ bins


@functools.lru_cache(maxsize=None)
def build_tables(samples):
    width = LAGS
    residues = samples // width
    groups = residues // 2
    half = width // 2
    per_band = BAND // residues
    order = np.concatenate([np.arange(i, half, per_band) for i in range(per_band)])
    steps = np.arange(width)
    slots = np.arange(width + 1)
    forward = np.zeros((groups, 2 * width, 4 * half))
    to_bins = np.zeros((2, groups, 4 * half, 4, width))
    root = 1.0 / math.sqrt(2.0)
    re_a, im_a, re_b, im_b = (slice(i * half, (i + 1) * half) for i in range(4))
    for g in range(groups):
        freq_a = g + residues * order
        freq_b = (residues - g if g else groups) + residues * order
        wave_a = np.exp(-2j * np.pi * ((steps[:, None] * freq_a[None]) % samples) / samples)
        wave_b = np.exp(-2j * np.pi * ((steps[:, None] * freq_b[None]) % samples) / samples)
        top, low = forward[g, :width], forward[g, width:]
        top[:, re_a], top[:, im_a] = wave_a.real, wave_a.imag
        if g == 0:
            low[:, re_b], low[:, im_b] = wave_b.real, wave_b.imag
        else:
            low[:, re_a], low[:, im_a] = -wave_a.imag, wave_a.real
            top[:, re_b], top[:, im_b] = wave_b.real, wave_b.imag
            low[:, re_b], low[:, im_b] = wave_b.imag, -wave_b.real
        for side in range(2):
            window, shift = ((width, 0), (2 * width, half))[side]
            leak = functools.partial(
                leak_spectrum, samples=samples, window=window, shift=shift, slots=slots, period=2 * width
            )
            pos_a, neg_a, pos_b, neg_b = leak(freq_a), leak(-freq_a), leak(freq_b), leak(-freq_b)
            spec = np.zeros((2, 4 * half, width + 1), complex)
            if g == 0:
                zero = (freq_a == 0)[:, None]
                spec[0, re_a] = np.where(zero, pos_a, root * (pos_a + neg_a))
                spec[0, im_a] = np.where(zero, 0.0, root * 1j * (pos_a - neg_a))
                spec[1, re_b] = root * (pos_b + neg_b)
                spec[1, im_b] = root * 1j * (pos_b - neg_b)
            else:
                spec[0, re_a], spec[0, im_a] = root * pos_a, root * 1j * pos_a
                spec[0, re_b], spec[0, im_b] = root * neg_b, -root * 1j * neg_b
                spec[1, re_b], spec[1, im_b] = root * pos_b, root * 1j * pos_b
                spec[1, re_a], spec[1, im_a] = root * neg_a, -root * 1j * neg_a
            table = to_bins[side, g]
            table[:, 0], table[:, 1] = spec[0, :, :width].real, spec[0, :, :width].imag
            table[:, 2], table[:, 3] = spec[1, :, :width].real, spec[1, :, :width].imag
            if g == 0:
                ends = (spec[0, :, 0].real, spec[1, :, 0].real, spec[0, :, width].real, spec[1, :, width].real)
            else:
                ends = tuple(
                    math.sqrt(2.0) * v
                    for v in (spec[0, :, 0].real, spec[0, :, 0].imag, spec[0, :, width].real, spec[0, :, width].imag)
                )
            for q in range(4):
                table[:, q, 0] = ends[q]
    lags = np.arange(LAGS)
    phase = 2 * np.pi * ((steps[:, None] * lags[None]) % (2 * width)) / (2 * width)
    lag = np.stack([2 * np.cos(phase), -2 * np.sin(phase)])
    lag[0, 0], lag[1, 0] = 1.0, (-1.0) ** lags
    bf16 = ml_dtypes.bfloat16
    forward_t = forward.transpose(0, 2, 1)
    forward_hi = forward_t.astype(bf16)
    forward_lo = (forward_t - forward_hi.astype(np.float64)).astype(bf16)
    bins_t = to_bins.transpose(0, 1, 3, 4, 2).reshape(2, groups, 4 * width, 4 * half).astype(bf16)
    lag = lag.reshape(2 * width, LAGS).T.astype(bf16)
    scale = residues / (2.0 * width * samples) / math.sqrt(samples)
    return forward_hi, forward_lo, bins_t, lag, scale


def real_dft(values):
    n = len(values)
    if n == 2:
        return [(values[0] + values[1], None), (values[0] - values[1], None)]
    even, odd = real_dft(values[0::2]), real_dft(values[1::2])
    out = [None] * (n // 2 + 1)
    for k in range(n // 4 + 1):
        (er, ei), (pr, pi) = even[k], odd[k]
        angle = -2.0 * math.pi * k / n
        c, s = math.cos(angle), math.sin(angle)
        if k == 0:
            out[0] = (er + pr, None)
            out[n // 2] = (er - pr, None)
            continue
        if 4 * k == n:
            out[k] = (er, -pr)
            continue
        if pi is None:
            tr, ti = pr * c, pr * s
        elif 8 * k == n:
            tr, ti = (pr + pi) * c, (pi - pr) * c
        else:
            tr, ti = pr * c - pi * s, pr * s + pi * c
        if ei is None:
            out[k] = (er + tr, ti)
            out[n // 2 - k] = (er - tr, ti)
        else:
            out[k] = (er + tr, ei + ti)
            out[n // 2 - k] = (er - tr, ti - ei)
    return out


def whiten(copies_of, records, copies, fhi, flo, yhi, ylo, spec):
    channels, samples = records[0].shape
    width = LAGS
    residues = samples // width
    groups = residues // 2
    rows = len(records) * copies_of * channels
    tiles = rows // width
    step = 16

    def split(value):
        high = value.astype(jnp.bfloat16)
        return high, (value - high.astype(jnp.float32)).astype(jnp.bfloat16)

    def transform(n, carry):
        for index, ref in enumerate(records):
            block = ref[pl.ds(pl.multiple_of(n * step, step), step), :].astype(jnp.float32)
            terms = real_dft([block[:, a * width:(a + 1) * width] for a in range(residues)])
            for g in range(groups):
                parts = terms[g] if g else (terms[0][0], terms[groups][0])
                for side, part in enumerate(parts):
                    hi, lo = split(part)
                    for copy_to in range(copies_of):
                        row = pl.multiple_of((index * copies_of + copy_to) * channels + n * step, step)
                        yhi[g, pl.ds(row, step), side * width:(side + 1) * width] = hi
                        ylo[g, pl.ds(row, step), side * width:(side + 1) * width] = lo
        return carry

    lax.fori_loop(0, channels // step, transform, 0)
    copies[0].wait()
    copies[1].wait()
    nt = (((1,), (1,)), ((), ()))
    bands = (samples // 2) // BAND

    def place(g, tile):
        return pl.ds(pl.multiple_of((g * tiles + tile) * 2 * width, 2 * width), 2 * width)

    def forward(g, power):
        value = lax.dot_general(fhi[g], yhi[g], nt, preferred_element_type=jnp.float32)
        value += lax.dot_general(flo[g], yhi[g], nt, preferred_element_type=jnp.float32)
        value += lax.dot_general(fhi[g], ylo[g], nt, preferred_element_type=jnp.float32)
        for tile in range(tiles):
            spec[place(g, tile), :] = value[:, tile * width:(tile + 1) * width]
        squared = (value * value).reshape(2 * width // bands, bands, rows)
        return power + squared.sum(0)

    power = lax.fori_loop(0, groups, forward, jnp.zeros((bands, rows), jnp.float32), unroll=8)
    gain = 1.0 / jnp.sqrt(power * (1.0 / BAND) + 1e-6)

    def white(g):
        value = jnp.concatenate([spec[place(g, tile), :] for tile in range(tiles)], axis=1)
        value = value.reshape(2 * width // bands, bands, rows) * gain[None]
        return value.reshape(2 * width, rows).astype(jnp.bfloat16)

    return white


def start_copies(sources, targets, sems):
    copies = [
        pltpu.make_async_copy(source, target, sems.at[i])
        for i, (source, target) in enumerate(zip(sources, targets))
    ]
    for copy in copies:
        copy.start()
    return copies


def write_out(chunks, fill, stage, out_hbm, sems):
    per_chunk = stage.shape[0] // chunks
    copies = []
    for chunk in range(chunks):
        def one(n, carry):
            stage[chunk * per_chunk + n] = fill(chunk * per_chunk + n)
            return carry

        lax.fori_loop(0, per_chunk, one, 0, unroll=8)
        part = pl.ds(chunk * per_chunk, per_chunk)
        copies.append(pltpu.make_async_copy(stage.at[part], out_hbm.at[part], sems.at[chunk]))
        copies[-1].start()
    for copy in copies:
        copy.wait()


def own_spectra_kernel(windows, *refs):
    records, (fhi_hbm, flo_hbm, out_ref, fhi, flo, yhi, ylo, spec, sems) = refs[:windows], refs[windows:]
    copies = start_copies((fhi_hbm, flo_hbm), (fhi, flo), sems)
    white = whiten(2, records, copies, fhi, flo, yhi, ylo, spec)

    def write(g, carry):
        out_ref[g] = white(g)
        return carry

    lax.fori_loop(0, out_ref.shape[0], write, 0, unroll=4)


def own_bins_kernel(windows, white_ref, bins_hbm, out_hbm, bins, wide, stage, sems, out_sems):
    groups, rows, _ = bins.shape
    width, lanes, depth = stage.shape
    chunks = sems.shape[0]
    per_chunk = groups // chunks
    parts = [pl.ds(chunk * per_chunk, per_chunk) for chunk in range(chunks)]
    copies = start_copies([bins_hbm.at[p] for p in parts], [bins.at[p] for p in parts], sems)
    left = lax.broadcasted_iota(jnp.int32, (width, windows * lanes), 1) % lanes < lanes // 2
    ends = lax.broadcasted_iota(jnp.int32, (width, windows * lanes), 0) == 0
    for chunk in range(chunks):
        copies[chunk].wait()
        for g in range(chunk * per_chunk, (chunk + 1) * per_chunk):
            value = jnp.dot(bins[g], white_ref[g], preferred_element_type=jnp.float32)
            parts = [value[q * width:(q + 1) * width] for q in range(4)]
            turned = [parts[1], -parts[0], parts[3], -parts[2]]
            zero = jnp.zeros_like(parts[0])
            for q in range(4):
                real = parts[q] if q < 2 else jnp.where(ends, zero, parts[q])
                imag = jnp.where(ends, zero if q < 2 else parts[q], turned[q])
                both = jnp.where(left, real, imag)
                for w in range(windows):
                    start = w * (groups * 4) + g * 4 + q
                    wide[pl.ds(start, width, stride=depth + 1), :] = both[:, w * lanes:(w + 1) * lanes]

    def turn(k):
        return wide[pl.ds(k * (depth + 1), depth), :].T.astype(jnp.bfloat16)

    write_out(out_sems.shape[0], turn, stage, out_hbm, out_sems)


def fill_bins(white, bins, wide):
    groups, rows, _ = bins.shape
    width = rows // 4

    def to_bins(g, carry):
        value = jnp.dot(bins[g], white(g), preferred_element_type=jnp.float32)
        for q in range(4):
            for tile, ref in enumerate(wide):
                ref[pl.ds(g * 4 + q, width, stride=groups * 4 + 1), :] = (
                    value[q * width:(q + 1) * width, tile * width:(tile + 1) * width]
                )
        return carry

    lax.fori_loop(0, groups, to_bins, 0, unroll=8)


def partner_bins(wide, k, depth):
    part = pl.ds(k * (depth + 1), depth)
    return jnp.concatenate([ref[part, :].astype(jnp.bfloat16) for ref in wide], axis=0)


def pair_kernel(windows, *refs):
    records, sources, refs = refs[:2 * windows], refs[2 * windows:2 * windows + 3], refs[2 * windows + 3:]
    out_hbm, fhi, flo, bins, yhi, ylo, spec, *wide, stage, sems, out_sems = refs
    copies = start_copies(sources, (fhi, flo, bins), sems)
    white = whiten(1, records, copies, fhi, flo, yhi, ylo, spec)
    copies[2].wait()
    fill_bins(white, bins, wide)
    depth = stage.shape[1] // windows
    write_out(out_sems.shape[0], lambda k: partner_bins(wide, k, depth), stage, out_hbm, out_sems)


def last_kernel(windows, earlier, *refs):
    records, refs = refs[:2 * windows], refs[2 * windows:]
    count, pairs = 4 + earlier, 1 + earlier
    sources, (lag_ref, slot_ref, keep_ref, out_hbm), scratch = refs[:count], refs[count:count + 4], refs[count + 4:]
    loaded, (yhi, ylo, *scratch) = scratch[:count], scratch[count:]
    wide, cross, (stage, sems, out_sems) = scratch[:windows], scratch[windows:windows + pairs], scratch[windows + pairs:]
    fhi, flo, bins, own_ref, *early = loaded
    copies = start_copies(sources, loaded, sems)
    white = whiten(1, records, copies, fhi, flo, yhi, ylo, cross[0])
    copies[2].wait()
    fill_bins(white, bins, wide)
    for copy in copies[3:]:
        copy.wait()
    width, lanes, _ = own_ref.shape
    channels = lanes // 2
    depth = bins.shape[0] * 4

    def one_bin(k, carry):
        block = jnp.concatenate([ref[k] for ref in early] + [partner_bins(wide, k, depth)], axis=1)
        value = jnp.dot(own_ref[k], block, preferred_element_type=jnp.float32)
        for tile, ref in enumerate(cross):
            for part in range(2):
                ref[pl.ds(part * width + k, channels, stride=2 * width + 1), :] = (
                    value[part * channels:(part + 1) * channels, tile * lanes:(tile + 1) * lanes]
                )
        return carry

    lax.fori_loop(0, width, one_bin, 0, unroll=16)
    rows = 2 * width
    _, offsets, per_out, channels, _ = stage.shape
    chunks = channels // per_out

    def leave(chunk, slot):
        target = out_hbm.at[:, pl.ds(chunk * per_out, per_out)]
        return pltpu.make_async_copy(stage.at[slot], target, out_sems.at[slot])

    def two_chunks(t, carry):
        for slot in range(2):
            chunk = t * 2 + slot

            @pl.when(t > 0)
            def _():
                leave(chunk - 2, slot).wait()

            def one(n, inner):
                i = chunk * per_out + n
                block = jnp.concatenate(
                    [ref[pl.ds(i * (rows + 1), rows), :].astype(jnp.bfloat16) for ref in cross], axis=1
                )
                value = jnp.dot(lag_ref[...], block, preferred_element_type=jnp.float32).T
                for o in range(offsets):
                    stage[slot, slot_ref[o], n] = value[o * channels:(o + 1) * channels] * keep_ref[o]
                return inner

            lax.fori_loop(0, per_out, one, 0, unroll=8)
            leave(chunk, slot).start()
        return carry

    lax.fori_loop(0, chunks // 2, two_chunks, 0)
    for slot in range(2):
        leave(chunks - 2 + slot, slot).wait()


def call(kernel, name, operands, streamed, small, out_shape, out_space, scratch, flops, limit=50):
    vmem_spec = pl.BlockSpec(memory_space=pltpu.VMEM)
    smem_spec = pl.BlockSpec(memory_space=pltpu.SMEM)
    return pl.pallas_call(
        kernel,
        out_shape=out_shape,
        in_specs=[vmem_spec] * len(operands)
        + [pl.BlockSpec(memory_space=pl.ANY)] * len(streamed)
        + [vmem_spec if v.ndim > 1 else smem_spec for v in small],
        out_specs=pl.BlockSpec(memory_space=out_space),
        scratch_shapes=scratch,
        compiler_params=pltpu.CompilerParams(vmem_limit_bytes=limit * 2**20),
        cost_estimate=pl.CostEstimate(flops=flops, bytes_accessed=14 * 2**20, transcendentals=0),
        name=name,
    )(*operands, *streamed, *small)


def per_device(traces, live, reach):
    windows, channels, samples = traces.shape
    blocks = lax.axis_size("fibre")
    splits = lax.axis_size("freq")
    owned = OFF // splits
    place = lax.axis_index("freq")
    forward_hi, forward_lo, bins_t, lag, scale = build_tables(samples)
    forward_hi, forward_lo = jnp.asarray(forward_hi), jnp.asarray(forward_lo)
    masked = [jnp.where(live[:, None] > 0, traces[w], jnp.zeros((), traces.dtype)) for w in range(windows)]

    quads = blocks // owned
    half = owned // 2
    u = lax.axis_index("fibre") % owned
    core, pair = u % half, u // half

    def rank(q, pair, core, part):
        return (q * owned + pair * half + core) * splits + part

    def send(payload, route):
        pairs = []
        for q in range(quads):
            for p in range(2):
                for c in range(half):
                    for g in range(splits):
                        source = route(q, p, c, g)
                        if source[0] < quads:
                            pairs.append((rank(*source), rank(q, p, c, g)))
        return lax.ppermute(payload, ("fibre", "freq"), pairs)

    def from_neighbours(mine, upper):
        core_payload = jnp.where((core == 1) & (place == 0), mine, upper)
        across_payload = jnp.where((pair == 1) & (place == 0), mine, upper)
        beside = send(core_payload, lambda q, p, c, g: (q + c * g, p, 1 - c, 1 - g if c else g))
        across = send(across_payload, lambda q, p, c, g: (q + p * g, 1 - p, c, g))
        return jnp.where(place == 0, mine, upper), beside, across

    width = LAGS
    lanes = 2 * channels
    groups = samples // width // 2
    depth = 4 * groups
    pairs = 2
    bf16, f32 = jnp.bfloat16, jnp.float32
    dma = pltpu.SemaphoreType.DMA
    table_shapes = [pltpu.VMEM(t.shape, bf16) for t in (forward_hi, forward_lo, bins_t[0])]
    own_table, partner_table = jnp.asarray(bins_t[1]), jnp.asarray(bins_t[0])
    split_shapes = [pltpu.VMEM((groups, 2 * lanes, 2 * width), bf16)] * 2
    spec_shape = pltpu.VMEM((groups * 2 * lanes // width * 2 * width, width), f32)
    wide_shapes = [pltpu.VMEM((width * (depth + 1), lanes), f32)] * windows
    work = 16 * groups * 2 * lanes * 4 * width * width

    above = lambda q, p, c, g: (quads if p and c and not g else q + 1, p, c, g)
    upper = [send(mine, above) for mine in masked]
    own_white = call(
        functools.partial(own_spectra_kernel, windows), "own_spectra", masked, (forward_hi, forward_lo), (),
        jax.ShapeDtypeStruct((groups, 2 * width, windows * lanes), bf16), pltpu.VMEM,
        table_shapes[:2] + split_shapes + [spec_shape, dma((2,))], work // 2,
    )
    upper[0], own_white = lax.optimization_barrier((upper[0], own_white))
    own_shape = (width, lanes, windows * depth)
    own = call(
        functools.partial(own_bins_kernel, windows), "own_bins", [own_white], [own_table], (),
        jax.ShapeDtypeStruct(own_shape, bf16), pl.ANY,
        [table_shapes[2], pltpu.VMEM((width * (windows * depth + 1), lanes), f32), pltpu.VMEM(own_shape, bf16),
         dma((4,)), dma((4,))], work // 2,
    )
    slots = jnp.stack([0, 1 + 2 * core, 2, 3 - 2 * core]).astype(jnp.int32)
    offset_ids = place * owned + slots
    keep = jnp.where(offset_ids < reach[0], jnp.float32(scale), jnp.float32(0.0))
    here, beside, across = [], [], []
    for w in range(windows):
        if w:
            upper[w], beside[w - 1], own, slots, keep = lax.optimization_barrier(
                (upper[w], beside[w - 1], own, slots, keep)
            )
        for known, new in zip((here, beside, across), from_neighbours(masked[w], upper[w])):
            known.append(new)
    across[0], beside[-1] = lax.optimization_barrier((across[0], beside[-1]))
    shape = (width, windows * depth, lanes)
    first = call(
        functools.partial(pair_kernel, windows), "first_pair", [r for both in zip(here, beside) for r in both],
        (forward_hi, forward_lo, partner_table), (), jax.ShapeDtypeStruct(shape, bf16), pl.ANY,
        table_shapes + split_shapes + [spec_shape] + wide_shapes
        + [pltpu.VMEM(shape, bf16), dma((3,)), dma((4,))], work,
    )
    across[-1], first = lax.optimization_barrier((across[-1], first))
    across_beside = [send(block, lambda q, p, c, g: (q, p, 1 - c, g)) for block in across]
    early = [first]
    result = call(
        functools.partial(last_kernel, windows, len(early)), "second_pair",
        [r for both in zip(across, across_beside) for r in both],
        (forward_hi, forward_lo, partner_table, own, *early), (jnp.asarray(lag), slots, keep),
        jax.ShapeDtypeStruct((owned, channels, channels, LAGS), f32), pl.ANY,
        table_shapes + [pltpu.VMEM(own_shape, bf16)] + [pltpu.VMEM(e.shape, bf16) for e in early]
        + split_shapes + wide_shapes + [pltpu.VMEM((channels * (2 * width + 1), lanes), f32)] * pairs
        + [pltpu.VMEM((2, owned, channels // 8, channels, LAGS), f32), dma((4 + len(early),)), dma((2,))],
        2 * work,
    )
    return result[None]


def solution(mesh):
    placed = (P(None, "fibre", None), P("fibre"), P("fibre"))
    return jax.shard_map(
        per_device,
        mesh=mesh,
        in_specs=placed,
        out_specs=P("fibre", "freq", None, None, None),
        check_vma=False,
    )
```
